32 devices in a mesh: section: 2 (over core), dp: 16 (over z, y, x).
Axes of the slice: x: 2, y: 2, z: 4, core: 2. Of those that a mesh axis runs over, the one named last changes fastest.
Arguments:
- long_input: bfloat16 [8192, 768], P('dp'), may hold values from -6 to 6
- global_input: bfloat16 [1024, 768], P('dp'), may hold values from -6 to 6
- counts: int32 [32], P('dp'), may hold values from 2 to 32, as said below
- w_query: bfloat16 [2, 768, 768], P('section'), may hold values from -0.21875 to 0.21875
- b_query: bfloat16 [2, 768], P('section'), may hold values from -3 to 3
- w_key: bfloat16 [2, 768, 768], P('section'), may hold values from -0.21875 to 0.21875
- w_value: bfloat16 [2, 768, 768], P('section'), may hold values from -0.21875 to 0.21875
- b_value: bfloat16 [2, 768], P('section'), may hold values from -3 to 3
- w_out: bfloat16 [2, 768, 768], P('section'), may hold values from -0.875 to 0.875
- b_out: bfloat16 [2, 768], P('section'), may hold values from -3 to 3
- rel_table: bfloat16 [2, 169, 768], P('section'), may hold values from -6 to 6
- norm1_gain: bfloat16 [2, 768], P('section'), may hold values from 0.5 to 1.5
- norm1_bias: bfloat16 [2, 768], P('section'), may hold values from -3 to 3
- w_up: bfloat16 [2, 768, 3072], P('section'), may hold values from -0.21875 to 0.21875
- b_up: bfloat16 [2, 3072], P('section'), may hold values from -3 to 3
- w_down: bfloat16 [2, 3072, 768], P('section'), may hold values from -0.21875 to 0.21875
- b_down: bfloat16 [2, 768], P('section'), may hold values from -3 to 3
- norm2_gain: bfloat16 [2, 768], P('section'), may hold values from 0.5 to 1.5
- norm2_bias: bfloat16 [2, 768], P('section'), may hold values from -3 to 3
- long_cot: bfloat16 [8192, 768], P('dp'), may hold values from -6 to 6
- global_cot: bfloat16 [1024, 768], P('dp'), may hold values from -6 to 6
Outputs:
- long_outputs: bfloat16 [2, 8192, 768], P('section', 'dp')
- global_outputs: bfloat16 [2, 1024, 768], P('section', 'dp')
- long_grads: float32 [2, 8192, 768], P('section', 'dp')
- global_grads: float32 [2, 1024, 768], P('section', 'dp')
- grad_w_query: float32 [2, 768, 768], P('section', None, 'dp')
- grad_b_query: float32 [2, 768], P('section', 'dp')
- grad_w_key: float32 [2, 768, 768], P('section', None, 'dp')
- grad_w_value: float32 [2, 768, 768], P('section', None, 'dp')
- grad_b_value: float32 [2, 768], P('section', 'dp')
- grad_w_out: float32 [2, 768, 768], P('section', None, 'dp')
- grad_b_out: float32 [2, 768], P('section', 'dp')
- grad_rel_table: float32 [2, 169, 768], P('section', None, 'dp')
- grad_norm1_gain: float32 [2, 768], P('section', 'dp')
- grad_norm1_bias: float32 [2, 768], P('section', 'dp')
- grad_w_up: float32 [2, 768, 3072], P('section', None, 'dp')
- grad_b_up: float32 [2, 3072], P('section', 'dp')
- grad_w_down: float32 [2, 3072, 768], P('section', 'dp')
- grad_b_down: float32 [2, 768], P('section', 'dp')
- grad_norm2_gain: float32 [2, 768], P('section', 'dp')
- grad_norm2_bias: float32 [2, 768], P('section', 'dp')
The draws below stay inside these ranges and needn't reach their ends.
Inputs may be any that keep to these rules, and one draw needn't show every extreme that they name: `counts`: global slots at or beyond an item's count are unused; one item has all 32 slots live.
All inputs are finite; a program needn't handle non-finite values.
Results may differ from the reference program's by a relative error of at most 0.025.
Values may be sent and summed in bfloat16 or wider, within the bound.
A program may use at most 320 MiB of HBM per device.

```python
import math
import jax
import jax.numpy as jnp
from jax import lax

D = 768
H = 12
HD = 64
FF = 3072
R = 84
LABELS = 169
L = 256
G = 32
ITEMS = 32
TOKENS = 8192
GTOT = 1024


def draw_counts(key, part):
    key = jax.random.fold_in(key, 7)
    count_key, pick_key = jax.random.split(key)
    lowest = max(2, G // 16)
    drawn = jax.random.randint(count_key, (ITEMS,), lowest, G + 1)
    chosen = jax.random.randint(pick_key, (), 0, ITEMS)
    return drawn.at[chosen].set(G).astype(jnp.int32)


def strengthened(entries, own_key, source, target, shards_of, factor):
    owner, partner = [(jnp.arange(entries.shape[axis_at]) // (entries.shape[axis_at] // shards_of)).reshape([-1 if axis == axis_at else 1 for axis in range(entries.ndim)]) for axis_at in (source, target)]
    chosen = jax.random.permutation(own_key, shards_of)[partner]
    strong = (owner == chosen) | (owner == (partner + shards_of // 2) % shards_of)
    return jnp.where(strong, factor * entries, entries)


def level_of(rng, shape, cuts, low, largest):
    level, own = 1.0, jax.random.fold_in(rng, 6)
    for position, shards_of in cuts:
        heights = jnp.exp(jax.random.uniform(jax.random.fold_in(own, position), (shards_of,), jnp.float32, low / len(cuts), largest / len(cuts)))
        level = level * jnp.repeat(heights, shape[position] // shards_of).reshape([-1 if axis == position else 1 for axis in range(len(shape))])
    return level


def normal_values(rng, shape, scale, bound, cuts=(), kind=jnp.bfloat16):
    array = jax.random.normal(rng, shape, jnp.float32) * scale
    if len(cuts) > 0:
        array = level_of(rng, shape, cuts, -0.22, 0.18) * array
    return jnp.clip(array, min=-bound, max=bound).astype(kind)


def noise_with(rng, extent, width, reach, cuts, heavy, kind=jnp.bfloat16):
    array = width * jax.random.normal(rng, extent, jnp.float32)
    if cuts:
        array = array * level_of(rng, extent, cuts, -0.22, 0.18)
    return jnp.clip(strengthened(array, jax.random.fold_in(rng, 3), *heavy), -reach, reach).astype(kind)


def setup_inputs(seed: int = 0) -> dict:
    key_list = jax.random.split(jax.random.key(seed), 22)
    return {
        "long_input": normal_values(key_list[0], (TOKENS, D), 1.0, 6.0, ((0, 16),)),
        "global_input": normal_values(key_list[1], (GTOT, D), 1.0, 6.0, ((0, 16),)),
        "counts": draw_counts(jax.random.fold_in(key_list[21], 71), 0),
        "w_query": normal_values(key_list[3], (2, D, D), D ** -0.5, 0.21875, ((0, 2),)),
        "b_query": normal_values(key_list[4], (2, D), 0.5, 3.0, ((0, 2),)),
        "w_key": normal_values(key_list[5], (2, D, D), D ** -0.5, 0.21875, ((0, 2),)),
        "w_value": normal_values(key_list[6], (2, D, D), D ** -0.5, 0.21875, ((0, 2),)),
        "b_value": normal_values(key_list[7], (2, D), 0.5, 3.0, ((0, 2),)),
        "w_out": normal_values(key_list[8], (2, D, D), (D // 16) ** -0.5, 0.875, ((0, 2),)),
        "b_out": normal_values(key_list[9], (2, D), 0.5, 3.0, ((0, 2),)),
        "rel_table": normal_values(key_list[10], (2, LABELS, D), 1.0, 6.0, ((0, 2),)),
        "norm1_gain": jnp.clip(1.0 + 0.1 * jax.random.normal(key_list[11], (2, D), jnp.float32), 0.5, 1.5).astype(jnp.bfloat16),
        "norm1_bias": normal_values(key_list[12], (2, D), 0.5, 3.0, ((0, 2),)),
        "w_up": normal_values(key_list[13], (2, D, FF), D ** -0.5, 0.21875, ((0, 2),)),
        "b_up": normal_values(key_list[14], (2, FF), 0.5, 3.0, ((0, 2),)),
        "w_down": normal_values(key_list[15], (2, FF, D), (FF // 4) ** -0.5, 0.21875, ((0, 2),)),
        "b_down": normal_values(key_list[16], (2, D), 0.5, 3.0, ((0, 2),)),
        "norm2_gain": jnp.clip(1.0 + 0.1 * jax.random.normal(key_list[17], (2, D), jnp.float32), 0.5, 1.5).astype(jnp.bfloat16),
        "norm2_bias": normal_values(key_list[18], (2, D), 0.5, 3.0, ((0, 2),)),
        "long_cot": noise_with(key_list[19], (TOKENS, D), 1.0, 6.0, ((0, 16),), (0, 1, 16, 2.0)),
        "global_cot": normal_values(key_list[20], (GTOT, D), 1.0, 6.0, ((0, 16),)),
    }


@jax.custom_vjp
def low(v):
    return lax.optimization_barrier(v.astype(jnp.bfloat16)).astype(jnp.float32)

@jax.custom_vjp
def low_back(v):
    return v

def low_keep(v):
    return (low(v), None)

def low_pass(kept, grad):
    return (grad,)

def back_keep(v):
    return (v, None)

def back_low(kept, grad):
    return (low(grad),)
low.defvjp(low_keep, low_pass)
low_back.defvjp(back_keep, back_low)

def matmul(left_mat, right_mat):
    return jnp.dot(left_mat, right_mat, precision=lax.Precision.HIGHEST)

def layer_norm(layer_rows, gain_vec, shift_vec):
    center = layer_rows - lax.optimization_barrier(jnp.mean(layer_rows, axis=-1, keepdims=True))
    spread = lax.optimization_barrier(jnp.mean(center * center, axis=-1, keepdims=True))
    return center * lax.rsqrt(spread + 1e-05) * gain_vec + shift_vec

def masked_softmax(scores, allowed):
    masked = jnp.where(allowed, scores, -1e+30)
    row_max = lax.optimization_barrier(jnp.max(masked, axis=-1, keepdims=True))
    exponent = jnp.exp(masked - row_max)
    return exponent / lax.optimization_barrier(jnp.sum(exponent, axis=-1, keepdims=True))

def to_heads(layer_rows):
    return layer_rows.reshape(layer_rows.shape[0], H, HD).transpose(1, 0, 2)

def item_layer(params, long_rows, glob_rows, count_now):
    w_query, b_query, w_key, w_value, b_value, w_out, b_out, rel_table, gain_one, shift_one, w_up, b_up, w_down, b_down, gain_two, shift_two = params
    layer_rows = jnp.concatenate([long_rows, glob_rows], 0)
    row_count = layer_rows.shape[0]
    score_scale = 1.0 / math.sqrt(HD)
    queries = low_back(low(matmul(layer_rows, w_query) + b_query))
    keys_all = low_back(low(matmul(layer_rows, w_key)))
    values_all = low_back(low(matmul(layer_rows, w_value) + b_value))
    query_heads = to_heads(queries)
    key_heads = to_heads(keys_all)
    value_heads = to_heads(values_all)
    table_heads = to_heads(rel_table)
    positions = jnp.arange(L, dtype=jnp.int32)
    offset = positions[None, :] - positions[:, None]
    labels = jnp.clip(offset + R, 0, 2 * R)
    live_slot = jnp.arange(G, dtype=jnp.int32) < count_now
    slot_of = positions * count_now // L
    long_query = query_heads[:, :L]
    direct = jnp.einsum('hid,hjd->hij', long_query, key_heads, precision=lax.Precision.HIGHEST)
    relative = jnp.einsum('hid,hld->hil', long_query, table_heads, precision=lax.Precision.HIGHEST)
    rel_full = jnp.take_along_axis(relative, jnp.broadcast_to(labels, (H, L, L)), axis=2)
    extra_term = jnp.pad(rel_full, ((0, 0), (0, 0), (0, G)))
    long_scores = low_back((direct + extra_term) * score_scale)
    long_allowed = jnp.concatenate([jnp.abs(offset) <= R, jnp.broadcast_to(live_slot[None, :], (L, G))], 1)
    long_probs = low(masked_softmax(long_scores, long_allowed[None]))
    long_result = jnp.einsum('hij,hjd->hid', long_probs, value_heads, precision=lax.Precision.HIGHEST)
    glob_scores = low_back(jnp.einsum('hid,hjd->hij', query_heads[:, L:], key_heads, precision=lax.Precision.HIGHEST) * score_scale)
    own_slot = (slot_of[None, :] == jnp.arange(G, dtype=jnp.int32)[:, None]) & live_slot[:, None]
    glob_allowed = jnp.concatenate([own_slot, jnp.broadcast_to(live_slot[None, :], (G, G))], 1)
    glob_probs = low(masked_softmax(glob_scores, glob_allowed[None]))
    glob_result = jnp.einsum('hij,hjd->hid', glob_probs, value_heads, precision=lax.Precision.HIGHEST)
    attended = jnp.concatenate([long_result, glob_result], 1).transpose(1, 0, 2).reshape(row_count, D)
    attended = low_back(low(attended))
    branch = low_back(matmul(attended, w_out) + b_out)
    normed = layer_norm(layer_rows + branch, gain_one, shift_one)
    hidden_pre = low_back(matmul(low(normed), w_up) + b_up)
    activated = low(jax.nn.gelu(hidden_pre, approximate=True))
    ffn_result = low_back(matmul(activated, w_down) + b_down)
    result = layer_norm(normed + ffn_result, gain_two, shift_two)
    row_live = jnp.concatenate([jnp.ones((L,), jnp.float32), live_slot.astype(jnp.float32)])
    result = result * row_live[:, None]
    return (result[:L], result[L:])

def reference(long_input, global_input, counts, w_query, b_query, w_key, w_value, b_value, w_out, b_out, rel_table, norm1_gain, norm1_bias, w_up, b_up, w_down, b_down, norm2_gain, norm2_bias, long_cot, global_cot):
    stacked = tuple((tensor.astype(jnp.float32) for tensor in (w_query, b_query, w_key, w_value, b_value, w_out, b_out, rel_table, norm1_gain, norm1_bias, w_up, b_up, w_down, b_down, norm2_gain, norm2_bias)))
    first_params = tuple((tensor[0] for tensor in stacked))
    second_params = tuple((tensor[1] for tensor in stacked))
    long_items = long_input.astype(jnp.float32).reshape(ITEMS, L, D)
    glob_items = global_input.astype(jnp.float32).reshape(ITEMS, G, D)
    long_extra = jnp.zeros_like(long_items)
    glob_extra = jnp.zeros_like(glob_items)

    def forward(long_rows_all, glob_rows_all, long_pad, glob_pad, params_one, params_two):

        def two_layers(inputs):
            long_rows, glob_rows, count_now, long_add, glob_add = inputs
            mid_long, mid_glob = item_layer(params_one, long_rows, glob_rows, count_now)
            mid_long = low(mid_long)
            mid_glob = low(mid_glob)
            next_long = low_back(mid_long) + long_add
            next_glob = low_back(mid_glob) + glob_add
            end_long, end_glob = item_layer(params_two, next_long, next_glob, count_now)
            return (mid_long, mid_glob, low(end_long), low(end_glob))
        return lax.map(jax.checkpoint(two_layers), (long_rows_all, glob_rows_all, counts, long_pad, glob_pad))
    outputs, pull = jax.vjp(forward, long_items, glob_items, long_extra, glob_extra, first_params, second_params)
    mid_long, mid_glob, end_long, end_glob = outputs
    cotangent = (jnp.zeros_like(long_items), jnp.zeros_like(glob_items), long_cot.astype(jnp.float32).reshape(ITEMS, L, D), global_cot.astype(jnp.float32).reshape(ITEMS, G, D))
    d_long, d_glob, d_long_next, d_glob_next, d_first, d_second = pull(cotangent)
    long_outputs = jnp.stack([mid_long.reshape(TOKENS, D), end_long.reshape(TOKENS, D)]).astype(jnp.bfloat16)
    global_outputs = jnp.stack([mid_glob.reshape(GTOT, D), end_glob.reshape(GTOT, D)]).astype(jnp.bfloat16)
    long_grads = jnp.stack([d_long.reshape(TOKENS, D), d_long_next.reshape(TOKENS, D)])
    global_grads = jnp.stack([d_glob.reshape(GTOT, D), d_glob_next.reshape(GTOT, D)])
    grad_w_query, grad_b_query, grad_w_key, grad_w_value, grad_b_value, grad_w_out, grad_b_out, grad_rel_table, grad_norm1_gain, grad_norm1_bias, grad_w_up, grad_b_up, grad_w_down, grad_b_down, grad_norm2_gain, grad_norm2_bias = tuple((jnp.stack([one_grad, two_grad]) for one_grad, two_grad in zip(d_first, d_second)))
    return (long_outputs, global_outputs, long_grads, global_grads, grad_w_query, grad_b_query, grad_w_key, grad_w_value, grad_b_value, grad_w_out, grad_b_out, grad_rel_table, grad_norm1_gain, grad_norm1_bias, grad_w_up, grad_b_up, grad_w_down, grad_b_down, grad_norm2_gain, grad_norm2_bias)
```

```python
import functools
import math

import jax
import jax.numpy as jnp
from jax import lax
from jax.experimental import pallas as pl
from jax.experimental.pallas import tpu as pltpu
from jax.sharding import PartitionSpec as P

H = 12
F32 = jnp.float32
BF16 = jnp.bfloat16
ANY = pl.BlockSpec(memory_space=pl.ANY)
SMEM = pl.BlockSpec(memory_space=pltpu.SMEM)
NEG = -1e30
(
    W_QUERY, W_KEY, W_VALUE, W_OUT, W_UP, W_DOWN, TABLE, B_QUERY, B_VALUE, B_OUT, NORM1_GAIN, NORM1_BIAS, B_UP, B_DOWN, NORM2_GAIN, NORM2_BIAS,
    D_FFN, D_HIDDEN, D_BRANCH, D_Q, D_K, D_V, S_X, S_Q, S_K, S_V, S_ATT, S_N1, S_XH1, S_XH2, S_U, S_GP, S_P, S_RS1, S_RS2, S_TAB,
) = range(36)


def mm(a, b):
    return jnp.dot(a, b, preferred_element_type=F32)


def mm_t(a, b):
    return lax.dot_general(a, b, (((1,), (1,)), ((), ())), preferred_element_type=F32)


def mm_c(a, b):
    return lax.dot_general(a, b, (((0,), (0,)), ((), ())), preferred_element_type=F32)


class Copies:
    def __init__(self, sems):
        self.sems = sems
        self.used = 0

    def make(self, src, dst):
        copy = pltpu.make_async_copy(src, dst, self.sems.at[self.used])
        self.used += 1
        return copy

    def start(self, src, dst):
        copy = self.make(src, dst)
        copy.start()
        return copy

    def choose(self, first, src_a, src_b, dst):
        a = pltpu.make_async_copy(src_a, dst, self.sems.at[self.used])
        b = pltpu.make_async_copy(src_b, dst, self.sems.at[self.used])
        self.used += 1
        pl.when(first)(a.start)
        pl.when(jnp.logical_not(first))(b.start)
        return a


def normalize(rows):
    center = rows - jnp.mean(rows, axis=-1, keepdims=True)
    spread = jnp.mean(center * center, axis=-1, keepdims=True)
    rstd = lax.rsqrt(spread + 1e-05)
    return center * rstd, rstd


GELU_C = math.sqrt(2.0 / math.pi)


def gelu_parts(z):
    zz = z * z
    t = jnp.tanh(z * (GELU_C + (GELU_C * 0.044715) * zz))
    half = 0.5 + 0.5 * t
    slope = half + (0.5 * z) * (1.0 - t * t) * (GELU_C + (3.0 * GELU_C * 0.044715) * zz)
    return z * half, slope


WEIGHTS = (
    W_QUERY, W_KEY, W_VALUE, W_OUT, W_UP, W_DOWN, TABLE,
    B_QUERY, B_VALUE, B_OUT, NORM1_GAIN, NORM1_BIAS, B_UP, B_DOWN, NORM2_GAIN, NORM2_BIAS,
)
STATE = (S_X, S_Q, S_K, S_V, S_ATT, S_N1, S_XH1, S_XH2, S_U, S_GP, S_P, S_RS1, S_RS2)


def state_shapes(items, rows, width, hidden, keys):
    low = lambda *s: jax.ShapeDtypeStruct((items,) + s, BF16)
    shapes = {name: low(rows, width) for name in (S_X, S_Q, S_K, S_V, S_ATT, S_N1, S_XH1, S_XH2)}
    shapes[S_U] = shapes[S_GP] = low(rows, hidden)
    shapes[S_P] = low(H, rows, keys)
    shapes[S_RS1] = shapes[S_RS2] = jax.ShapeDtypeStruct((items, rows, 128), F32)
    return [shapes[name] for name in STATE]


def head_masks():
    lane = lax.broadcasted_iota(jnp.int32, (1, 128), 1)
    return [lane < 64, lane >= 64]


def fwd_kernel(cfg, *refs):
    seq, slots, radius, first_call = cfg
    rows = seq + slots
    meta, x_long, x_glob, recv = refs[:4]
    w_hbm = dict(zip(WEIGHTS, refs[4:20]))
    refs = refs[20:]
    if not first_call:
        refs = refs[len(STATE) + 2:]
    st = dict(zip(STATE, refs[:len(STATE)]))
    long_out, glob_out, y_send = refs[len(STATE):len(STATE) + 3]
    refs = refs[len(STATE) + 3:]
    w = dict(zip(WEIGHTS, refs[:16]))
    sc = dict(zip(STATE, refs[16:16 + len(STATE)]))
    y_v, vc, bandm, ownm, sems = refs[16 + len(STATE):]
    item, count, active, from_recv = meta[0], meta[1], meta[2], meta[3]

    @pl.when(active == 1)
    def _():
        cp = Copies(sems)
        fresh = from_recv == 0
        long_rows = pl.ds(pl.multiple_of(item * seq, seq), seq)
        glob_rows = pl.ds(pl.multiple_of(item * slots, slots), slots)
        c_x = cp.choose(fresh, x_long.at[long_rows], recv.at[0:seq], sc[S_X].at[0:seq])
        c_g = cp.choose(fresh, x_glob.at[glob_rows], recv.at[seq:rows], sc[S_X].at[seq:rows])
        loads = {}
        for name in (W_QUERY, B_QUERY, W_KEY, W_VALUE, B_VALUE, TABLE, W_OUT, B_OUT, NORM1_GAIN,
                     NORM1_BIAS, W_UP, B_UP, W_DOWN, B_DOWN, NORM2_GAIN, NORM2_BIAS):
            dst = w[name].at[0:w_hbm[name].shape[0]] if name == TABLE else w[name]
            loads[name] = cp.start(w_hbm[name], dst)
        outs = []

        def save(name):
            outs.append(cp.start(sc[name], st[name].at[item]))

        def vec(name):
            loads[name].wait()
            return w[name][...].astype(F32)

        row = lax.broadcasted_iota(jnp.int32, (seq, seq), 0)
        col = lax.broadcasted_iota(jnp.int32, (seq, seq), 1)
        bandm[...] = jnp.where(jnp.abs(col - row) <= radius, 0.0, NEG)
        key = lax.broadcasted_iota(jnp.int32, (slots, seq), 1)
        slot = lax.broadcasted_iota(jnp.int32, (slots, seq), 0)
        ownm[...] = jnp.where(lax.div(key * count, jnp.int32(seq)) == slot, 0.0, NEG)
        lane = lax.broadcasted_iota(jnp.int32, (1, 128), 1)
        globm = jnp.where((lane >= 64) & (lane < 64 + count), 0.0, NEG)
        vc[seq:, :] = jnp.zeros((128, vc.shape[1]), BF16)
        tab = w[TABLE]
        tab[192:, :] = jnp.zeros((tab.shape[0] - 192, tab.shape[1]), BF16)

        c_x.wait()
        c_g.wait()
        x = sc[S_X][...]
        save(S_X)
        loads[W_QUERY].wait()
        sc[S_Q][...] = (mm(x, w[W_QUERY][...]) + vec(B_QUERY)).astype(BF16)
        save(S_Q)
        loads[W_KEY].wait()
        k = mm(x, w[W_KEY][...]).astype(BF16)
        sc[S_K][...] = k
        save(S_K)
        loads[W_VALUE].wait()
        v = (mm(x, w[W_VALUE][...]) + vec(B_VALUE)).astype(BF16)
        sc[S_V][...] = v
        save(S_V)
        vc[0:seq, :] = v[0:seq]
        vc[seq + 64:seq + 64 + slots, :] = v[seq:rows]
        loads[TABLE].wait()
        tab[192:192 + slots, :] = k[seq:rows]
        halves = head_masks()

        def pair(p, carry):
            cols = pl.ds(pl.multiple_of(p * 128, 128), 128)
            qp = sc[S_Q][:, cols]
            kp = sc[S_K][0:seq, cols]
            rk = tab[:, cols]
            vp = vc[:, cols]
            got = []
            for hh in range(2):
                qm = jnp.where(halves[hh], qp, jnp.zeros_like(qp))
                s1 = mm_t(qm, kp)
                s2 = mm_t(qm, rk)
                band = pltpu.roll(s2[0:seq], (2 * seq - radius - 12) % seq, 1, stride=1, stride_axis=0)
                parts = []
                for sl, sg in (
                    ((s1[0:seq] + band) * 0.125 + bandm[...], s2[0:seq, 128:256] * 0.125 + globm),
                    (s1[seq:rows] * 0.125 + ownm[...], s2[seq:rows, 128:256] * 0.125 + globm),
                ):
                    top = jnp.maximum(jnp.max(sl, axis=-1, keepdims=True), jnp.max(sg, axis=-1, keepdims=True))
                    el = jnp.exp(sl - top)
                    eg = jnp.exp(sg - top)
                    total = jnp.sum(el, axis=-1, keepdims=True) + jnp.sum(eg, axis=-1, keepdims=True)
                    inv = 1.0 / total
                    parts.append(((el * inv).astype(BF16), (eg * inv).astype(BF16)))
                h = p * 2 + hh
                sc[S_P][h, 0:seq, 0:seq] = parts[0][0]
                sc[S_P][h, 0:seq, seq:] = parts[0][1]
                sc[S_P][h, seq:rows, 0:seq] = parts[1][0]
                sc[S_P][h, seq:rows, seq:] = parts[1][1]
                got.append(mm(sc[S_P][h], vp))
            sc[S_ATT][:, cols] = jnp.where(halves[0], got[0], got[1]).astype(BF16)
            return carry

        lax.fori_loop(0, H // 2, pair, 0)
        save(S_P)
        save(S_ATT)
        loads[W_OUT].wait()
        r1 = x.astype(F32) + mm(sc[S_ATT][...], w[W_OUT][...]) + vec(B_OUT)
        xh1, rstd1 = normalize(r1)
        sc[S_XH1][...] = xh1.astype(BF16)
        save(S_XH1)
        sc[S_RS1][...] = jnp.broadcast_to(rstd1, (rows, 128))
        save(S_RS1)
        n1 = xh1 * vec(NORM1_GAIN) + vec(NORM1_BIAS)
        n1_low = n1.astype(BF16)
        sc[S_N1][...] = n1_low
        save(S_N1)
        hidden = w[W_UP].shape[1]
        step = 768
        loads[W_UP].wait()
        b_up = vec(B_UP)
        acc = n1 + vec(B_DOWN)
        for c in range(hidden // step):
            z = mm(n1_low, w[W_UP][:, c * step:(c + 1) * step]) + b_up[:, c * step:(c + 1) * step]
            act, slope = gelu_parts(z)
            act = act.astype(BF16)
            sc[S_U][:, c * step:(c + 1) * step] = act
            sc[S_GP][:, c * step:(c + 1) * step] = slope.astype(BF16)
            if c == 0:
                loads[W_DOWN].wait()
            acc = acc + mm(act, w[W_DOWN][c * step:(c + 1) * step, :])
        save(S_U)
        save(S_GP)
        xh2, rstd2 = normalize(acc)
        sc[S_XH2][...] = xh2.astype(BF16)
        save(S_XH2)
        sc[S_RS2][...] = jnp.broadcast_to(rstd2, (rows, 128))
        save(S_RS2)
        y = xh2 * vec(NORM2_GAIN) + vec(NORM2_BIAS)
        pos = lax.broadcasted_iota(jnp.int32, (rows, 1), 0)
        y = jnp.where(pos < seq + count, y, 0.0)
        y_v[...] = y.astype(BF16)
        outs.append(cp.start(y_v, y_send))
        outs.append(cp.start(y_v.at[0:seq], long_out.at[long_rows]))
        outs.append(cp.start(y_v.at[seq:rows], glob_out.at[glob_rows]))
        for copy in outs:
            copy.wait()


def vm(shape, dtype=BF16):
    return pltpu.VMEM(shape, dtype)


def run_forward(meta, x_long, x_glob, recv, weights, state, outs, seq, slots, radius):
    rows, width = seq + slots, x_long.shape[1]
    hidden = weights[4].shape[1]
    items = x_long.shape[0] // seq
    keys = seq + 128
    shapes = state_shapes(items, rows, width, hidden, keys)
    out_shape = shapes + [
        jax.ShapeDtypeStruct(x_long.shape, BF16),
        jax.ShapeDtypeStruct(x_glob.shape, BF16),
        jax.ShapeDtypeStruct((rows, width), BF16),
    ]
    first = state is None
    operands = [meta, x_long, x_glob, recv] + list(weights)
    aliases = {}
    if not first:
        base = len(operands)
        operands += list(state) + list(outs)
        aliases = {base + n: n for n in range(len(state) + 2)}
    scratch = []
    for name, t in zip(WEIGHTS, weights):
        scratch.append(vm((256, width)) if name == TABLE else vm(t.shape))
    scratch += [vm(s.shape[1:], s.dtype) for s in shapes]
    scratch += [vm((rows, width)), vm((keys, width)), vm((seq, seq), F32), vm((slots, seq), F32),
                pltpu.SemaphoreType.DMA((48,))]
    result = pl.pallas_call(
        functools.partial(fwd_kernel, (seq, slots, radius, first)),
        out_shape=out_shape,
        in_specs=[SMEM] + [ANY] * (len(operands) - 1),
        out_specs=[ANY] * len(out_shape),
        scratch_shapes=scratch,
        input_output_aliases=aliases,
        compiler_params=pltpu.CompilerParams(vmem_limit_bytes=60 << 20),
        name="layer_forward",
    )(*operands)
    n = len(STATE)
    return result[:n], result[n:n + 2], result[n + 2]


USED = (S_Q, S_K, S_V, S_XH1, S_XH2, S_GP, S_P, S_RS1, S_RS2)
FACTORS = (D_FFN, D_HIDDEN, D_BRANCH, D_Q, D_K, D_V)
BWEIGHTS = (W_QUERY, W_KEY, W_VALUE, W_OUT, W_UP, W_DOWN, TABLE, NORM1_GAIN, NORM2_GAIN)


def bwd_kernel(cfg, *refs):
    seq, slots, radius, first_call = cfg
    rows = seq + slots
    meta, c_long, c_glob, recv = refs[:4]
    w_hbm = dict(zip(BWEIGHTS, refs[4:13]))
    st = dict(zip(USED, refs[13:22]))
    refs = refs[22:]
    n_out = len(FACTORS) + 3
    if not first_call:
        refs = refs[n_out:]
    fac = dict(zip(FACTORS, refs[:6]))
    tab_out, long_back, glob_back, d_send = refs[6:10]
    refs = refs[10:]
    w = dict(zip(BWEIGHTS, refs[:9]))
    sc = dict(zip(USED, refs[9:18]))
    fs = dict(zip(FACTORS, refs[18:24]))
    dy, da, dx, dx_low, tab_s, small, flip, vc, sems = refs[24:]
    item, count, active, from_recv = meta[0], meta[1], meta[2], meta[3]

    @pl.when(active == 1)
    def _():
        cp = Copies(sems)
        fresh = from_recv == 0
        long_rows = pl.ds(pl.multiple_of(item * seq, seq), seq)
        glob_rows = pl.ds(pl.multiple_of(item * slots, slots), slots)
        c_y = cp.choose(fresh, c_long.at[long_rows], recv.at[0:seq], dy.at[0:seq])
        c_g = cp.choose(fresh, c_glob.at[glob_rows], recv.at[seq:rows], dy.at[seq:rows])
        loads = {}
        for name in (NORM2_GAIN, S_XH2, S_RS2, W_DOWN, S_GP, W_UP, NORM1_GAIN, S_XH1, S_RS1, W_OUT, S_Q, S_K, S_V,
                     TABLE, S_P, W_QUERY, W_KEY, W_VALUE):
            if name in w:
                dst = w[name].at[0:w_hbm[name].shape[0]] if name == TABLE else w[name]
                loads[name] = cp.start(w_hbm[name], dst)
            else:
                loads[name] = cp.start(st[name].at[item], sc[name])
        outs = []

        def save(name):
            outs.append(cp.start(fs[name], fac[name].at[item]))

        row = lax.broadcasted_iota(jnp.int32, (seq, seq), 0)
        col = lax.broadcasted_iota(jnp.int32, (seq, seq), 1)
        turn = (radius + 12) % seq
        flip[...] = jnp.where((row + col == turn) | (row + col == turn + seq), 1.0, 0.0).astype(BF16)
        vc[seq:, :] = jnp.zeros((128, vc.shape[1]), BF16)
        tab = w[TABLE]
        tab[192:, :] = jnp.zeros((tab.shape[0] - 192, tab.shape[1]), BF16)
        small[...] = jnp.zeros_like(small)
        pos = lax.broadcasted_iota(jnp.int32, (rows, 1), 0)

        def norm_back(grad, xh, rstd, gain, at):
            small[at:at + 1, :] = jnp.sum(grad * xh, axis=0, keepdims=True)
            small[at + 1:at + 2, :] = jnp.sum(grad, axis=0, keepdims=True)
            dxh = grad * gain
            return rstd * (
                dxh - jnp.mean(dxh, axis=-1, keepdims=True) - xh * jnp.mean(dxh * xh, axis=-1, keepdims=True)
            )

        c_y.wait()
        c_g.wait()
        grad = jnp.where(pos < seq + count, dy[...].astype(F32), 0.0)
        for name in (NORM2_GAIN, S_XH2, S_RS2):
            loads[name].wait()
        d_second = norm_back(
            grad, sc[S_XH2][...].astype(F32), sc[S_RS2][:, 0:1], w[NORM2_GAIN][...].astype(F32), 70
        )
        d_ffn = d_second.astype(BF16)
        fs[D_FFN][...] = d_ffn
        save(D_FFN)
        small[69:70, :] = jnp.sum(d_ffn.astype(F32), axis=0, keepdims=True)
        loads[W_DOWN].wait()
        loads[S_GP].wait()
        hidden = w[W_UP].shape[1]
        step = small.shape[1]
        d_normed = d_second
        for c in range(hidden // step):
            sl = slice(c * step, (c + 1) * step)
            d_hid = (sc[S_GP][:, sl].astype(F32) * mm_t(d_ffn, w[W_DOWN][sl, :])).astype(BF16)
            fs[D_HIDDEN][:, sl] = d_hid
            if c == 0:
                loads[W_UP].wait()
            d_normed = d_normed + mm_t(d_hid, w[W_UP][:, sl])
        save(D_HIDDEN)
        for name in (NORM1_GAIN, S_XH1, S_RS1):
            loads[name].wait()
        d_first = norm_back(
            d_normed, sc[S_XH1][...].astype(F32), sc[S_RS1][:, 0:1], w[NORM1_GAIN][...].astype(F32), 67
        )
        d_branch = d_first.astype(BF16)
        fs[D_BRANCH][...] = d_branch
        save(D_BRANCH)
        small[66:67, :] = jnp.sum(d_branch.astype(F32), axis=0, keepdims=True)
        dx[...] = d_first
        loads[W_OUT].wait()
        da[...] = mm_t(d_branch, w[W_OUT][...]).astype(BF16)
        for name in (S_Q, S_K, S_V, TABLE, S_P):
            loads[name].wait()
        vc[0:seq, :] = sc[S_V][0:seq, :]
        vc[seq + 64:seq + 64 + slots, :] = sc[S_V][seq:rows, :]
        tab[192:192 + slots, :] = sc[S_K][seq:rows, :]
        halves = head_masks()
        label = lax.broadcasted_iota(jnp.int32, (1, 256), 1)
        own_label = (label >= 12) & (label < 12 + 2 * radius + 1)

        def pair(p, carry):
            cols = pl.ds(pl.multiple_of(p * 128, 128), 128)
            qp = sc[S_Q][:, cols]
            kp = sc[S_K][0:seq, cols]
            rk = tab[:, cols]
            vp = vc[:, cols]
            dap = da[:, cols]
            q_t = qp.T
            da_t = dap.T
            dq, dk_t, dv_t = [], [], []
            for hh in range(2):
                h = p * 2 + hh
                dam = jnp.where(halves[hh], dap, jnp.zeros_like(dap))
                prob_low = sc[S_P][h]
                prob = prob_low.astype(F32)
                d_prob = mm_t(dam, vp)
                delta = jnp.sum(prob * d_prob, axis=-1, keepdims=True)
                ds = (prob * (d_prob - delta)).astype(BF16)
                ds1 = ds[:, 0:seq]
                turned = mm(flip[...], ds1[0:seq]).astype(BF16)
                turned = pltpu.roll(turned, 0, 1, stride=1, stride_axis=0)
                rel = mm(flip[...], turned).astype(BF16)
                far = jnp.concatenate(
                    [
                        jnp.concatenate([rel[:, 0:128], rel[:, 128:256] + ds[0:seq, seq:]], 1),
                        jnp.concatenate([jnp.zeros((slots, 128), BF16), ds[seq:rows, seq:]], 1),
                    ],
                    0,
                )
                dq.append(mm(ds1, kp) + mm(far, rk))
                own = slice(64 * hh, 64 * hh + 64)
                dk_t.append(jnp.concatenate([mm(q_t[own], ds1), mm(q_t[own], far)], 1) * 0.125)
                dv_t.append(mm(da_t[own], prob_low))
            fs[D_Q][:, cols] = (jnp.where(halves[0], dq[0], dq[1]) * 0.125).astype(BF16)
            dk_t = jnp.concatenate(dk_t, 0)
            dv_t = jnp.concatenate(dv_t, 0)
            fs[D_K][0:seq, cols] = dk_t[:, 0:seq].T.astype(BF16)
            fs[D_K][seq:rows, cols] = dk_t[:, seq + 128:].T[64:64 + slots].astype(BF16)
            fs[D_V][0:seq, cols] = dv_t[:, 0:seq].T.astype(BF16)
            fs[D_V][seq:rows, cols] = dv_t[:, seq:].T[64:64 + slots].astype(BF16)
            tab_s[cols, :] = jnp.where(own_label, dk_t[:, seq:], 0.0)
            return carry

        lax.fori_loop(0, H // 2, pair, 0)
        save(D_Q)
        save(D_K)
        save(D_V)
        small[64:65, :] = jnp.sum(fs[D_Q][...].astype(F32), axis=0, keepdims=True)
        small[65:66, :] = jnp.sum(fs[D_V][...].astype(F32), axis=0, keepdims=True)
        for name in (W_QUERY, W_KEY, W_VALUE):
            loads[name].wait()
        d_rows = (
            dx[...]
            + mm_t(fs[D_Q][...], w[W_QUERY][...])
            + mm_t(fs[D_K][...], w[W_KEY][...])
            + mm_t(fs[D_V][...], w[W_VALUE][...])
        )
        dx[...] = d_rows
        dx_low[...] = d_rows.astype(BF16)
        outs.append(cp.start(dx_low, d_send))
        outs.append(cp.start(dx.at[0:seq], long_back.at[long_rows]))
        outs.append(cp.start(dx.at[seq:rows], glob_back.at[glob_rows]))
        tab_s[:, 128:] += small[...].T
        outs.append(cp.start(tab_s, tab_out.at[item]))
        for copy in outs:
            copy.wait()


def run_backward(meta, c_long, c_glob, recv, weights, state, made, seq, slots, radius):
    rows, width = seq + slots, c_long.shape[1]
    named = dict(zip(WEIGHTS, weights))
    kept = dict(zip(STATE, state))
    hidden = named[W_UP].shape[1]
    items = c_long.shape[0] // seq
    keys = seq + 128
    low = lambda n: jax.ShapeDtypeStruct((items, rows, n), BF16)
    out_shape = [low(width), low(hidden), low(width), low(width), low(width), low(width),
                 jax.ShapeDtypeStruct((items, width, 256), F32),
                 jax.ShapeDtypeStruct(c_long.shape, F32), jax.ShapeDtypeStruct(c_glob.shape, F32),
                 jax.ShapeDtypeStruct((rows, width), BF16)]
    operands = [meta, c_long, c_glob, recv] + [named[n] for n in BWEIGHTS] + [kept[n] for n in USED]
    first = made is None
    aliases = {}
    if not first:
        base = len(operands)
        operands += list(made)
        aliases = {base + n: n for n in range(len(made))}
    scratch = [vm((256, width)) if n == TABLE else vm(named[n].shape) for n in BWEIGHTS]
    scratch += [vm(kept[n].shape[1:], kept[n].dtype) for n in USED]
    scratch += [vm(s.shape[1:]) for s in out_shape[:6]]
    scratch += [vm((rows, width)), vm((rows, width)), vm((rows, width), F32), vm((rows, width)),
                vm((width, 256), F32), vm((128, width), F32), vm((seq, seq)), vm((keys, width)),
                pltpu.SemaphoreType.DMA((48,))]
    result = pl.pallas_call(
        functools.partial(bwd_kernel, (seq, slots, radius, first)),
        out_shape=out_shape,
        in_specs=[SMEM] + [ANY] * (len(operands) - 1),
        out_specs=[ANY] * len(out_shape),
        scratch_shapes=scratch,
        input_output_aliases=aliases,
        compiler_params=pltpu.CompilerParams(vmem_limit_bytes=60 << 20),
        name="layer_backward",
    )(*operands)
    return result[:9], result[9]


TILE = 16
MESH_ID = pl.DeviceIdType.MESH
NZ, NY, NX = 4, 2, 2
SHARDS = NZ * NY * NX
GRADS = (S_U, D_FFN, S_N1, D_HIDDEN, S_ATT, D_BRANCH, S_X, D_Q, D_K, D_V)
CHUNKS = ((2, 2, 1),) * 7 + ((0, 1, 1),)
STAGES = 6
BIAS_LANE = 72


def reduce_kernel(cfg, *refs):
    rows, width, hidden = cfg
    ins = dict(zip(GRADS, refs[:10]))
    tab_hbm, red = refs[10], refs[11]
    refs = refs[12:]
    buf = dict(zip(GRADS, refs[:10]))
    tab, extra, g, ax, ay, az, bx, by, bz, cx, cy, cz, load_sems, send_sems, recv_sems = refs[10:]
    section = lax.axis_index("section")
    me = lax.axis_index("dp")
    x, y, z = lax.rem(me, NX), lax.rem(lax.div(me, NX), NY), lax.div(me, NX * NY)

    def at(zz, yy, xx):
        return (section, (zz * NY + yy) * NX + xx)

    across_x, across_y = at(z, y, 1 - x), at(z, 1 - y, x)
    above, below = at(z + 1, y, x), at(z - 1, y, x)

    loads = {}
    for n, name in enumerate(GRADS):
        loads[name] = pltpu.make_async_copy(ins[name], buf[name], load_sems.at[n])
        loads[name].start()
    loads[S_TAB] = pltpu.make_async_copy(tab_hbm, tab, load_sems.at[10])
    loads[S_TAB].start()

    barrier = pltpu.get_barrier_semaphore()
    for other in (across_x, across_y):
        pl.semaphore_signal(barrier, inc=1, device_id=other, device_id_type=MESH_ID)

    @pl.when(z > 0)
    def _():
        pl.semaphore_signal(barrier, inc=1, device_id=below, device_id_type=MESH_ID)

    @pl.when(z < NZ - 1)
    def _():
        pl.semaphore_signal(barrier, inc=1, device_id=above, device_id_type=MESH_ID)

    ready = set()

    def need(*names):
        for name in names:
            if name not in ready:
                ready.add(name)
                loads[name].wait()

    wide, narrow = hidden // SHARDS, width // SHARDS

    def form_wide(left, right, at_row, bias=False):
        need(left, right)
        lane = lax.broadcasted_iota(jnp.int32, (1, 128), 1)
        ones = jnp.ones((rows, 128), BF16)

        def body(n, carry):
            cols = pl.ds(pl.multiple_of(n * 2 * wide, 2 * wide), 2 * wide)
            part = mm_c(buf[left][:, cols], buf[right][...]).astype(BF16)
            g[lax.div(n, NY), lax.rem(n, NY), 0, at_row:at_row + wide, :] = part[0:wide]
            g[lax.div(n, NY), lax.rem(n, NY), 1, at_row:at_row + wide, :] = part[wide:]
            if bias:
                sums = mm_c(buf[left][:, cols], ones)
                for side in range(2):
                    block = jnp.zeros((narrow, 128), F32)
                    for k in range(wide // narrow):
                        here = sums[side * wide + k * narrow:side * wide + (k + 1) * narrow]
                        block = jnp.where(lane == BIAS_LANE + k, here, block)
                    extra[pl.ds(pl.multiple_of((2 * n + side) * narrow, narrow), narrow), :] = block
            return carry

        lax.fori_loop(0, SHARDS // 2, body, 0)

    def form_narrow(left, right, at_row):
        need(left, right)

        def body(n, carry):
            cols = pl.ds(pl.multiple_of(n * 8 * narrow, 8 * narrow), 8 * narrow)
            part = mm_c(buf[left][:, cols], buf[right][...]).astype(BF16)
            for k in range(8):
                g[2 * n + k // 4, (k // 2) % 2, k % 2, at_row:at_row + narrow, :] = part[k * narrow:(k + 1) * narrow]
            return carry

        lax.fori_loop(0, SHARDS // 8, body, 0)

    def form_table(at_row):
        need(S_TAB)
        third = narrow // TILE

        def body(n, carry):
            for k in range(third):
                rows_k = pl.ds(pl.multiple_of(n * narrow + k * TILE, TILE), TILE)
                part = tab[0, rows_k, :] + tab[1, rows_k, :]
                shard = g.at[lax.div(n, 4), lax.rem(lax.div(n, 2), 2), lax.rem(n, 2), at_row:at_row + TILE]
                shard[:, 256 * k:256 * k + 128] = part[:, 0:128].astype(BF16)
                shard[:, 256 * k + 128:256 * k + 256] = (part[:, 128:] + extra[rows_k, :]).astype(BF16)
            return carry

        lax.fori_loop(0, SHARDS, body, 0)

    first = [0]
    for a, b, c in CHUNKS:
        first.append(first[-1] + a + b + c)

    def spans(chunk, route):
        counts = CHUNKS[chunk]
        start = first[chunk] + sum(counts[:route])
        own = sum(CHUNKS[n][route] for n in range(chunk))
        size = counts[route] * TILE
        return slice(start * TILE, start * TILE + size), slice(own * TILE, own * TILE + size), size

    pending = []

    def remote(src, dst, index, target):
        return pltpu.make_async_remote_copy(
            src_ref=src, dst_ref=dst, send_sem=send_sems.at[index], recv_sem=recv_sems.at[index],
            device_id=target, device_id_type=MESH_ID,
        )

    def send(src, dst, index, target):
        remote(src, dst, index, target).start()
        pending.append((None, lambda: remote(src, dst, index, target).wait_send()))

    def add(dst, src, lead):
        total = 1
        for n in lead:
            total *= n

        def body(n, carry):
            idx, rest = [], n
            for size in reversed(lead):
                idx.insert(0, lax.rem(rest, size))
                rest = lax.div(rest, size)
            d, s = dst(*idx), src(*idx)
            d[...] = (d[...].astype(F32) + s[...].astype(F32)).astype(BF16)
            return carry

        if total == 1:
            body(0, 0)
        else:
            lax.fori_loop(0, total, body, 0)

    def flow_z(stage, own, room, base, lead):
        def slot_index(slot):
            return base + slot

        def take(shard, slot, source):
            copy = remote(own(shard), room(slot), slot_index(slot), source)
            copy.wait_recv()
            add(lambda *i: own(shard).at[i] if i else own(shard), lambda *i: room(slot).at[i] if i else room(slot), lead)

        def put(zz, shard, target):
            slot = NZ if (shard < zz and shard == zz - 1) else shard
            remote(own(shard), room(slot), slot_index(slot), target).start()
            pending.append((zz, lambda: remote(own(shard), room(slot), slot_index(slot), target).wait_send()))

        for zz in range(NZ):
            @pl.when(z == zz)
            def _():
                if zz > 0 and stage == zz:
                    for shard in range(NZ - 1, zz - 1, -1):
                        take(shard, shard, below)
                        if shard > zz:
                            put(zz, shard, above)
                elif zz == 0 and stage == 0:
                    for shard in range(NZ - 1, 0, -1):
                        put(zz, shard, above)
                if zz < NZ - 1 and stage == NZ - 1 - zz:
                    for shard in range(zz + 1):
                        take(shard, NZ if shard == zz else shard, above)
                        if shard < zz:
                            put(zz, shard, below)
                elif zz == NZ - 1 and stage == 0:
                    for shard in range(NZ - 1):
                        put(zz, shard, below)

    per_chunk = 21

    def run(chunk, route, stage):
        rs, own, size = spans(chunk, route)
        if size == 0:
            return
        base = chunk * per_chunk + route * 7
        if route == 0:
            if stage == 0:
                send(g.at[:, :, 1 - x, rs], ax.at[:, :, own], base, across_x)
            if stage == 1:
                remote(g.at[:, :, 1 - x, rs], ax.at[:, :, own], base, across_x).wait_recv()
                add(lambda i, j: g.at[i, j, x, rs], lambda i, j: ax.at[i, j, own], (NZ, NY))
                send(g.at[:, 1 - y, x, rs], ay.at[:, own], base + 1, across_y)
            if stage == 2:
                remote(g.at[:, 1 - y, x, rs], ay.at[:, own], base + 1, across_y).wait_recv()
                add(lambda i: g.at[i, y, x, rs], lambda i: ay.at[i, own], (NZ,))
            if stage >= 2:
                flow_z(stage - 2, lambda s: g.at[s, y, x, rs], lambda s: az.at[s, own], base + 2, ())
        if route == 1:
            if stage == 0:
                send(g.at[:, 1 - y, :, rs], by.at[:, :, own], base, across_y)
            if stage == 1:
                remote(g.at[:, 1 - y, :, rs], by.at[:, :, own], base, across_y).wait_recv()
                add(lambda i, j: g.at[i, y, j, rs], lambda i, j: by.at[i, j, own], (NZ, NX))
                send(g.at[:, y, 1 - x, rs], bx.at[:, own], base + 1, across_x)
            if stage == 2:
                remote(g.at[:, y, 1 - x, rs], bx.at[:, own], base + 1, across_x).wait_recv()
                add(lambda i: g.at[i, y, x, rs], lambda i: bx.at[i, own], (NZ,))
            if stage >= 2:
                flow_z(stage - 2, lambda s: g.at[s, y, x, rs], lambda s: bz.at[s, own], base + 2, ())
        if route == 2:
            if stage <= 3:
                flow_z(stage, lambda s: g.at[s, :, :, rs], lambda s: cz.at[s, :, :, own], base + 2, (NY, NX))
            if stage == 3:
                send(g.at[z, :, 1 - x, rs], cx.at[:, own], base, across_x)
            if stage == 4:
                remote(g.at[z, :, 1 - x, rs], cx.at[:, own], base, across_x).wait_recv()
                add(lambda i: g.at[z, i, x, rs], lambda i: cx.at[i, own], (NY,))
                send(g.at[z, 1 - y, x, rs], cy.at[own], base + 1, across_y)
            if stage == 5:
                remote(g.at[z, 1 - y, x, rs], cy.at[own], base + 1, across_y).wait_recv()
                add(lambda: g.at[z, y, x, rs], lambda: cy.at[own], ())
        if stage == 5:
            red[rs, :] = g[z, y, x, rs, :].astype(F32)

    forms = [
        (0, lambda: form_wide(S_U, D_FFN, 0)),
        (wide, lambda: form_wide(D_HIDDEN, S_N1, wide, True)),
        (2 * wide, lambda: form_narrow(D_BRANCH, S_ATT, 2 * wide)),
        (2 * wide + narrow, lambda: form_narrow(D_Q, S_X, 2 * wide + narrow)),
        (2 * wide + 2 * narrow, lambda: form_narrow(D_K, S_X, 2 * wide + 2 * narrow)),
        (2 * wide + 3 * narrow, lambda: form_narrow(D_V, S_X, 2 * wide + 3 * narrow)),
        (2 * wide + 4 * narrow, lambda: form_table(2 * wide + 4 * narrow)),
    ]
    entered = False
    for slot in range(len(CHUNKS) + STAGES - 1):
        if slot < len(CHUNKS):
            while forms and forms[0][0] < first[slot + 1] * TILE:
                forms.pop(0)[1]()
            if not entered:
                entered = True

                @pl.when((z == 0) | (z == NZ - 1))
                def _():
                    pl.semaphore_wait(barrier, 3)

                @pl.when((z > 0) & (z < NZ - 1))
                def _():
                    pl.semaphore_wait(barrier, 4)

        for stage in range(STAGES):
            chunk = slot - stage
            if 0 <= chunk < len(CHUNKS):
                for route in (2, 0, 1):
                    run(chunk, route, stage)
    for zz, wait in pending:
        if zz is None:
            wait()
        else:
            pl.when(z == zz)(wait)


def reduce_grads(parts, tab):
    rows, width = parts[S_X].shape
    hidden = parts[S_U].shape[1]
    share = 2 * (hidden // SHARDS) + 4 * (width // SHARDS) + TILE
    t = [sum(c[n] for c in CHUNKS) * TILE for n in range(3)]
    assert sum(t) == share
    n_sem = len(CHUNKS) * 21
    scratch = [vm(parts[n].shape) for n in GRADS]
    scratch += [
        vm(tab.shape, F32), vm((width, 128), F32),
        vm((NZ, NY, NX, share, width)),
        vm((NZ, NY, t[0], width)), vm((NZ, t[0], width)), vm((NZ + 1, t[0], width)),
        vm((NZ, t[1], width)), vm((NZ, NX, t[1], width)), vm((NZ + 1, t[1], width)),
        vm((NY, t[2], width)), vm((t[2], width)), vm((NZ + 1, NY, NX, t[2], width)),
        pltpu.SemaphoreType.DMA((11,)), pltpu.SemaphoreType.DMA((n_sem,)), pltpu.SemaphoreType.DMA((n_sem,)),
    ]
    return pl.pallas_call(
        functools.partial(reduce_kernel, (rows, width, hidden)),
        out_shape=jax.ShapeDtypeStruct((share, width), F32),
        in_specs=[ANY] * 11,
        out_specs=pl.BlockSpec(memory_space=pltpu.VMEM),
        scratch_shapes=scratch,
        compiler_params=pltpu.CompilerParams(collective_id=0, has_side_effects=True, vmem_limit_bytes=62 << 20),
        name="reduce_grads",
    )(*[parts[n] for n in GRADS], tab)


def share_of(red, width, hidden):
    wide, narrow = hidden // SHARDS, width // SHARDS
    low = 2 * wide
    cut = [red[low + n * narrow:low + (n + 1) * narrow].T for n in range(4)]
    packed = red[low + 4 * narrow:]
    table = jnp.concatenate([packed[:, 256 * k:256 * k + 256] for k in range(narrow // TILE)], 0)
    return cut, red[wide:low].T, red[0:wide], table


def sums_elsewhere(parts, tab):
    def scatter(value, dim):
        return lax.psum_scatter(value, "dp", scatter_dimension=dim, tiled=True)

    cut = [scatter(mm_c(parts[a], parts[b]), 1)
           for a, b in ((S_ATT, D_BRANCH), (S_X, D_Q), (S_X, D_K), (S_X, D_V))]
    w_up = scatter(mm_c(parts[S_N1], parts[D_HIDDEN]), 1)
    w_down = scatter(mm_c(parts[S_U], parts[D_FFN]), 0)
    b_up = scatter(jnp.sum(parts[D_HIDDEN].astype(F32), axis=0), 0)
    return cut, w_up, w_down, scatter(tab[0] + tab[1], 0), b_up


def per_device(
    long_input, global_input, counts, w_query, b_query, w_key, w_value, b_value, w_out, b_out, rel_table,
    norm1_gain, norm1_bias, w_up, b_up, w_down, b_down, norm2_gain, norm2_bias, long_cot, global_cot,
):
    items = counts.shape[0]
    seq, slots, width = long_input.shape[0] // items, global_input.shape[0] // items, long_input.shape[1]
    rows, hidden = seq + slots, w_up.shape[2]
    labels = rel_table.shape[1]
    radius = (labels - 1) // 2
    section = lax.axis_index("section")
    weights = [w_query[0], w_key[0], w_value[0], w_out[0], w_up[0], w_down[0],
               jnp.pad(rel_table[0], ((12, 192 - 12 - labels), (0, 0))),
               b_query, b_value, b_out, norm1_gain, norm1_bias, b_up, b_down, norm2_gain, norm2_bias]

    def meta_of(item):
        active = (item >= 0) & (item < items)
        item = jnp.clip(item, 0, items - 1)
        return [item, lax.dynamic_index_in_dim(counts, item, keepdims=False), active.astype(jnp.int32)]

    recv = jnp.zeros((rows, width), BF16)
    state = outs = None
    for step in range(items + 1):
        meta = jnp.stack(meta_of(step - section) + [section])
        state, outs, sent = run_forward(
            meta, long_input, global_input, recv, weights, state, outs, seq, slots, radius)
        if step < items:
            recv = lax.ppermute(sent, "section", [(0, 1)])
    made = None
    for step in range(items + 1):
        meta = jnp.stack(meta_of(step - (1 - section)) + [1 - section])
        made, sent = run_backward(meta, long_cot, global_cot, recv, weights, state, made, seq, slots, radius)
        if step < items:
            recv = lax.ppermute(sent, "section", [(1, 0)])
    kept = dict(zip(STATE, state))
    parts = {n: kept[n] for n in (S_X, S_ATT, S_N1, S_U)}
    parts.update(zip(FACTORS, made[:6]))
    parts = {n: t.reshape(items * rows, t.shape[2]) for n, t in parts.items()}
    tab, long_back, glob_back = made[6:9]
    if lax.axis_size("dp") == SHARDS:
        cut, g_up, g_down, table = share_of(reduce_grads(parts, tab), width, hidden)
        g_b_up = jnp.concatenate([table[:, 128 + BIAS_LANE + k] for k in range(hidden // width)], 0)
    else:
        cut, g_up, g_down, table, g_b_up = sums_elsewhere(parts, tab)
    g_out, g_query, g_key, g_value = cut
    small = [table[:, 192 + n] for n in range(8)]
    g_bq, g_bv, g_bo, g_g1, g_s1, g_bd, g_g2, g_s2 = small
    grads = (g_query, g_bq, g_key, g_value, g_bv, g_out, g_bo, table[:, 12:12 + labels].T, g_g1, g_s1,
             g_up, g_b_up, g_down, g_bd, g_g2, g_s2)
    return tuple(t[None] for t in (outs[0], outs[1], long_back, glob_back) + grads)


def solution(mesh):
    part = P("section", "dp", None)
    vector = P("section", "dp")
    columns = P("section", None, "dp")
    matrix = P("section", None, None)
    row = P("section", None)
    items = P("dp", None)
    in_specs = (items, items, P("dp"), matrix, row, matrix, matrix, row, matrix, row, matrix, row, row,
                matrix, row, matrix, row, row, row, items, items)
    out_specs = (part, part, part, part, columns, vector, columns, columns, vector, columns, vector, columns,
                 vector, vector, columns, vector, part, vector, vector, vector)
    return jax.shard_map(per_device, mesh=mesh, in_specs=in_specs, out_specs=out_specs, check_vma=False)
```

```python
import functools
import math

import jax
import jax.numpy as jnp
from jax import lax
from jax.experimental import pallas as pl
from jax.experimental.pallas import tpu as pltpu
from jax.sharding import PartitionSpec as P

H = 12
F32 = jnp.float32
BF16 = jnp.bfloat16
ANY = pl.BlockSpec(memory_space=pl.ANY)
SMEM = pl.BlockSpec(memory_space=pltpu.SMEM)
NEG = -1e30
SHARDS = 16
BIAS_LANE = 72
(
    W_QUERY, W_KEY, W_VALUE, W_OUT, W_UP, W_DOWN, TABLE, B_QUERY, B_VALUE, B_OUT, NORM1_GAIN, NORM1_BIAS, B_UP, B_DOWN, NORM2_GAIN, NORM2_BIAS,
    D_FFN, D_HIDDEN, D_BRANCH, D_Q, D_K, D_V, S_X, S_Q, S_K, S_V, S_ATT, S_N1, S_XH1, S_XH2, S_U, S_GP, S_P, S_RS1, S_RS2, S_TAB,
) = range(36)


def mm(a, b):
    return jnp.dot(a, b, preferred_element_type=F32)


def mm_t(a, b):
    return lax.dot_general(a, b, (((1,), (1,)), ((), ())), preferred_element_type=F32)


def mm_c(a, b):
    return lax.dot_general(a, b, (((0,), (0,)), ((), ())), preferred_element_type=F32)


class Copies:
    def __init__(self, sems):
        self.sems = sems
        self.used = 0

    def make(self, src, dst):
        copy = pltpu.make_async_copy(src, dst, self.sems.at[self.used])
        self.used += 1
        return copy

    def start(self, src, dst):
        copy = self.make(src, dst)
        copy.start()
        return copy

    def choose(self, first, src_a, src_b, dst):
        a = pltpu.make_async_copy(src_a, dst, self.sems.at[self.used])
        b = pltpu.make_async_copy(src_b, dst, self.sems.at[self.used])
        self.used += 1
        pl.when(first)(a.start)
        pl.when(jnp.logical_not(first))(b.start)
        return a


def normalize(rows):
    center = rows - jnp.mean(rows, axis=-1, keepdims=True)
    spread = jnp.mean(center * center, axis=-1, keepdims=True)
    rstd = lax.rsqrt(spread + 1e-05)
    return center * rstd, rstd


GELU_C = math.sqrt(2.0 / math.pi)


def gelu_parts(z):
    zz = z * z
    t = jnp.tanh(z * (GELU_C + (GELU_C * 0.044715) * zz))
    half = 0.5 + 0.5 * t
    slope = half + (0.5 * z) * (1.0 - t * t) * (GELU_C + (3.0 * GELU_C * 0.044715) * zz)
    return z * half, slope


WEIGHTS = (
    W_QUERY, W_KEY, W_VALUE, W_OUT, W_UP, W_DOWN, TABLE,
    B_QUERY, B_VALUE, B_OUT, NORM1_GAIN, NORM1_BIAS, B_UP, B_DOWN, NORM2_GAIN, NORM2_BIAS,
)
STATE = (S_X, S_Q, S_K, S_V, S_ATT, S_N1, S_XH1, S_XH2, S_GP, S_P, S_RS1, S_RS2)


def state_shapes(items, rows, width, hidden, keys):
    low = lambda *s: jax.ShapeDtypeStruct((items,) + s, BF16)
    shapes = {name: low(rows, width) for name in (S_X, S_Q, S_K, S_V, S_ATT, S_N1, S_XH1, S_XH2)}
    shapes[S_GP] = low(rows, hidden)
    shapes[S_P] = low(H, rows, keys)
    shapes[S_RS1] = shapes[S_RS2] = jax.ShapeDtypeStruct((items, rows, 128), F32)
    return [shapes[name] for name in STATE]


def head_masks():
    lane = lax.broadcasted_iota(jnp.int32, (1, 128), 1)
    return [lane < 64, lane >= 64]


def fwd_kernel(cfg, *refs):
    seq, slots, radius, first_call = cfg
    rows = seq + slots
    meta, x_long, x_glob, recv = refs[:4]
    w_hbm = dict(zip(WEIGHTS, refs[4:20]))
    refs = refs[20:]
    if not first_call:
        refs = refs[len(STATE) + 2:]
    st = dict(zip(STATE, refs[:len(STATE)]))
    long_out, glob_out, y_send = refs[len(STATE):len(STATE) + 3]
    refs = refs[len(STATE) + 3:]
    w = dict(zip(WEIGHTS, refs[:16]))
    sc = dict(zip(STATE, refs[16:16 + len(STATE)]))
    y_v, vc, bandm, ownm, sems = refs[16 + len(STATE):]
    item, count, active, from_recv = meta[0], meta[1], meta[2], meta[3]

    @pl.when(active == 1)
    def _():
        cp = Copies(sems)
        fresh = from_recv == 0
        long_rows = pl.ds(pl.multiple_of(item * seq, seq), seq)
        glob_rows = pl.ds(pl.multiple_of(item * slots, slots), slots)
        c_x = cp.choose(fresh, x_long.at[long_rows], recv.at[0:seq], sc[S_X].at[0:seq])
        c_g = cp.choose(fresh, x_glob.at[glob_rows], recv.at[seq:rows], sc[S_X].at[seq:rows])
        loads = {}
        for name in (W_QUERY, B_QUERY, W_KEY, W_VALUE, B_VALUE, TABLE, W_OUT, B_OUT, NORM1_GAIN,
                     NORM1_BIAS, W_UP, B_UP, W_DOWN, B_DOWN, NORM2_GAIN, NORM2_BIAS):
            dst = w[name].at[0:w_hbm[name].shape[0]] if name == TABLE else w[name]
            loads[name] = cp.start(w_hbm[name], dst)
        outs = []

        def save(name):
            outs.append(cp.start(sc[name], st[name].at[item]))

        def vec(name):
            loads[name].wait()
            return w[name][...].astype(F32)

        row = lax.broadcasted_iota(jnp.int32, (seq, seq), 0)
        col = lax.broadcasted_iota(jnp.int32, (seq, seq), 1)
        bandm[...] = jnp.where(jnp.abs(col - row) <= radius, 0.0, NEG)
        key = lax.broadcasted_iota(jnp.int32, (slots, seq), 1)
        slot = lax.broadcasted_iota(jnp.int32, (slots, seq), 0)
        ownm[...] = jnp.where(lax.div(key * count, jnp.int32(seq)) == slot, 0.0, NEG)
        lane = lax.broadcasted_iota(jnp.int32, (1, 128), 1)
        globm = jnp.where((lane >= 64) & (lane < 64 + count), 0.0, NEG)
        vc[seq:, :] = jnp.zeros((128, vc.shape[1]), BF16)
        tab = w[TABLE]
        tab[192:, :] = jnp.zeros((tab.shape[0] - 192, tab.shape[1]), BF16)

        c_x.wait()
        c_g.wait()
        x = sc[S_X][...]
        save(S_X)
        loads[W_QUERY].wait()
        sc[S_Q][...] = (mm(x, w[W_QUERY][...]) + vec(B_QUERY)).astype(BF16)
        save(S_Q)
        loads[W_KEY].wait()
        k = mm(x, w[W_KEY][...]).astype(BF16)
        sc[S_K][...] = k
        save(S_K)
        loads[W_VALUE].wait()
        v = (mm(x, w[W_VALUE][...]) + vec(B_VALUE)).astype(BF16)
        sc[S_V][...] = v
        save(S_V)
        vc[0:seq, :] = v[0:seq]
        vc[seq + 64:seq + 64 + slots, :] = v[seq:rows]
        loads[TABLE].wait()
        tab[192:192 + slots, :] = k[seq:rows]
        halves = head_masks()

        def pair(p, carry):
            cols = pl.ds(pl.multiple_of(p * 128, 128), 128)
            qp = sc[S_Q][:, cols]
            kp = sc[S_K][0:seq, cols]
            rk = tab[:, cols]
            vp = vc[:, cols]
            got = []
            for hh in range(2):
                qm = jnp.where(halves[hh], qp, jnp.zeros_like(qp))
                s1 = mm_t(qm, kp)
                s2 = mm_t(qm, rk)
                band = pltpu.roll(s2[0:seq], (2 * seq - radius - 12) % seq, 1, stride=1, stride_axis=0)
                parts = []
                for sl, sg in (
                    ((s1[0:seq] + band) * 0.125 + bandm[...], s2[0:seq, 128:256] * 0.125 + globm),
                    (s1[seq:rows] * 0.125 + ownm[...], s2[seq:rows, 128:256] * 0.125 + globm),
                ):
                    top = jnp.maximum(jnp.max(sl, axis=-1, keepdims=True), jnp.max(sg, axis=-1, keepdims=True))
                    el = jnp.exp(sl - top)
                    eg = jnp.exp(sg - top)
                    total = jnp.sum(el, axis=-1, keepdims=True) + jnp.sum(eg, axis=-1, keepdims=True)
                    inv = 1.0 / total
                    parts.append(((el * inv).astype(BF16), (eg * inv).astype(BF16)))
                h = p * 2 + hh
                sc[S_P][h, 0:seq, 0:seq] = parts[0][0]
                sc[S_P][h, 0:seq, seq:] = parts[0][1]
                sc[S_P][h, seq:rows, 0:seq] = parts[1][0]
                sc[S_P][h, seq:rows, seq:] = parts[1][1]
                got.append(mm(sc[S_P][h], vp))
            sc[S_ATT][:, cols] = jnp.where(halves[0], got[0], got[1]).astype(BF16)
            return carry

        lax.fori_loop(0, H // 2, pair, 0)
        save(S_P)
        save(S_ATT)
        loads[W_OUT].wait()
        r1 = x.astype(F32) + mm(sc[S_ATT][...], w[W_OUT][...]) + vec(B_OUT)
        xh1, rstd1 = normalize(r1)
        sc[S_XH1][...] = xh1.astype(BF16)
        save(S_XH1)
        sc[S_RS1][...] = jnp.broadcast_to(rstd1, (rows, 128))
        save(S_RS1)
        n1 = xh1 * vec(NORM1_GAIN) + vec(NORM1_BIAS)
        n1_low = n1.astype(BF16)
        sc[S_N1][...] = n1_low
        save(S_N1)
        hidden = w[W_UP].shape[1]
        step = 768
        loads[W_UP].wait()
        b_up = vec(B_UP)
        acc = n1 + vec(B_DOWN)
        for c in range(hidden // step):
            z = mm(n1_low, w[W_UP][:, c * step:(c + 1) * step]) + b_up[:, c * step:(c + 1) * step]
            act, slope = gelu_parts(z)
            act = act.astype(BF16)
            sc[S_GP][:, c * step:(c + 1) * step] = slope.astype(BF16)
            if c == 0:
                loads[W_DOWN].wait()
            acc = acc + mm(act, w[W_DOWN][c * step:(c + 1) * step, :])
        save(S_GP)
        xh2, rstd2 = normalize(acc)
        sc[S_XH2][...] = xh2.astype(BF16)
        save(S_XH2)
        sc[S_RS2][...] = jnp.broadcast_to(rstd2, (rows, 128))
        save(S_RS2)
        y = xh2 * vec(NORM2_GAIN) + vec(NORM2_BIAS)
        pos = lax.broadcasted_iota(jnp.int32, (rows, 1), 0)
        y = jnp.where(pos < seq + count, y, 0.0)
        y_v[...] = y.astype(BF16)
        outs.append(cp.start(y_v, y_send))
        outs.append(cp.start(y_v.at[0:seq], long_out.at[long_rows]))
        outs.append(cp.start(y_v.at[seq:rows], glob_out.at[glob_rows]))
        for copy in outs:
            copy.wait()


def vm(shape, dtype=BF16):
    return pltpu.VMEM(shape, dtype)


def run_forward(meta, x_long, x_glob, recv, weights, state, outs, seq, slots, radius):
    rows, width = seq + slots, x_long.shape[1]
    hidden = weights[4].shape[1]
    items = x_long.shape[0] // seq
    keys = seq + 128
    shapes = state_shapes(items, rows, width, hidden, keys)
    out_shape = shapes + [
        jax.ShapeDtypeStruct(x_long.shape, BF16),
        jax.ShapeDtypeStruct(x_glob.shape, BF16),
        jax.ShapeDtypeStruct((rows, width), BF16),
    ]
    first = state is None
    operands = [meta, x_long, x_glob, recv] + list(weights)
    aliases = {}
    if not first:
        base = len(operands)
        operands += list(state) + list(outs)
        aliases = {base + n: n for n in range(len(state) + 2)}
    scratch = []
    for name, t in zip(WEIGHTS, weights):
        scratch.append(vm((256, width)) if name == TABLE else vm(t.shape))
    scratch += [vm(s.shape[1:], s.dtype) for s in shapes]
    scratch += [vm((rows, width)), vm((keys, width)), vm((seq, seq), F32), vm((slots, seq), F32),
                pltpu.SemaphoreType.DMA((48,))]
    result = pl.pallas_call(
        functools.partial(fwd_kernel, (seq, slots, radius, first)),
        out_shape=out_shape,
        in_specs=[SMEM] + [ANY] * (len(operands) - 1),
        out_specs=[ANY] * len(out_shape),
        scratch_shapes=scratch,
        input_output_aliases=aliases,
        compiler_params=pltpu.CompilerParams(vmem_limit_bytes=60 << 20),
        name="layer_forward",
    )(*operands)
    n = len(STATE)
    return result[:n], result[n:n + 2], result[n + 2]


HIDDEN_USED = (S_XH1, S_XH2, S_GP, S_RS1, S_RS2)
HIDDEN_WEIGHTS = (W_UP, W_DOWN, NORM1_GAIN, NORM2_GAIN)
ATTENTION_USED = (S_Q, S_K, S_V, S_P)
ATTENTION_WEIGHTS = (W_QUERY, W_KEY, W_VALUE, W_OUT, TABLE)


def rows_of(ref, item, size):
    return ref.at[pl.ds(pl.multiple_of(item * size, size), size)]


def hidden_back_kernel(cfg, *refs):
    seq, slots, first_call = cfg
    rows = seq + slots
    meta, c_long, c_glob, recv = refs[:4]
    w_hbm = dict(zip(HIDDEN_WEIGHTS, refs[4:8]))
    st = dict(zip(HIDDEN_USED, refs[8:13]))
    refs = refs[13:]
    if not first_call:
        refs = refs[2:]
    ffn_out, branch_out, ffn_now, first_out, small_out = refs[:5]
    refs = refs[5:]
    w = dict(zip(HIDDEN_WEIGHTS, refs[:4]))
    sc = dict(zip(HIDDEN_USED, refs[4:9]))
    dy, d_ffn_s, d_branch_s, d_first_s, small, small_t, sems = refs[9:]
    item, count, active, from_recv = meta[0], meta[1], meta[2], meta[3]

    @pl.when(active == 1)
    def _():
        cp = Copies(sems)
        fresh = from_recv == 0
        c_y = cp.choose(fresh, rows_of(c_long, item, seq), recv.at[0:seq], dy.at[0:seq])
        c_g = cp.choose(fresh, rows_of(c_glob, item, slots), recv.at[seq:rows], dy.at[seq:rows])
        hidden, width = w[W_DOWN].shape
        step = width
        parts = [slice(c * step, (c + 1) * step) for c in range(hidden // step)]
        loads = {}
        for name in (S_RS2, S_XH2):
            loads[name] = cp.start(st[name].at[item], sc[name])
        loads[NORM2_GAIN] = cp.start(w_hbm[NORM2_GAIN], w[NORM2_GAIN])
        loads[S_GP] = cp.start(st[S_GP].at[item], sc[S_GP])
        for c, sl in enumerate(parts):
            loads[W_DOWN, c] = cp.start(w_hbm[W_DOWN].at[sl], w[W_DOWN].at[sl])
            loads[W_UP, c] = cp.start(w_hbm[W_UP].at[:, sl], w[W_UP].at[:, sl])
        for name in (S_RS1, S_XH1):
            loads[name] = cp.start(st[name].at[item], sc[name])
        loads[NORM1_GAIN] = cp.start(w_hbm[NORM1_GAIN], w[NORM1_GAIN])
        small[...] = jnp.zeros_like(small)
        pos = lax.broadcasted_iota(jnp.int32, (rows, 1), 0)
        lane = lax.broadcasted_iota(jnp.int32, (1, 128), 1)
        ones = jnp.ones((rows, 128), BF16)

        def norm_back(grad, xh, rstd, gain, at):
            small[at:at + 1, :] = jnp.sum(grad * xh, axis=0, keepdims=True)
            small[at + 1:at + 2, :] = jnp.sum(grad, axis=0, keepdims=True)
            dxh = grad * gain
            return rstd * (
                dxh - jnp.mean(dxh, axis=-1, keepdims=True) - xh * jnp.mean(dxh * xh, axis=-1, keepdims=True)
            )

        c_y.wait()
        c_g.wait()
        grad = jnp.where(pos < seq + count, dy[...].astype(F32), 0.0)
        for name in (NORM2_GAIN, S_XH2, S_RS2):
            loads[name].wait()
        d_second = norm_back(
            grad, sc[S_XH2][...].astype(F32), sc[S_RS2][:, 0:1], w[NORM2_GAIN][...].astype(F32), 70
        )
        d_ffn = d_second.astype(BF16)
        d_ffn_s[...] = d_ffn
        outs = [cp.start(d_ffn_s, ffn_out.at[item]), cp.start(d_ffn_s, ffn_now)]
        small[69:70, :] = jnp.sum(d_ffn.astype(F32), axis=0, keepdims=True)
        loads[S_GP].wait()
        d_normed = d_second
        wide, narrow = hidden // SHARDS, width // SHARDS
        for c, sl in enumerate(parts):
            loads[W_DOWN, c].wait()
            d_hid = (sc[S_GP][:, sl].astype(F32) * mm_t(d_ffn, w[W_DOWN][sl, :])).astype(BF16)
            loads[W_UP, c].wait()
            d_normed = d_normed + mm_t(d_hid, w[W_UP][:, sl])
            sums = mm_c(d_hid, ones)
            for shard in range(step // wide):
                block = jnp.zeros((narrow, 128), F32)
                for k in range(wide // narrow):
                    at = shard * wide + k * narrow
                    block = jnp.where(lane == BIAS_LANE + k, sums[at:at + narrow], block)
                at = (c * (step // wide) + shard) * narrow
                small_t[at:at + narrow, :] = block
        for name in (NORM1_GAIN, S_XH1, S_RS1):
            loads[name].wait()
        d_first = norm_back(
            d_normed, sc[S_XH1][...].astype(F32), sc[S_RS1][:, 0:1], w[NORM1_GAIN][...].astype(F32), 67
        )
        d_first_s[...] = d_first
        outs.append(cp.start(d_first_s, first_out))
        d_branch = d_first.astype(BF16)
        d_branch_s[...] = d_branch
        outs.append(cp.start(d_branch_s, branch_out.at[item]))
        small[66:67, :] = jnp.sum(d_branch.astype(F32), axis=0, keepdims=True)
        small_t[...] += small[...].T
        outs.append(cp.start(small_t, small_out))
        for copy in outs:
            copy.wait()


def run_hidden_back(meta, c_long, c_glob, recv, weights, state, made, seq, slots):
    rows, width = seq + slots, c_long.shape[1]
    named, kept = dict(zip(WEIGHTS, weights)), dict(zip(STATE, state))
    items = c_long.shape[0] // seq
    low = jax.ShapeDtypeStruct((items, rows, width), BF16)
    out_shape = [low, low, jax.ShapeDtypeStruct((rows, width), BF16), jax.ShapeDtypeStruct((rows, width), F32),
                 jax.ShapeDtypeStruct((width, 128), F32)]
    operands = [meta, c_long, c_glob, recv] + [named[n] for n in HIDDEN_WEIGHTS] + [kept[n] for n in HIDDEN_USED]
    aliases = {}
    if made is not None:
        aliases = {len(operands): 0, len(operands) + 1: 1}
        operands += list(made)
    scratch = [vm(named[n].shape) for n in HIDDEN_WEIGHTS]
    scratch += [vm(kept[n].shape[1:], kept[n].dtype) for n in HIDDEN_USED]
    scratch += [vm((rows, width)), vm((rows, width)), vm((rows, width)), vm((rows, width), F32),
                vm((128, width), F32), vm((width, 128), F32), pltpu.SemaphoreType.DMA((32,))]
    result = pl.pallas_call(
        functools.partial(hidden_back_kernel, (seq, slots, made is None)),
        out_shape=out_shape,
        in_specs=[SMEM] + [ANY] * (len(operands) - 1),
        out_specs=[ANY] * len(out_shape),
        scratch_shapes=scratch,
        input_output_aliases=aliases,
        compiler_params=pltpu.CompilerParams(vmem_limit_bytes=60 << 20),
        name="hidden_back",
    )(*operands)
    return result[:2], result[2], result[3], result[4]


def attention_back_kernel(cfg, *refs):
    seq, slots, radius, first_call = cfg
    rows = seq + slots
    meta, first_hbm, small_hbm = refs[:3]
    w_hbm = dict(zip(ATTENTION_WEIGHTS, refs[3:8]))
    st = dict(zip(ATTENTION_USED, refs[8:12]))
    refs = refs[12:]
    if not first_call:
        refs = refs[6:]
    fac = dict(zip((D_Q, D_K, D_V), refs[:3]))
    tab_out, long_back, glob_back, d_send = refs[3:7]
    refs = refs[7:]
    w = dict(zip(ATTENTION_WEIGHTS, refs[:5]))
    sc = dict(zip(ATTENTION_USED, refs[5:9]))
    fs = dict(zip((D_Q, D_K, D_V), refs[9:12]))
    da, dx, dx_low, tab_s, small, small_t, flip, vc, sems = refs[12:]
    item, active = meta[0], meta[2]

    @pl.when(active == 1)
    def _():
        cp = Copies(sems)
        loads = {S_X: cp.start(first_hbm, dx)}
        for name in (W_OUT, S_V, S_P, TABLE, S_K, S_Q):
            if name in w:
                dst = w[name].at[0:w_hbm[name].shape[0]] if name == TABLE else w[name]
                loads[name] = cp.start(w_hbm[name], dst)
            else:
                loads[name] = cp.start(st[name].at[item], sc[name])
        loads[S_TAB] = cp.start(small_hbm, small_t)
        for name in (W_QUERY, W_KEY, W_VALUE):
            loads[name] = cp.start(w_hbm[name], w[name])
        outs = []

        def save(name):
            outs.append(cp.start(fs[name], fac[name].at[item]))

        row = lax.broadcasted_iota(jnp.int32, (seq, seq), 0)
        col = lax.broadcasted_iota(jnp.int32, (seq, seq), 1)
        turn = (radius + 12) % seq
        flip[...] = jnp.where((row + col == turn) | (row + col == turn + seq), 1.0, 0.0).astype(BF16)
        vc[seq:, :] = jnp.zeros((128, vc.shape[1]), BF16)
        tab = w[TABLE]
        tab[192:, :] = jnp.zeros((tab.shape[0] - 192, tab.shape[1]), BF16)
        small[...] = jnp.zeros_like(small)
        loads[S_X].wait()
        loads[W_OUT].wait()
        da[...] = mm_t(dx[...].astype(BF16), w[W_OUT][...]).astype(BF16)
        for name in (S_Q, S_K, S_V, TABLE, S_P):
            loads[name].wait()
        vc[0:seq, :] = sc[S_V][0:seq, :]
        vc[seq + 64:seq + 64 + slots, :] = sc[S_V][seq:rows, :]
        tab[192:192 + slots, :] = sc[S_K][seq:rows, :]
        halves = head_masks()
        label = lax.broadcasted_iota(jnp.int32, (1, 256), 1)
        own_label = (label >= 12) & (label < 12 + 2 * radius + 1)

        def pair(p, carry):
            cols = pl.ds(pl.multiple_of(p * 128, 128), 128)
            qp = sc[S_Q][:, cols]
            kp = sc[S_K][0:seq, cols]
            rk = tab[:, cols]
            vp = vc[:, cols]
            dap = da[:, cols]
            q_t = qp.T
            da_t = dap.T
            dq, dk_t, dv_t = [], [], []
            for hh in range(2):
                h = p * 2 + hh
                dam = jnp.where(halves[hh], dap, jnp.zeros_like(dap))
                prob_low = sc[S_P][h]
                prob = prob_low.astype(F32)
                d_prob = mm_t(dam, vp)
                delta = jnp.sum(prob * d_prob, axis=-1, keepdims=True)
                ds = (prob * (d_prob - delta)).astype(BF16)
                ds1 = ds[:, 0:seq]
                turned = mm(flip[...], ds1[0:seq]).astype(BF16)
                turned = pltpu.roll(turned, 0, 1, stride=1, stride_axis=0)
                rel = mm(flip[...], turned).astype(BF16)
                far = jnp.concatenate(
                    [
                        jnp.concatenate([rel[:, 0:128], rel[:, 128:256] + ds[0:seq, seq:]], 1),
                        jnp.concatenate([jnp.zeros((slots, 128), BF16), ds[seq:rows, seq:]], 1),
                    ],
                    0,
                )
                dq.append(mm(ds1, kp) + mm(far, rk))
                own = slice(64 * hh, 64 * hh + 64)
                dk_t.append(jnp.concatenate([mm(q_t[own], ds1), mm(q_t[own], far)], 1) * 0.125)
                dv_t.append(mm(da_t[own], prob_low))
            fs[D_Q][:, cols] = (jnp.where(halves[0], dq[0], dq[1]) * 0.125).astype(BF16)
            dk_t = jnp.concatenate(dk_t, 0)
            dv_t = jnp.concatenate(dv_t, 0)
            fs[D_K][0:seq, cols] = dk_t[:, 0:seq].T.astype(BF16)
            fs[D_K][seq:rows, cols] = dk_t[:, seq + 128:].T[64:64 + slots].astype(BF16)
            fs[D_V][0:seq, cols] = dv_t[:, 0:seq].T.astype(BF16)
            fs[D_V][seq:rows, cols] = dv_t[:, seq:].T[64:64 + slots].astype(BF16)
            tab_s[cols, :] = jnp.where(own_label, dk_t[:, seq:], 0.0)
            return carry

        lax.fori_loop(0, H // 2, pair, 0)
        save(D_Q)
        save(D_K)
        save(D_V)
        small[64:65, :] = jnp.sum(fs[D_Q][...].astype(F32), axis=0, keepdims=True)
        small[65:66, :] = jnp.sum(fs[D_V][...].astype(F32), axis=0, keepdims=True)
        for name in (W_QUERY, W_KEY, W_VALUE, S_TAB):
            loads[name].wait()
        d_rows = (
            dx[...]
            + mm_t(fs[D_Q][...], w[W_QUERY][...])
            + mm_t(fs[D_K][...], w[W_KEY][...])
            + mm_t(fs[D_V][...], w[W_VALUE][...])
        )
        dx_low[...] = d_rows.astype(BF16)
        outs.append(cp.start(dx_low, d_send))
        dx[...] = d_rows
        outs.append(cp.start(dx.at[0:seq], rows_of(long_back, item, seq)))
        outs.append(cp.start(dx.at[seq:rows], rows_of(glob_back, item, slots)))
        tab_s[:, 128:] += small[...].T + small_t[...]
        outs.append(cp.start(tab_s, tab_out.at[item]))
        for copy in outs:
            copy.wait()


def run_attention_back(meta, d_first, small, weights, state, made, seq, slots, radius):
    rows, width = d_first.shape
    named, kept = dict(zip(WEIGHTS, weights)), dict(zip(STATE, state))
    items = kept[S_Q].shape[0]
    low = jax.ShapeDtypeStruct((items, rows, width), BF16)
    out_shape = [low, low, low, jax.ShapeDtypeStruct((items, width, 256), F32),
                 jax.ShapeDtypeStruct((items * seq, width), F32), jax.ShapeDtypeStruct((items * slots, width), F32),
                 jax.ShapeDtypeStruct((rows, width), BF16)]
    operands = [meta, d_first, small] + [named[n] for n in ATTENTION_WEIGHTS] + [kept[n] for n in ATTENTION_USED]
    aliases = {}
    if made is not None:
        aliases = {len(operands) + n: n for n in range(6)}
        operands += list(made)
    scratch = [vm((256, width)) if n == TABLE else vm(named[n].shape) for n in ATTENTION_WEIGHTS]
    scratch += [vm(kept[n].shape[1:], kept[n].dtype) for n in ATTENTION_USED]
    scratch += [vm((rows, width))] * 3
    scratch += [vm((rows, width)), vm((rows, width), F32), vm((rows, width)), vm((width, 256), F32), vm((128, width), F32),
                vm((width, 128), F32), vm((seq, seq)), vm((seq + 128, width)), pltpu.SemaphoreType.DMA((32,))]
    result = pl.pallas_call(
        functools.partial(attention_back_kernel, (seq, slots, radius, made is None)),
        out_shape=out_shape,
        in_specs=[SMEM] + [ANY] * (len(operands) - 1),
        out_specs=[ANY] * len(out_shape),
        scratch_shapes=scratch,
        input_output_aliases=aliases,
        compiler_params=pltpu.CompilerParams(vmem_limit_bytes=60 << 20),
        name="attention_back",
    )(*operands)
    return result[:6], result[6]


TILE = 16
MESH_ID = pl.DeviceIdType.MESH
NZ, NY, NX = 4, 2, 2
LOADED = (S_X, S_ATT, D_BRANCH, D_Q, D_K, D_V)
CHUNKS = ((1, 0), (0, 1)) * 6 + ((1, 0),)
ENTER = (0, 0, 1, 3, 4, 5, 6, 7, 8, 9, 10, 11, 12)
PIECES = 4
SPACING = 2
FFN_ORDER = (0, 3, 1, 2)
STAGES = 6
PER_CHUNK = 7
PER_FFN = 4


def reduce_kernel(cfg, *refs):
    rows, width, hidden = cfg
    wide, narrow = hidden // SHARDS, width // SHARDS
    ins = dict(zip(LOADED, refs[:6]))
    n1_hbm, n1_near, df_hbm, df_a, df_b, df_c, up_hbm, bias_hbm, down_hbm, tab_hbm, red = refs[6:17]
    refs = refs[17:]
    buf = dict(zip(LOADED, refs[:6]))
    n1, df, w_up, b_up, w_down, tab, ga, gf, ay, ax, az, by, bz, bx, fx, fz, u, d_hid = refs[6:24]
    load_sems, send_sems, recv_sems = refs[24:]
    section = lax.axis_index("section")
    me = lax.axis_index("dp")
    x, y, z = lax.rem(me, NX), lax.rem(lax.div(me, NX), NY), lax.div(me, NX * NY)
    half = rows // 2

    def at(zz, yy, xx):
        return (section, (zz * NY + yy) * NX + xx)

    across_x, across_y = at(z, y, 1 - x), at(z, 1 - y, x)
    above, below = at(z + 1, y, x), at(z - 1, y, x)

    cp = Copies(load_sems)
    loads = {}
    for name in (D_BRANCH, S_ATT):
        loads[name] = [cp.start(ins[name], buf[name])]
    loads[S_N1] = [cp.start(n1_hbm, n1.at[0:rows]), cp.start(n1_near, n1.at[rows:])]
    loads[D_FFN] = [cp.start(df_hbm, df.at[0:rows])]
    first_section = section == 0
    loads[D_FFN].append(cp.choose(first_section, df_b, df_a, df.at[rows:rows + half]))
    loads[D_FFN].append(cp.choose(first_section, df_c, df_b, df.at[rows + half:]))
    loads[B_UP] = [cp.start(bias_hbm, b_up)]
    for n in FFN_ORDER:
        units = pl.ds(pl.multiple_of((2 * n + y) * 2 * wide, 2 * wide), 2 * wide)
        loads[W_UP, n] = [cp.start(up_hbm.at[:, units], w_up.at[n]), cp.start(down_hbm.at[units], w_down.at[n])]
    for name in (S_X, D_Q, D_K, D_V):
        loads[name] = [cp.start(ins[name], buf[name])]
    loads[S_TAB] = [cp.start(tab_hbm, tab)]

    barrier = pltpu.get_barrier_semaphore()
    for other in (across_x, across_y):
        pl.semaphore_signal(barrier, inc=1, device_id=other, device_id_type=MESH_ID)

    @pl.when(z > 0)
    def _():
        pl.semaphore_signal(barrier, inc=1, device_id=below, device_id_type=MESH_ID)

    @pl.when(z < NZ - 1)
    def _():
        pl.semaphore_signal(barrier, inc=1, device_id=above, device_id_type=MESH_ID)

    def need(*names):
        for name in names:
            for copy in loads.pop(name, ()):
                copy.wait()

    def units_of(n):
        return pl.ds(pl.multiple_of((2 * n + y) * 2 * wide, 2 * wide), 2 * wide)

    def form_hidden(n):
        need(S_N1, D_FFN, B_UP, (W_UP, n))
        act, slope = gelu_parts(mm(n1[...], w_up[n]) + b_up[:, units_of(n)].astype(F32))
        u[...] = act.astype(BF16)
        d_hid[...] = (slope * mm_t(df[...], w_down[n])).astype(BF16)

    def form_down(n):
        part = mm_c(u[...], df[...]).astype(BF16)
        gf[n, 0, 0:wide, :] = part[0:wide]
        gf[n, 1, 0:wide, :] = part[wide:]

    def form_up(n):
        part = mm_c(d_hid[...], n1[...]).astype(BF16)
        gf[n, 0, wide:, :] = part[0:wide]
        gf[n, 1, wide:, :] = part[wide:]

    def form_narrow(left, right, at_row):
        need(left, right)

        def body(n, carry):
            cols = pl.ds(pl.multiple_of(n * 8 * narrow, 8 * narrow), 8 * narrow)
            part = mm_c(buf[left][:, cols], buf[right][...]).astype(BF16)
            for k in range(8):
                ga[2 * n + k // 4, (k // 2) % 2, k % 2, at_row:at_row + narrow, :] = part[k * narrow:(k + 1) * narrow]
            return carry

        lax.fori_loop(0, SHARDS // 8, body, 0)

    def form_table(at_row):
        need(S_TAB)

        def body(n, carry):
            for k in range(narrow // TILE):
                rows_k = pl.ds(pl.multiple_of(n * narrow + k * TILE, TILE), TILE)
                part = tab[0, rows_k, :] + tab[1, rows_k, :]
                shard = ga.at[lax.div(n, 4), lax.rem(lax.div(n, 2), 2), lax.rem(n, 2), at_row:at_row + TILE]
                shard[:, 256 * k:256 * k + 256] = part.astype(BF16)
            return carry

        lax.fori_loop(0, SHARDS, body, 0)

    first = [0]
    for counts in CHUNKS:
        first.append(first[-1] + sum(counts))

    def spans(chunk, route):
        counts = CHUNKS[chunk]
        start = first[chunk] + sum(counts[:route])
        own = sum(CHUNKS[n][route] for n in range(chunk))
        size = counts[route] * TILE
        return slice(start * TILE, start * TILE + size), slice(own * TILE, own * TILE + size), size

    pending = []

    def remote(src, dst, index, target):
        return pltpu.make_async_remote_copy(
            src_ref=src, dst_ref=dst, send_sem=send_sems.at[index], recv_sem=recv_sems.at[index],
            device_id=target, device_id_type=MESH_ID,
        )

    def send(src, dst, index, target):
        remote(src, dst, index, target).start()
        pending.append((None, lambda: remote(src, dst, index, target).wait_send()))

    def add(dst, src, lead):
        total = 1
        for n in lead:
            total *= n

        def body(n, carry):
            idx, rest = [], n
            for size in reversed(lead):
                idx.insert(0, lax.rem(rest, size))
                rest = lax.div(rest, size)
            d, s = dst(*idx), src(*idx)
            d[...] = (d[...].astype(F32) + s[...].astype(F32)).astype(BF16)
            return carry

        if total == 1:
            body(0, 0)
        else:
            lax.fori_loop(0, total, body, 0)

    def flow_z(stage, own, room, base, lead, shards=tuple(range(NZ))):
        def take(shard, slot, source):
            remote(own(shard), room(slot), base(slot), source).wait_recv()
            add(lambda *i: own(shard).at[i] if i else own(shard), lambda *i: room(slot).at[i] if i else room(slot), lead)

        def put(zz, shard, target):
            slot = NZ if (shard < zz and shard == zz - 1) else shard
            remote(own(shard), room(slot), base(slot), target).start()
            pending.append((zz, lambda: remote(own(shard), room(slot), base(slot), target).wait_send()))

        for zz in range(NZ):
            ups = [s for s in range(NZ - 1, zz - 1, -1) if s in shards]
            downs = [s for s in range(zz + 1) if s in shards]

            @pl.when(z == zz)
            def _():
                if stage == zz:
                    for shard in ups:
                        if zz > 0:
                            take(shard, shard, below)
                        if shard > zz:
                            put(zz, shard, above)
                if stage == NZ - 1 - zz:
                    for shard in downs:
                        if zz < NZ - 1:
                            take(shard, NZ if shard == zz else shard, above)
                        if shard < zz:
                            put(zz, shard, below)

    ffn_sems = len(CHUNKS) * PER_CHUNK

    def run(chunk, route, stage):
        rs, own, size = spans(chunk, route)
        if size == 0:
            return
        base = chunk * PER_CHUNK
        flow_base = lambda slot: base + 2 + slot
        out = slice(2 * wide + rs.start, 2 * wide + rs.stop)
        if stage == 0:
            room = ay if route == 0 else by
            send(ga.at[:, 1 - y, :, rs], room.at[:, :, own], base, across_y)
        if stage == 1:
            room = ay if route == 0 else by
            remote(ga.at[:, 1 - y, :, rs], room.at[:, :, own], base, across_y).wait_recv()
            add(lambda i, j: ga.at[i, y, j, rs], lambda i, j: room.at[i, j, own], (NZ, NX))
        if route == 0:
            if stage == 1:
                send(ga.at[:, y, 1 - x, rs], ax.at[:, own], base + 1, across_x)
            if stage == 2:
                remote(ga.at[:, y, 1 - x, rs], ax.at[:, own], base + 1, across_x).wait_recv()
                add(lambda i: ga.at[i, y, x, rs], lambda i: ax.at[i, own], (NZ,))
            if stage >= 2:
                flow_z(stage - 2, lambda s: ga.at[s, y, x, rs], lambda s: az.at[s, own], flow_base, ())
        else:
            if 1 <= stage <= 4:
                flow_z(stage - 1, lambda s: ga.at[s, y, :, rs], lambda s: bz.at[s, :, own], flow_base, (NX,))
            if stage == 4:
                send(ga.at[z, y, 1 - x, rs], bx.at[own], base + 1, across_x)
            if stage == 5:
                remote(ga.at[z, y, 1 - x, rs], bx.at[own], base + 1, across_x).wait_recv()
                add(lambda: ga.at[z, y, x, rs], lambda: bx.at[own], ())
        if stage == 5:
            red[out, :] = ga[z, y, x, rs, :].astype(F32)

    def run_ffn(n, piece, stage):
        base = ffn_sems + (n * PIECES + piece) * PER_FFN
        size = 2 * wide // PIECES
        rs = slice(piece * size, (piece + 1) * size)
        if stage == 0:
            send(gf.at[n, 1 - x, rs], fx.at[n, rs], base, across_x)
        if stage == 1:
            remote(gf.at[n, 1 - x, rs], fx.at[n, rs], base, across_x).wait_recv()
            add(lambda: gf.at[n, x, rs], lambda: fx.at[n, rs], ())
        if 1 <= stage <= 4:
            room = lambda slot: fz.at[1 if slot == NZ else 0, n, rs]
            flow_z(stage - 1, lambda s: gf.at[s, x, rs], room, lambda slot: base + (2 if slot == NZ else 1), (), (n,))
        if stage == 5:
            @pl.when(z == n)
            def _():
                red[rs, :] = gf[n, x, rs, :].astype(F32)

    def narrow_task(n):
        left, right = ((D_BRANCH, S_ATT), (D_Q, S_X), (D_K, S_X), (D_V, S_X))[n]
        return lambda: form_narrow(left, right, n * narrow)

    a, b, c, d = FFN_ORDER
    hidden_task = lambda n: lambda: form_hidden(n)
    down_task = lambda n: lambda: form_down(n)
    up_task = lambda n: lambda: form_up(n)
    tasks = [(up_task(a),), (narrow_task(1),), (hidden_task(b),), (down_task(b),), (narrow_task(2),), (up_task(b),),
             (hidden_task(c),), (down_task(c),), (narrow_task(3),), (up_task(c),),
             (hidden_task(d), lambda: form_table(4 * narrow)), (down_task(d),), (up_task(d),)]
    narrow_task(0)()

    @pl.when((z == 0) | (z == NZ - 1))
    def _():
        pl.semaphore_wait(barrier, 3)

    @pl.when((z > 0) & (z < NZ - 1))
    def _():
        pl.semaphore_wait(barrier, 4)

    starts = [(n, None, slot) for n, slot in enumerate(ENTER)]
    starts += [(FFN_ORDER[k // PIECES], k % PIECES, k) for k in range(NZ * PIECES)]
    last = max(slot for _, _, slot in starts) + SPACING * (STAGES - 1)
    for slot in range(last + 1):
        for stage in range(STAGES):
            for n, piece, enter in starts:
                if enter + stage * SPACING == slot:
                    if slot == 0 and piece == 0:
                        form_hidden(a)
                        form_down(a)
                    if piece is None:
                        run(n, 0, stage)
                        run(n, 1, stage)
                    else:
                        run_ffn(n, piece, stage)
            if stage == 0:
                for task in tasks.pop(0) if tasks else ():
                    task()
    for zz, wait in pending:
        if zz is None:
            wait()
        else:
            pl.when(z == zz)(wait)


def reduce_grads(parts, near, weights, tab):
    rows, width = parts[S_X].shape
    hidden = weights[W_UP].shape[1]
    wide, narrow = hidden // SHARDS, width // SHARDS
    share = 4 * narrow + TILE
    t = [sum(c[n] for c in CHUNKS) * TILE for n in range(2)]
    assert sum(t) == share
    n_sem = len(CHUNKS) * PER_CHUNK + NZ * PIECES * PER_FFN
    scratch = [vm(parts[n].shape) for n in LOADED]
    scratch += [
        vm((2 * rows, width)), vm((2 * rows, width)), vm((NZ, width, 2 * wide)), vm((1, hidden)), vm((NZ, 2 * wide, width)),
        vm(tab.shape, F32),
        vm((NZ, NY, NX, share, width)), vm((NZ, NX, 2 * wide, width)),
        vm((NZ, NX, t[0], width)), vm((NZ, t[0], width)), vm((NZ + 1, t[0], width)),
        vm((NZ, NX, t[1], width)), vm((NZ + 1, NX, t[1], width)), vm((t[1], width)),
        vm((NZ, 2 * wide, width)), vm((2, NZ, 2 * wide, width)), vm((2 * rows, 2 * wide)), vm((2 * rows, 2 * wide)),
        pltpu.SemaphoreType.DMA((32,)), pltpu.SemaphoreType.DMA((n_sem,)), pltpu.SemaphoreType.DMA((n_sem,)),
    ]
    operands = [parts[n] for n in LOADED]
    operands += [parts[S_N1], near[0], parts[D_FFN]] + list(near[1:])
    operands += [weights[W_UP], weights[B_UP], weights[W_DOWN], tab]
    return pl.pallas_call(
        functools.partial(reduce_kernel, (rows, width, hidden)),
        out_shape=jax.ShapeDtypeStruct((2 * wide + share, width), F32),
        in_specs=[ANY] * len(operands),
        out_specs=pl.BlockSpec(memory_space=pltpu.VMEM),
        scratch_shapes=scratch,
        compiler_params=pltpu.CompilerParams(collective_id=0, has_side_effects=True, vmem_limit_bytes=62 << 20),
        name="reduce_grads",
    )(*operands)


def share_of(red, width, hidden):
    wide, narrow = hidden // SHARDS, width // SHARDS
    low = 2 * wide
    cut = [red[low + n * narrow:low + (n + 1) * narrow].T for n in range(4)]
    packed = red[low + 4 * narrow:]
    table = jnp.concatenate([packed[:, 256 * k:256 * k + 256] for k in range(narrow // TILE)], 0)
    return cut, red[wide:low].T, red[0:wide], table


def sums_elsewhere(parts, weights, tab):
    def scatter(value, dim):
        return lax.psum_scatter(value, "dp", scatter_dimension=dim, tiled=True)

    cut = [scatter(mm_c(parts[a], parts[b]), 1)
           for a, b in ((S_ATT, D_BRANCH), (S_X, D_Q), (S_X, D_K), (S_X, D_V))]
    act, slope = gelu_parts(mm(parts[S_N1], weights[W_UP]) + weights[B_UP].astype(F32))
    d_hid = (slope * mm_t(parts[D_FFN], weights[W_DOWN])).astype(BF16)
    w_up = scatter(mm_c(parts[S_N1], d_hid), 1)
    w_down = scatter(mm_c(act.astype(BF16), parts[D_FFN]), 0)
    b_up = scatter(jnp.sum(d_hid.astype(F32), axis=0), 0)
    return cut, w_up, w_down, scatter(tab[0] + tab[1], 0), b_up


def per_device(
    long_input, global_input, counts, w_query, b_query, w_key, w_value, b_value, w_out, b_out, rel_table,
    norm1_gain, norm1_bias, w_up, b_up, w_down, b_down, norm2_gain, norm2_bias, long_cot, global_cot,
):
    items = counts.shape[0]
    seq, slots, width = long_input.shape[0] // items, global_input.shape[0] // items, long_input.shape[1]
    rows, hidden = seq + slots, w_up.shape[2]
    labels = rel_table.shape[1]
    radius = (labels - 1) // 2
    section = lax.axis_index("section")
    weights = [w_query[0], w_key[0], w_value[0], w_out[0], w_up[0], w_down[0],
               jnp.pad(rel_table[0], ((12, 192 - 12 - labels), (0, 0))),
               b_query, b_value, b_out, norm1_gain, norm1_bias, b_up, b_down, norm2_gain, norm2_bias]

    def meta_of(item):
        active = (item >= 0) & (item < items)
        item = jnp.clip(item, 0, items - 1)
        return [item, lax.dynamic_index_in_dim(counts, item, keepdims=False), active.astype(jnp.int32)]

    recv = jnp.zeros((rows, width), BF16)
    state = outs = None
    for step in range(items + 1):
        meta = jnp.stack(meta_of(step - section) + [section])
        state, outs, sent = run_forward(
            meta, long_input, global_input, recv, weights, state, outs, seq, slots, radius)
        if step < items:
            recv = lax.ppermute(sent, "section", [(0, 1)])
    kept = dict(zip(STATE, state))
    shards = lax.axis_size("dp")
    paired = shards == SHARDS
    if paired:
        near = [lax.ppermute(kept[S_N1], "dp", [(n, n ^ NX) for n in range(shards)]).reshape(items * rows, width)]
    low = made = None
    for step in range(items + 1):
        meta = jnp.stack(meta_of(step - (1 - section)) + [1 - section])
        low, d_ffn, d_first, small = run_hidden_back(
            meta, long_cot, global_cot, recv, weights, state, low, seq, slots)
        if paired:
            pairs = [(e * shards + n, e * shards + (n ^ NX)) for e in range(2) for n in range(shards)
                     if 0 <= step - (1 - e) < items]
            near.append(lax.ppermute(d_ffn, ("section", "dp"), pairs))
        made, sent = run_attention_back(
            meta, d_first, small, weights, state, made, seq, slots, radius)
        if step < items:
            recv = lax.ppermute(sent, "section", [(1, 0)])
    parts = {n: kept[n] for n in (S_X, S_ATT, S_N1)}
    parts.update(zip((D_FFN, D_BRANCH, D_Q, D_K, D_V), list(low) + list(made[:3])))
    parts = {n: t.reshape(items * rows, t.shape[2]) for n, t in parts.items()}
    tab, long_back, glob_back = made[3:6]
    named = dict(zip(WEIGHTS, weights))
    if paired:
        cut, g_up, g_down, table = share_of(reduce_grads(parts, near, named, tab), width, hidden)
        g_b_up = jnp.concatenate([table[:, 128 + BIAS_LANE + k] for k in range(hidden // width)], 0)
    else:
        cut, g_up, g_down, table, g_b_up = sums_elsewhere(parts, named, tab)
    g_out, g_query, g_key, g_value = cut
    small = [table[:, 192 + n] for n in range(8)]
    g_bq, g_bv, g_bo, g_g1, g_s1, g_bd, g_g2, g_s2 = small
    grads = (g_query, g_bq, g_key, g_value, g_bv, g_out, g_bo, table[:, 12:12 + labels].T, g_g1, g_s1,
             g_up, g_b_up, g_down, g_bd, g_g2, g_s2)
    return tuple(t[None] for t in (outs[0], outs[1], long_back, glob_back) + grads)


def solution(mesh):
    part = P("section", "dp", None)
    vector = P("section", "dp")
    columns = P("section", None, "dp")
    matrix = P("section", None, None)
    row = P("section", None)
    items = P("dp", None)
    in_specs = (items, items, P("dp"), matrix, row, matrix, matrix, row, matrix, row, matrix, row, row,
                matrix, row, matrix, row, row, row, items, items)
    out_specs = (part, part, part, part, columns, vector, columns, columns, vector, columns, vector, columns,
                 vector, vector, columns, vector, part, vector, vector, vector)
    return jax.shard_map(per_device, mesh=mesh, in_specs=in_specs, out_specs=out_specs, check_vma=False)
```

```python
import functools
import math

import jax
import jax.numpy as jnp
from jax import lax
from jax.experimental import pallas as pl
from jax.experimental.pallas import tpu as pltpu
from jax.sharding import PartitionSpec as P

H = 12
F32 = jnp.float32
BF16 = jnp.bfloat16
ANY = pl.BlockSpec(memory_space=pl.ANY)
SMEM = pl.BlockSpec(memory_space=pltpu.SMEM)
NEG = -1e30
SHARDS = 16
BIAS_LANE = 72
(
    W_QUERY, W_KEY, W_VALUE, W_OUT, W_UP, W_DOWN, TABLE, B_QUERY, B_VALUE, B_OUT, NORM1_GAIN, NORM1_BIAS, B_UP, B_DOWN, NORM2_GAIN, NORM2_BIAS,
    D_FFN, D_HIDDEN, D_BRANCH, D_Q, D_K, D_V, S_X, S_Q, S_K, S_V, S_ATT, S_N1, S_XH1, S_XH2, S_U, S_GP, S_P, S_RS1, S_RS2, S_TAB,
) = range(36)


def mm(a, b):
    return jnp.dot(a, b, preferred_element_type=F32)


def mm_t(a, b):
    return lax.dot_general(a, b, (((1,), (1,)), ((), ())), preferred_element_type=F32)


def mm_c(a, b):
    return lax.dot_general(a, b, (((0,), (0,)), ((), ())), preferred_element_type=F32)


class Copies:
    def __init__(self, sems):
        self.sems = sems
        self.used = 0

    def make(self, src, dst):
        copy = pltpu.make_async_copy(src, dst, self.sems.at[self.used])
        self.used += 1
        return copy

    def start(self, src, dst):
        copy = self.make(src, dst)
        copy.start()
        return copy

    def choose(self, first, src_a, src_b, dst):
        a = pltpu.make_async_copy(src_a, dst, self.sems.at[self.used])
        b = pltpu.make_async_copy(src_b, dst, self.sems.at[self.used])
        self.used += 1
        pl.when(first)(a.start)
        pl.when(jnp.logical_not(first))(b.start)
        return a


def normalize(rows):
    center = rows - jnp.mean(rows, axis=-1, keepdims=True)
    spread = jnp.mean(center * center, axis=-1, keepdims=True)
    rstd = lax.rsqrt(spread + 1e-05)
    return center * rstd, rstd


GELU_C = math.sqrt(2.0 / math.pi)


def gelu_parts(z):
    zz = z * z
    t = jnp.tanh(z * (GELU_C + (GELU_C * 0.044715) * zz))
    half = 0.5 + 0.5 * t
    slope = half + (0.5 * z) * (1.0 - t * t) * (GELU_C + (3.0 * GELU_C * 0.044715) * zz)
    return z * half, slope


WEIGHTS = (
    W_QUERY, W_KEY, W_VALUE, W_OUT, W_UP, W_DOWN, TABLE,
    B_QUERY, B_VALUE, B_OUT, NORM1_GAIN, NORM1_BIAS, B_UP, B_DOWN, NORM2_GAIN, NORM2_BIAS,
)
STATE = (S_X, S_Q, S_K, S_V, S_ATT, S_N1, S_XH1, S_XH2, S_GP, S_P, S_RS1, S_RS2)


def state_shapes(items, rows, width, hidden, keys):
    low = lambda *s: jax.ShapeDtypeStruct((items,) + s, BF16)
    shapes = {name: low(rows, width) for name in (S_X, S_Q, S_K, S_V, S_ATT, S_N1, S_XH1, S_XH2)}
    shapes[S_GP] = low(rows, hidden)
    shapes[S_P] = low(H, rows, keys)
    shapes[S_RS1] = shapes[S_RS2] = jax.ShapeDtypeStruct((items, rows, 128), F32)
    return [shapes[name] for name in STATE]


def head_masks():
    lane = lax.broadcasted_iota(jnp.int32, (1, 128), 1)
    return [lane < 64, lane >= 64]


def turn_of(counts, step_at, forward):
    section = lax.axis_index("section")
    first = (section == 0) if forward else (section == 1)
    turn = jnp.where(first, step_at, step_at - 1)
    item = jnp.clip(turn, 0, counts.shape[0] - 1)
    return item, counts[item], turn == item, first


def fwd_kernel(cfg, *refs):
    seq, slots, radius, first_call, step_at = cfg
    rows = seq + slots
    counts, x_long, x_glob, recv = refs[:4]
    w_hbm = dict(zip(WEIGHTS, refs[4:20]))
    refs = refs[20:]
    if not first_call:
        refs = refs[len(STATE) + 2:]
    st = dict(zip(STATE, refs[:len(STATE)]))
    long_out, glob_out, y_send = refs[len(STATE):len(STATE) + 3]
    refs = refs[len(STATE) + 3:]
    w = dict(zip(WEIGHTS, refs[:16]))
    sc = dict(zip(STATE, refs[16:16 + len(STATE)]))
    y_v, vc, bandm, ownm, sems = refs[16 + len(STATE):]
    item, count, active, fresh = turn_of(counts, step_at, True)

    @pl.when(active)
    def _():
        cp = Copies(sems)
        long_rows = pl.ds(pl.multiple_of(item * seq, seq), seq)
        glob_rows = pl.ds(pl.multiple_of(item * slots, slots), slots)
        c_x = cp.choose(fresh, x_long.at[long_rows], recv.at[0:seq], sc[S_X].at[0:seq])
        c_g = cp.choose(fresh, x_glob.at[glob_rows], recv.at[seq:rows], sc[S_X].at[seq:rows])
        loads = {}
        for name in (W_QUERY, B_QUERY, W_KEY, W_VALUE, B_VALUE, TABLE, W_OUT, B_OUT, NORM1_GAIN,
                     NORM1_BIAS, W_UP, B_UP, W_DOWN, B_DOWN, NORM2_GAIN, NORM2_BIAS):
            dst = w[name].at[0:w_hbm[name].shape[0]] if name == TABLE else w[name]
            loads[name] = cp.start(w_hbm[name], dst)
        outs = []

        def save(name):
            outs.append(cp.start(sc[name], st[name].at[item]))

        def vec(name):
            loads[name].wait()
            return w[name][...].astype(F32)

        row = lax.broadcasted_iota(jnp.int32, (seq, seq), 0)
        col = lax.broadcasted_iota(jnp.int32, (seq, seq), 1)
        bandm[...] = jnp.where(jnp.abs(col - row) <= radius, 0.0, NEG)
        key = lax.broadcasted_iota(jnp.int32, (slots, seq), 1)
        slot = lax.broadcasted_iota(jnp.int32, (slots, seq), 0)
        ownm[...] = jnp.where(lax.div(key * count, jnp.int32(seq)) == slot, 0.0, NEG)
        lane = lax.broadcasted_iota(jnp.int32, (1, 128), 1)
        globm = jnp.where((lane >= 64) & (lane < 64 + count), 0.0, NEG)
        vc[seq:, :] = jnp.zeros((128, vc.shape[1]), BF16)
        tab = w[TABLE]
        tab[192:, :] = jnp.zeros((tab.shape[0] - 192, tab.shape[1]), BF16)

        c_x.wait()
        c_g.wait()
        x = sc[S_X][...]
        save(S_X)
        loads[W_QUERY].wait()
        sc[S_Q][...] = (mm(x, w[W_QUERY][...]) + vec(B_QUERY)).astype(BF16)
        save(S_Q)
        loads[W_KEY].wait()
        k = mm(x, w[W_KEY][...]).astype(BF16)
        sc[S_K][...] = k
        save(S_K)
        loads[W_VALUE].wait()
        v = (mm(x, w[W_VALUE][...]) + vec(B_VALUE)).astype(BF16)
        sc[S_V][...] = v
        save(S_V)
        vc[0:seq, :] = v[0:seq]
        vc[seq + 64:seq + 64 + slots, :] = v[seq:rows]
        loads[TABLE].wait()
        tab[192:192 + slots, :] = k[seq:rows]
        halves = head_masks()

        def pair(p, carry):
            cols = pl.ds(pl.multiple_of(p * 128, 128), 128)
            qp = sc[S_Q][:, cols]
            kp = sc[S_K][0:seq, cols]
            rk = tab[:, cols]
            vp = vc[:, cols]
            got = []
            for hh in range(2):
                qm = jnp.where(halves[hh], qp, jnp.zeros_like(qp))
                s1 = mm_t(qm, kp)
                s2 = mm_t(qm, rk)
                band = pltpu.roll(s2[0:seq], (2 * seq - radius - 12) % seq, 1, stride=1, stride_axis=0)
                parts = []
                for sl, sg in (
                    ((s1[0:seq] + band) * 0.125 + bandm[...], s2[0:seq, 128:256] * 0.125 + globm),
                    (s1[seq:rows] * 0.125 + ownm[...], s2[seq:rows, 128:256] * 0.125 + globm),
                ):
                    top = jnp.maximum(jnp.max(sl, axis=-1, keepdims=True), jnp.max(sg, axis=-1, keepdims=True))
                    el = jnp.exp(sl - top)
                    eg = jnp.exp(sg - top)
                    total = jnp.sum(el, axis=-1, keepdims=True) + jnp.sum(eg, axis=-1, keepdims=True)
                    inv = 1.0 / total
                    parts.append(((el * inv).astype(BF16), (eg * inv).astype(BF16)))
                h = p * 2 + hh
                sc[S_P][h, 0:seq, 0:seq] = parts[0][0]
                sc[S_P][h, 0:seq, seq:] = parts[0][1]
                sc[S_P][h, seq:rows, 0:seq] = parts[1][0]
                sc[S_P][h, seq:rows, seq:] = parts[1][1]
                got.append(mm(sc[S_P][h], vp))
            sc[S_ATT][:, cols] = jnp.where(halves[0], got[0], got[1]).astype(BF16)
            return carry

        lax.fori_loop(0, H // 2, pair, 0)
        save(S_P)
        save(S_ATT)
        loads[W_OUT].wait()
        r1 = x.astype(F32) + mm(sc[S_ATT][...], w[W_OUT][...]) + vec(B_OUT)
        xh1, rstd1 = normalize(r1)
        sc[S_XH1][...] = xh1.astype(BF16)
        save(S_XH1)
        sc[S_RS1][...] = jnp.broadcast_to(rstd1, (rows, 128))
        save(S_RS1)
        n1 = xh1 * vec(NORM1_GAIN) + vec(NORM1_BIAS)
        n1_low = n1.astype(BF16)
        sc[S_N1][...] = n1_low
        save(S_N1)
        hidden = w[W_UP].shape[1]
        step = 768
        loads[W_UP].wait()
        b_up = vec(B_UP)
        acc = n1 + vec(B_DOWN)
        for c in range(hidden // step):
            z = mm(n1_low, w[W_UP][:, c * step:(c + 1) * step]) + b_up[:, c * step:(c + 1) * step]
            act, slope = gelu_parts(z)
            act = act.astype(BF16)
            sc[S_GP][:, c * step:(c + 1) * step] = slope.astype(BF16)
            if c == 0:
                loads[W_DOWN].wait()
            acc = acc + mm(act, w[W_DOWN][c * step:(c + 1) * step, :])
        save(S_GP)
        xh2, rstd2 = normalize(acc)
        sc[S_XH2][...] = xh2.astype(BF16)
        save(S_XH2)
        sc[S_RS2][...] = jnp.broadcast_to(rstd2, (rows, 128))
        save(S_RS2)
        y = xh2 * vec(NORM2_GAIN) + vec(NORM2_BIAS)
        pos = lax.broadcasted_iota(jnp.int32, (rows, 1), 0)
        y = jnp.where(pos < seq + count, y, 0.0)
        y_v[...] = y.astype(BF16)
        outs.append(cp.start(y_v, y_send))
        outs.append(cp.start(y_v.at[0:seq], long_out.at[long_rows]))
        outs.append(cp.start(y_v.at[seq:rows], glob_out.at[glob_rows]))
        for copy in outs:
            copy.wait()


def vm(shape, dtype=BF16):
    return pltpu.VMEM(shape, dtype)


def run_forward(step_at, counts, x_long, x_glob, recv, weights, state, outs, seq, slots, radius):
    rows, width = seq + slots, x_long.shape[1]
    hidden = weights[4].shape[1]
    items = x_long.shape[0] // seq
    keys = seq + 128
    shapes = state_shapes(items, rows, width, hidden, keys)
    out_shape = shapes + [
        jax.ShapeDtypeStruct(x_long.shape, BF16),
        jax.ShapeDtypeStruct(x_glob.shape, BF16),
        jax.ShapeDtypeStruct((rows, width), BF16),
    ]
    first = state is None
    operands = [counts, x_long, x_glob, recv] + list(weights)
    aliases = {}
    if not first:
        base = len(operands)
        operands += list(state) + list(outs)
        aliases = {base + n: n for n in range(len(state) + 2)}
    scratch = []
    for name, t in zip(WEIGHTS, weights):
        scratch.append(vm((256, width)) if name == TABLE else vm(t.shape))
    scratch += [vm(s.shape[1:], s.dtype) for s in shapes]
    scratch += [vm((rows, width)), vm((keys, width)), vm((seq, seq), F32), vm((slots, seq), F32),
                pltpu.SemaphoreType.DMA((48,))]
    result = pl.pallas_call(
        functools.partial(fwd_kernel, (seq, slots, radius, first, step_at)),
        out_shape=out_shape,
        in_specs=[SMEM] + [ANY] * (len(operands) - 1),
        out_specs=[ANY] * len(out_shape),
        scratch_shapes=scratch,
        input_output_aliases=aliases,
        compiler_params=pltpu.CompilerParams(vmem_limit_bytes=60 << 20),
        cost_estimate=pl.CostEstimate(flops=20 * 10**9, bytes_accessed=20 * 10**6, transcendentals=0),
        name="layer_forward",
    )(*operands)
    n = len(STATE)
    return result[:n], result[n:n + 2], result[n + 2]


HIDDEN_USED = (S_XH1, S_XH2, S_GP, S_RS1, S_RS2)
HIDDEN_WEIGHTS = (W_UP, W_DOWN, NORM1_GAIN, NORM2_GAIN)
ATTENTION_USED = (S_Q, S_K, S_V, S_P)
ATTENTION_WEIGHTS = (W_QUERY, W_KEY, W_VALUE, W_OUT, TABLE)


def rows_of(ref, item, size):
    return ref.at[pl.ds(pl.multiple_of(item * size, size), size)]


def hidden_back_kernel(cfg, *refs):
    seq, slots, first_call, step_at, unread = cfg
    rows = seq + slots
    counts, c_long, c_glob, recv = refs[:4]
    w_hbm = dict(zip(HIDDEN_WEIGHTS, refs[4:8]))
    st = dict(zip(HIDDEN_USED, refs[8:13]))
    refs = refs[13:]
    if not first_call:
        refs = refs[2:]
    refs = refs[unread:]
    ffn_out, branch_out, ffn_now, first_out, small_out = refs[:5]
    refs = refs[5:]
    w = dict(zip(HIDDEN_WEIGHTS, refs[:4]))
    sc = dict(zip(HIDDEN_USED, refs[4:9]))
    dy, d_ffn_s, d_branch_s, d_first_s, small, small_t, sems = refs[9:]
    item, count, active, fresh = turn_of(counts, step_at, False)

    @pl.when(active)
    def _():
        cp = Copies(sems)
        c_y = cp.choose(fresh, rows_of(c_long, item, seq), recv.at[0:seq], dy.at[0:seq])
        c_g = cp.choose(fresh, rows_of(c_glob, item, slots), recv.at[seq:rows], dy.at[seq:rows])
        hidden, width = w[W_DOWN].shape
        step = width
        parts = [slice(c * step, (c + 1) * step) for c in range(hidden // step)]
        loads = {}
        for name in (S_RS2, S_XH2):
            loads[name] = cp.start(st[name].at[item], sc[name])
        loads[NORM2_GAIN] = cp.start(w_hbm[NORM2_GAIN], w[NORM2_GAIN])
        loads[S_GP] = cp.start(st[S_GP].at[item], sc[S_GP])
        for c, sl in enumerate(parts):
            loads[W_DOWN, c] = cp.start(w_hbm[W_DOWN].at[sl], w[W_DOWN].at[sl])
            loads[W_UP, c] = cp.start(w_hbm[W_UP].at[:, sl], w[W_UP].at[:, sl])
        for name in (S_RS1, S_XH1):
            loads[name] = cp.start(st[name].at[item], sc[name])
        loads[NORM1_GAIN] = cp.start(w_hbm[NORM1_GAIN], w[NORM1_GAIN])
        small[...] = jnp.zeros_like(small)
        pos = lax.broadcasted_iota(jnp.int32, (rows, 1), 0)
        lane = lax.broadcasted_iota(jnp.int32, (1, 128), 1)
        ones = jnp.ones((rows, 128), BF16)

        def norm_back(grad, xh, rstd, gain, at):
            small[at:at + 1, :] = jnp.sum(grad * xh, axis=0, keepdims=True)
            small[at + 1:at + 2, :] = jnp.sum(grad, axis=0, keepdims=True)
            dxh = grad * gain
            return rstd * (
                dxh - jnp.mean(dxh, axis=-1, keepdims=True) - xh * jnp.mean(dxh * xh, axis=-1, keepdims=True)
            )

        c_y.wait()
        c_g.wait()
        grad = jnp.where(pos < seq + count, dy[...].astype(F32), 0.0)
        for name in (NORM2_GAIN, S_XH2, S_RS2):
            loads[name].wait()
        d_second = norm_back(
            grad, sc[S_XH2][...].astype(F32), sc[S_RS2][:, 0:1], w[NORM2_GAIN][...].astype(F32), 70
        )
        d_ffn = d_second.astype(BF16)
        d_ffn_s[...] = d_ffn
        outs = [cp.start(d_ffn_s, ffn_out.at[item]), cp.start(d_ffn_s, ffn_now)]
        small[69:70, :] = jnp.sum(d_ffn.astype(F32), axis=0, keepdims=True)
        loads[S_GP].wait()
        d_normed = d_second
        wide, narrow = hidden // SHARDS, width // SHARDS
        for c, sl in enumerate(parts):
            loads[W_DOWN, c].wait()
            d_hid = (sc[S_GP][:, sl].astype(F32) * mm_t(d_ffn, w[W_DOWN][sl, :])).astype(BF16)
            loads[W_UP, c].wait()
            d_normed = d_normed + mm_t(d_hid, w[W_UP][:, sl])
            sums = mm_c(d_hid, ones)
            for shard in range(step // wide):
                block = jnp.zeros((narrow, 128), F32)
                for k in range(wide // narrow):
                    at = shard * wide + k * narrow
                    block = jnp.where(lane == BIAS_LANE + k, sums[at:at + narrow], block)
                at = (c * (step // wide) + shard) * narrow
                small_t[at:at + narrow, :] = block
        for name in (NORM1_GAIN, S_XH1, S_RS1):
            loads[name].wait()
        d_first = norm_back(
            d_normed, sc[S_XH1][...].astype(F32), sc[S_RS1][:, 0:1], w[NORM1_GAIN][...].astype(F32), 67
        )
        d_first_s[...] = d_first
        outs.append(cp.start(d_first_s, first_out))
        d_branch = d_first.astype(BF16)
        d_branch_s[...] = d_branch
        outs.append(cp.start(d_branch_s, branch_out.at[item]))
        small[66:67, :] = jnp.sum(d_branch.astype(F32), axis=0, keepdims=True)
        small_t[...] += small[...].T
        outs.append(cp.start(small_t, small_out))
        for copy in outs:
            copy.wait()


def run_hidden_back(step_at, counts, c_long, c_glob, recv, weights, state, made, arrived, seq, slots):
    rows, width = seq + slots, c_long.shape[1]
    named, kept = dict(zip(WEIGHTS, weights)), dict(zip(STATE, state))
    items = c_long.shape[0] // seq
    low = jax.ShapeDtypeStruct((items, rows, width), BF16)
    out_shape = [low, low, jax.ShapeDtypeStruct((rows, width), BF16), jax.ShapeDtypeStruct((rows, width), F32),
                 jax.ShapeDtypeStruct((width, 128), F32)]
    operands = [counts, c_long, c_glob, recv] + [named[n] for n in HIDDEN_WEIGHTS] + [kept[n] for n in HIDDEN_USED]
    aliases = {}
    if made is not None:
        aliases = {len(operands): 0, len(operands) + 1: 1}
        operands += list(made)
    operands += list(arrived)
    scratch = [vm(named[n].shape) for n in HIDDEN_WEIGHTS]
    scratch += [vm(kept[n].shape[1:], kept[n].dtype) for n in HIDDEN_USED]
    scratch += [vm((rows, width)), vm((rows, width)), vm((rows, width)), vm((rows, width), F32),
                vm((128, width), F32), vm((width, 128), F32), pltpu.SemaphoreType.DMA((32,))]
    result = pl.pallas_call(
        functools.partial(hidden_back_kernel, (seq, slots, made is None, step_at, len(arrived))),
        out_shape=out_shape,
        in_specs=[SMEM] + [ANY] * (len(operands) - 1),
        out_specs=[ANY] * len(out_shape),
        scratch_shapes=scratch,
        input_output_aliases=aliases,
        compiler_params=pltpu.CompilerParams(vmem_limit_bytes=60 << 20),
        cost_estimate=pl.CostEstimate(flops=9 * 10**9, bytes_accessed=20 * 10**6, transcendentals=0),
        name="hidden_back",
    )(*operands)
    return result[:2], result[2], result[3], result[4]


def attention_back_kernel(cfg, *refs):
    seq, slots, radius, first_call, step_at = cfg
    rows = seq + slots
    counts, first_hbm, small_hbm = refs[:3]
    w_hbm = dict(zip(ATTENTION_WEIGHTS, refs[3:8]))
    st = dict(zip(ATTENTION_USED, refs[8:12]))
    refs = refs[12:]
    if not first_call:
        refs = refs[6:]
    fac = dict(zip((D_Q, D_K, D_V), refs[:3]))
    tab_out, long_back, glob_back, d_send = refs[3:7]
    refs = refs[7:]
    w = dict(zip(ATTENTION_WEIGHTS, refs[:5]))
    sc = dict(zip(ATTENTION_USED, refs[5:9]))
    fs = dict(zip((D_Q, D_K, D_V), refs[9:12]))
    da, dx, dx_low, tab_s, small, small_t, flip, vc, sems = refs[12:]
    item, _, active, _ = turn_of(counts, step_at, False)

    @pl.when(active)
    def _():
        cp = Copies(sems)
        loads = {S_X: cp.start(first_hbm, dx)}
        for name in (W_OUT, S_V, S_P, TABLE, S_K, S_Q):
            if name in w:
                dst = w[name].at[0:w_hbm[name].shape[0]] if name == TABLE else w[name]
                loads[name] = cp.start(w_hbm[name], dst)
            else:
                loads[name] = cp.start(st[name].at[item], sc[name])
        loads[S_TAB] = cp.start(small_hbm, small_t)
        for name in (W_QUERY, W_KEY, W_VALUE):
            loads[name] = cp.start(w_hbm[name], w[name])
        outs = []

        def save(name):
            outs.append(cp.start(fs[name], fac[name].at[item]))

        row = lax.broadcasted_iota(jnp.int32, (seq, seq), 0)
        col = lax.broadcasted_iota(jnp.int32, (seq, seq), 1)
        turn = (radius + 12) % seq
        flip[...] = jnp.where((row + col == turn) | (row + col == turn + seq), 1.0, 0.0).astype(BF16)
        vc[seq:, :] = jnp.zeros((128, vc.shape[1]), BF16)
        tab = w[TABLE]
        tab[192:, :] = jnp.zeros((tab.shape[0] - 192, tab.shape[1]), BF16)
        small[...] = jnp.zeros_like(small)
        loads[S_X].wait()
        loads[W_OUT].wait()
        da[...] = mm_t(dx[...].astype(BF16), w[W_OUT][...]).astype(BF16)
        for name in (S_Q, S_K, S_V, TABLE, S_P):
            loads[name].wait()
        vc[0:seq, :] = sc[S_V][0:seq, :]
        vc[seq + 64:seq + 64 + slots, :] = sc[S_V][seq:rows, :]
        tab[192:192 + slots, :] = sc[S_K][seq:rows, :]
        halves = head_masks()
        label = lax.broadcasted_iota(jnp.int32, (1, 256), 1)
        own_label = (label >= 12) & (label < 12 + 2 * radius + 1)

        def pair(p, carry):
            cols = pl.ds(pl.multiple_of(p * 128, 128), 128)
            qp = sc[S_Q][:, cols]
            kp = sc[S_K][0:seq, cols]
            rk = tab[:, cols]
            vp = vc[:, cols]
            dap = da[:, cols]
            q_t = qp.T
            da_t = dap.T
            dq, dk_t, dv_t = [], [], []
            for hh in range(2):
                h = p * 2 + hh
                dam = jnp.where(halves[hh], dap, jnp.zeros_like(dap))
                prob_low = sc[S_P][h]
                prob = prob_low.astype(F32)
                d_prob = mm_t(dam, vp)
                delta = jnp.sum(prob * d_prob, axis=-1, keepdims=True)
                ds = (prob * (d_prob - delta)).astype(BF16)
                ds1 = ds[:, 0:seq]
                turned = mm(flip[...], ds1[0:seq]).astype(BF16)
                turned = pltpu.roll(turned, 0, 1, stride=1, stride_axis=0)
                rel = mm(flip[...], turned).astype(BF16)
                far = jnp.concatenate(
                    [
                        jnp.concatenate([rel[:, 0:128], rel[:, 128:256] + ds[0:seq, seq:]], 1),
                        jnp.concatenate([jnp.zeros((slots, 128), BF16), ds[seq:rows, seq:]], 1),
                    ],
                    0,
                )
                dq.append(mm(ds1, kp) + mm(far, rk))
                own = slice(64 * hh, 64 * hh + 64)
                dk_t.append(jnp.concatenate([mm(q_t[own], ds1), mm(q_t[own], far)], 1) * 0.125)
                dv_t.append(mm(da_t[own], prob_low))
            fs[D_Q][:, cols] = (jnp.where(halves[0], dq[0], dq[1]) * 0.125).astype(BF16)
            dk_t = jnp.concatenate(dk_t, 0)
            dv_t = jnp.concatenate(dv_t, 0)
            fs[D_K][0:seq, cols] = dk_t[:, 0:seq].T.astype(BF16)
            fs[D_K][seq:rows, cols] = dk_t[:, seq + 128:].T[64:64 + slots].astype(BF16)
            fs[D_V][0:seq, cols] = dv_t[:, 0:seq].T.astype(BF16)
            fs[D_V][seq:rows, cols] = dv_t[:, seq:].T[64:64 + slots].astype(BF16)
            tab_s[cols, :] = jnp.where(own_label, dk_t[:, seq:], 0.0)
            return carry

        lax.fori_loop(0, H // 2, pair, 0)
        save(D_Q)
        save(D_K)
        save(D_V)
        small[64:65, :] = jnp.sum(fs[D_Q][...].astype(F32), axis=0, keepdims=True)
        small[65:66, :] = jnp.sum(fs[D_V][...].astype(F32), axis=0, keepdims=True)
        for name in (W_QUERY, W_KEY, W_VALUE, S_TAB):
            loads[name].wait()
        d_rows = (
            dx[...]
            + mm_t(fs[D_Q][...], w[W_QUERY][...])
            + mm_t(fs[D_K][...], w[W_KEY][...])
            + mm_t(fs[D_V][...], w[W_VALUE][...])
        )
        dx_low[...] = d_rows.astype(BF16)
        outs.append(cp.start(dx_low, d_send))
        dx[...] = d_rows
        outs.append(cp.start(dx.at[0:seq], rows_of(long_back, item, seq)))
        outs.append(cp.start(dx.at[seq:rows], rows_of(glob_back, item, slots)))
        tab_s[:, 128:] += small[...].T + small_t[...]
        outs.append(cp.start(tab_s, tab_out.at[item]))
        for copy in outs:
            copy.wait()


def run_attention_back(step_at, counts, d_first, small, weights, state, made, seq, slots, radius):
    rows, width = d_first.shape
    named, kept = dict(zip(WEIGHTS, weights)), dict(zip(STATE, state))
    items = kept[S_Q].shape[0]
    low = jax.ShapeDtypeStruct((items, rows, width), BF16)
    out_shape = [low, low, low, jax.ShapeDtypeStruct((items, width, 256), F32),
                 jax.ShapeDtypeStruct((items * seq, width), F32), jax.ShapeDtypeStruct((items * slots, width), F32),
                 jax.ShapeDtypeStruct((rows, width), BF16)]
    operands = [counts, d_first, small] + [named[n] for n in ATTENTION_WEIGHTS] + [kept[n] for n in ATTENTION_USED]
    aliases = {}
    if made is not None:
        aliases = {len(operands) + n: n for n in range(6)}
        operands += list(made)
    scratch = [vm((256, width)) if n == TABLE else vm(named[n].shape) for n in ATTENTION_WEIGHTS]
    scratch += [vm(kept[n].shape[1:], kept[n].dtype) for n in ATTENTION_USED]
    scratch += [vm((rows, width))] * 3
    scratch += [vm((rows, width)), vm((rows, width), F32), vm((rows, width)), vm((width, 256), F32), vm((128, width), F32),
                vm((width, 128), F32), vm((seq, seq)), vm((seq + 128, width)), pltpu.SemaphoreType.DMA((32,))]
    result = pl.pallas_call(
        functools.partial(attention_back_kernel, (seq, slots, radius, made is None, step_at)),
        out_shape=out_shape,
        in_specs=[SMEM] + [ANY] * (len(operands) - 1),
        out_specs=[ANY] * len(out_shape),
        scratch_shapes=scratch,
        input_output_aliases=aliases,
        compiler_params=pltpu.CompilerParams(vmem_limit_bytes=60 << 20),
        cost_estimate=pl.CostEstimate(flops=15 * 10**9, bytes_accessed=20 * 10**6, transcendentals=0),
        name="attention_back",
    )(*operands)
    return result[:6], result[6]


TILE = 16
MESH_ID = pl.DeviceIdType.MESH
NZ, NY, NX = 4, 2, 2
LOADED = (S_X, S_ATT, D_BRANCH, D_Q, D_K, D_V)
CHUNKS = ((1, 0), (0, 1)) * 6 + ((1, 0),)
ENTER = (0, 0, 1, 3, 4, 5, 6, 7, 8, 9, 10, 11, 12)
PIECES = 4
SPACING = 2
FFN_ORDER = (0, 3, 1, 2)
STAGES = 6
PER_CHUNK = 7
PER_FFN = 4


def reduce_kernel(cfg, *refs):
    rows, width, hidden = cfg
    wide, narrow = hidden // SHARDS, width // SHARDS
    ins = dict(zip(LOADED, refs[:6]))
    n1_hbm, n1_near, df_hbm, df_a, df_b, df_c, up_hbm, bias_hbm, down_hbm, tab_hbm, red = refs[6:17]
    refs = refs[17:]
    buf = dict(zip(LOADED, refs[:6]))
    n1, df, w_up, b_up, w_down, tab, ga, gf, ay, ax, az, by, bz, bx, fx, fz, u, d_hid = refs[6:24]
    load_sems, send_sems, recv_sems = refs[24:]
    section = lax.axis_index("section")
    me = lax.axis_index("dp")
    x, y, z = lax.rem(me, NX), lax.rem(lax.div(me, NX), NY), lax.div(me, NX * NY)
    half = rows // 2

    def at(zz, yy, xx):
        return (section, (zz * NY + yy) * NX + xx)

    across_x, across_y = at(z, y, 1 - x), at(z, 1 - y, x)
    above, below = at(z + 1, y, x), at(z - 1, y, x)

    cp = Copies(load_sems)
    loads = {}
    for name in (D_BRANCH, S_ATT):
        loads[name] = [cp.start(ins[name], buf[name])]
    loads[S_N1] = [cp.start(n1_hbm, n1.at[0:rows]), cp.start(n1_near, n1.at[rows:])]
    loads[D_FFN] = [cp.start(df_hbm, df.at[0:rows])]
    first_section = section == 0
    loads[D_FFN].append(cp.choose(first_section, df_b, df_a, df.at[rows:rows + half]))
    loads[D_FFN].append(cp.choose(first_section, df_c, df_b, df.at[rows + half:]))
    loads[B_UP] = [cp.start(bias_hbm, b_up)]
    for n in FFN_ORDER:
        units = pl.ds(pl.multiple_of((2 * n + y) * 2 * wide, 2 * wide), 2 * wide)
        loads[W_UP, n] = [cp.start(up_hbm.at[:, units], w_up.at[n]), cp.start(down_hbm.at[units], w_down.at[n])]
    for name in (S_X, D_Q, D_K, D_V):
        loads[name] = [cp.start(ins[name], buf[name])]
    loads[S_TAB] = [cp.start(tab_hbm, tab)]

    barrier = pltpu.get_barrier_semaphore()
    for other in (across_x, across_y):
        pl.semaphore_signal(barrier, inc=1, device_id=other, device_id_type=MESH_ID)

    @pl.when(z > 0)
    def _():
        pl.semaphore_signal(barrier, inc=1, device_id=below, device_id_type=MESH_ID)

    @pl.when(z < NZ - 1)
    def _():
        pl.semaphore_signal(barrier, inc=1, device_id=above, device_id_type=MESH_ID)

    def need(*names):
        for name in names:
            for copy in loads.pop(name, ()):
                copy.wait()

    def units_of(n):
        return pl.ds(pl.multiple_of((2 * n + y) * 2 * wide, 2 * wide), 2 * wide)

    def form_hidden(n):
        need(S_N1, D_FFN, B_UP, (W_UP, n))
        act, slope = gelu_parts(mm(n1[...], w_up[n]) + b_up[:, units_of(n)].astype(F32))
        u[...] = act.astype(BF16)
        d_hid[...] = (slope * mm_t(df[...], w_down[n])).astype(BF16)

    def form_down(n):
        part = mm_c(u[...], df[...]).astype(BF16)
        gf[n, 0, 0:wide, :] = part[0:wide]
        gf[n, 1, 0:wide, :] = part[wide:]

    def form_up(n):
        part = mm_c(d_hid[...], n1[...]).astype(BF16)
        gf[n, 0, wide:, :] = part[0:wide]
        gf[n, 1, wide:, :] = part[wide:]

    def form_narrow(left, right, at_row):
        need(left, right)

        def body(n, carry):
            cols = pl.ds(pl.multiple_of(n * 8 * narrow, 8 * narrow), 8 * narrow)
            part = mm_c(buf[left][:, cols], buf[right][...]).astype(BF16)
            for k in range(8):
                ga[2 * n + k // 4, (k // 2) % 2, k % 2, at_row:at_row + narrow, :] = part[k * narrow:(k + 1) * narrow]
            return carry

        lax.fori_loop(0, SHARDS // 8, body, 0)

    def form_table(at_row):
        need(S_TAB)

        def body(n, carry):
            for k in range(narrow // TILE):
                rows_k = pl.ds(pl.multiple_of(n * narrow + k * TILE, TILE), TILE)
                part = tab[0, rows_k, :] + tab[1, rows_k, :]
                shard = ga.at[lax.div(n, 4), lax.rem(lax.div(n, 2), 2), lax.rem(n, 2), at_row:at_row + TILE]
                shard[:, 256 * k:256 * k + 256] = part.astype(BF16)
            return carry

        lax.fori_loop(0, SHARDS, body, 0)

    first = [0]
    for counts in CHUNKS:
        first.append(first[-1] + sum(counts))

    def spans(chunk, route):
        counts = CHUNKS[chunk]
        start = first[chunk] + sum(counts[:route])
        own = sum(CHUNKS[n][route] for n in range(chunk))
        size = counts[route] * TILE
        return slice(start * TILE, start * TILE + size), slice(own * TILE, own * TILE + size), size

    pending = []

    def remote(src, dst, index, target):
        return pltpu.make_async_remote_copy(
            src_ref=src, dst_ref=dst, send_sem=send_sems.at[index], recv_sem=recv_sems.at[index],
            device_id=target, device_id_type=MESH_ID,
        )

    def send(src, dst, index, target):
        remote(src, dst, index, target).start()
        pending.append((None, lambda: remote(src, dst, index, target).wait_send()))

    def add(dst, src, lead):
        total = 1
        for n in lead:
            total *= n

        def body(n, carry):
            idx, rest = [], n
            for size in reversed(lead):
                idx.insert(0, lax.rem(rest, size))
                rest = lax.div(rest, size)
            d, s = dst(*idx), src(*idx)
            d[...] = (d[...].astype(F32) + s[...].astype(F32)).astype(BF16)
            return carry

        if total == 1:
            body(0, 0)
        else:
            lax.fori_loop(0, total, body, 0)

    def flow_z(stage, own, room, base, lead, shards=tuple(range(NZ))):
        def take(shard, slot, source):
            remote(own(shard), room(slot), base(slot), source).wait_recv()
            add(lambda *i: own(shard).at[i] if i else own(shard), lambda *i: room(slot).at[i] if i else room(slot), lead)

        def put(zz, shard, target):
            slot = NZ if (shard < zz and shard == zz - 1) else shard
            remote(own(shard), room(slot), base(slot), target).start()
            pending.append((zz, lambda: remote(own(shard), room(slot), base(slot), target).wait_send()))

        for zz in range(NZ):
            ups = [s for s in range(NZ - 1, zz - 1, -1) if s in shards]
            downs = [s for s in range(zz + 1) if s in shards]

            @pl.when(z == zz)
            def _():
                if stage == zz:
                    for shard in ups:
                        if zz > 0:
                            take(shard, shard, below)
                        if shard > zz:
                            put(zz, shard, above)
                if stage == NZ - 1 - zz:
                    for shard in downs:
                        if zz < NZ - 1:
                            take(shard, NZ if shard == zz else shard, above)
                        if shard < zz:
                            put(zz, shard, below)

    ffn_sems = len(CHUNKS) * PER_CHUNK

    def run(chunk, route, stage):
        rs, own, size = spans(chunk, route)
        if size == 0:
            return
        base = chunk * PER_CHUNK
        flow_base = lambda slot: base + 2 + slot
        out = slice(2 * wide + rs.start, 2 * wide + rs.stop)
        if stage == 0:
            room = ay if route == 0 else by
            send(ga.at[:, 1 - y, :, rs], room.at[:, :, own], base, across_y)
        if stage == 1:
            room = ay if route == 0 else by
            remote(ga.at[:, 1 - y, :, rs], room.at[:, :, own], base, across_y).wait_recv()
            add(lambda i, j: ga.at[i, y, j, rs], lambda i, j: room.at[i, j, own], (NZ, NX))
        if route == 0:
            if stage == 1:
                send(ga.at[:, y, 1 - x, rs], ax.at[:, own], base + 1, across_x)
            if stage == 2:
                remote(ga.at[:, y, 1 - x, rs], ax.at[:, own], base + 1, across_x).wait_recv()
                add(lambda i: ga.at[i, y, x, rs], lambda i: ax.at[i, own], (NZ,))
            if stage >= 2:
                flow_z(stage - 2, lambda s: ga.at[s, y, x, rs], lambda s: az.at[s, own], flow_base, ())
        else:
            if 1 <= stage <= 4:
                flow_z(stage - 1, lambda s: ga.at[s, y, :, rs], lambda s: bz.at[s, :, own], flow_base, (NX,))
            if stage == 4:
                send(ga.at[z, y, 1 - x, rs], bx.at[own], base + 1, across_x)
            if stage == 5:
                remote(ga.at[z, y, 1 - x, rs], bx.at[own], base + 1, across_x).wait_recv()
                add(lambda: ga.at[z, y, x, rs], lambda: bx.at[own], ())
        if stage == 5:
            red[out, :] = ga[z, y, x, rs, :].astype(F32)

    def run_ffn(n, piece, stage):
        base = ffn_sems + (n * PIECES + piece) * PER_FFN
        size = 2 * wide // PIECES
        rs = slice(piece * size, (piece + 1) * size)
        if stage == 0:
            send(gf.at[n, 1 - x, rs], fx.at[n, rs], base, across_x)
        if stage == 1:
            remote(gf.at[n, 1 - x, rs], fx.at[n, rs], base, across_x).wait_recv()
            add(lambda: gf.at[n, x, rs], lambda: fx.at[n, rs], ())
        if 1 <= stage <= 4:
            room = lambda slot: fz.at[1 if slot == NZ else 0, n, rs]
            flow_z(stage - 1, lambda s: gf.at[s, x, rs], room, lambda slot: base + (2 if slot == NZ else 1), (), (n,))
        if stage == 5:
            @pl.when(z == n)
            def _():
                red[rs, :] = gf[n, x, rs, :].astype(F32)

    def narrow_task(n):
        left, right = ((D_BRANCH, S_ATT), (D_Q, S_X), (D_K, S_X), (D_V, S_X))[n]
        return lambda: form_narrow(left, right, n * narrow)

    a, b, c, d = FFN_ORDER
    hidden_task = lambda n: lambda: form_hidden(n)
    down_task = lambda n: lambda: form_down(n)
    up_task = lambda n: lambda: form_up(n)
    tasks = [(up_task(a),), (narrow_task(1),), (hidden_task(b),), (down_task(b),), (narrow_task(2),), (up_task(b),),
             (hidden_task(c),), (down_task(c),), (narrow_task(3),), (up_task(c),),
             (hidden_task(d), lambda: form_table(4 * narrow)), (down_task(d),), (up_task(d),)]
    narrow_task(0)()

    @pl.when((z == 0) | (z == NZ - 1))
    def _():
        pl.semaphore_wait(barrier, 3)

    @pl.when((z > 0) & (z < NZ - 1))
    def _():
        pl.semaphore_wait(barrier, 4)

    starts = [(n, None, slot) for n, slot in enumerate(ENTER)]
    starts += [(FFN_ORDER[k // PIECES], k % PIECES, k) for k in range(NZ * PIECES)]
    last = max(slot for _, _, slot in starts) + SPACING * (STAGES - 1)
    for slot in range(last + 1):
        for stage in range(STAGES):
            for n, piece, enter in starts:
                if enter + stage * SPACING == slot:
                    if slot == 0 and piece == 0:
                        form_hidden(a)
                        form_down(a)
                    if piece is None:
                        run(n, 0, stage)
                        run(n, 1, stage)
                    else:
                        run_ffn(n, piece, stage)
            if stage == 0:
                for task in tasks.pop(0) if tasks else ():
                    task()
    for zz, wait in pending:
        if zz is None:
            wait()
        else:
            pl.when(z == zz)(wait)


def reduce_grads(parts, near, weights, tab):
    rows, width = parts[S_X].shape
    hidden = weights[W_UP].shape[1]
    wide, narrow = hidden // SHARDS, width // SHARDS
    share = 4 * narrow + TILE
    t = [sum(c[n] for c in CHUNKS) * TILE for n in range(2)]
    assert sum(t) == share
    n_sem = len(CHUNKS) * PER_CHUNK + NZ * PIECES * PER_FFN
    scratch = [vm(parts[n].shape) for n in LOADED]
    scratch += [
        vm((2 * rows, width)), vm((2 * rows, width)), vm((NZ, width, 2 * wide)), vm((1, hidden)), vm((NZ, 2 * wide, width)),
        vm(tab.shape, F32),
        vm((NZ, NY, NX, share, width)), vm((NZ, NX, 2 * wide, width)),
        vm((NZ, NX, t[0], width)), vm((NZ, t[0], width)), vm((NZ + 1, t[0], width)),
        vm((NZ, NX, t[1], width)), vm((NZ + 1, NX, t[1], width)), vm((t[1], width)),
        vm((NZ, 2 * wide, width)), vm((2, NZ, 2 * wide, width)), vm((2 * rows, 2 * wide)), vm((2 * rows, 2 * wide)),
        pltpu.SemaphoreType.DMA((32,)), pltpu.SemaphoreType.DMA((n_sem,)), pltpu.SemaphoreType.DMA((n_sem,)),
    ]
    operands = [parts[n] for n in LOADED]
    operands += [parts[S_N1], near[0], parts[D_FFN]] + list(near[1:])
    operands += [weights[W_UP], weights[B_UP], weights[W_DOWN], tab]
    return pl.pallas_call(
        functools.partial(reduce_kernel, (rows, width, hidden)),
        cost_estimate=pl.CostEstimate(flops=60 * 10**9, bytes_accessed=20 * 10**6, transcendentals=0),
        out_shape=jax.ShapeDtypeStruct((2 * wide + share, width), F32),
        in_specs=[ANY] * len(operands),
        out_specs=pl.BlockSpec(memory_space=pltpu.VMEM),
        scratch_shapes=scratch,
        compiler_params=pltpu.CompilerParams(collective_id=0, has_side_effects=True, vmem_limit_bytes=62 << 20),
        name="reduce_grads",
    )(*operands)


def share_of(red, width, hidden):
    wide, narrow = hidden // SHARDS, width // SHARDS
    low = 2 * wide
    cut = [red[low + n * narrow:low + (n + 1) * narrow].T for n in range(4)]
    packed = red[low + 4 * narrow:]
    table = jnp.concatenate([packed[:, 256 * k:256 * k + 256] for k in range(narrow // TILE)], 0)
    return cut, red[wide:low].T, red[0:wide], table


def sums_elsewhere(parts, weights, tab):
    def scatter(value, dim):
        return lax.psum_scatter(value, "dp", scatter_dimension=dim, tiled=True)

    cut = [scatter(mm_c(parts[a], parts[b]), 1)
           for a, b in ((S_ATT, D_BRANCH), (S_X, D_Q), (S_X, D_K), (S_X, D_V))]
    act, slope = gelu_parts(mm(parts[S_N1], weights[W_UP]) + weights[B_UP].astype(F32))
    d_hid = (slope * mm_t(parts[D_FFN], weights[W_DOWN])).astype(BF16)
    w_up = scatter(mm_c(parts[S_N1], d_hid), 1)
    w_down = scatter(mm_c(act.astype(BF16), parts[D_FFN]), 0)
    b_up = scatter(jnp.sum(d_hid.astype(F32), axis=0), 0)
    return cut, w_up, w_down, scatter(tab[0] + tab[1], 0), b_up


def per_device(
    long_input, global_input, counts, w_query, b_query, w_key, w_value, b_value, w_out, b_out, rel_table,
    norm1_gain, norm1_bias, w_up, b_up, w_down, b_down, norm2_gain, norm2_bias, long_cot, global_cot,
):
    items = counts.shape[0]
    seq, slots, width = long_input.shape[0] // items, global_input.shape[0] // items, long_input.shape[1]
    rows, hidden = seq + slots, w_up.shape[2]
    labels = rel_table.shape[1]
    radius = (labels - 1) // 2
    weights = [w_query[0], w_key[0], w_value[0], w_out[0], w_up[0], w_down[0],
               jnp.pad(rel_table[0], ((12, 192 - 12 - labels), (0, 0))),
               b_query, b_value, b_out, norm1_gain, norm1_bias, b_up, b_down, norm2_gain, norm2_bias]

    recv = long_input
    state = outs = None
    for step in range(items + 1):
        state, outs, sent = run_forward(
            step, counts, long_input, global_input, recv, weights, state, outs, seq, slots, radius)
        if step < items:
            recv = lax.ppermute(sent, "section", [(0, 1)])
    kept = dict(zip(STATE, state))
    shards = lax.axis_size("dp")
    paired = shards == SHARDS
    near, awaited = [], 0
    if paired:
        near = [lax.ppermute(kept[S_N1], "dp", [(n, n ^ NX) for n in range(shards)]).reshape(items * rows, width)]
    low = made = None
    for step in range(items + 1):
        low, d_ffn, d_first, small = run_hidden_back(
            step, counts, long_cot, global_cot, recv, weights, state, low, near[awaited:] if step else [], seq, slots)
        awaited = len(near) if step else 0
        if paired:
            pairs = [(e * shards + n, e * shards + (n ^ NX)) for e in range(2) for n in range(shards)
                     if 0 <= step - (1 - e) < items]
            near.append(lax.ppermute(d_ffn, ("section", "dp"), pairs))
        made, sent = run_attention_back(
            step, counts, d_first, small, weights, state, made, seq, slots, radius)
        if step < items:
            recv = lax.ppermute(sent, "section", [(1, 0)])
    parts = {n: kept[n] for n in (S_X, S_ATT, S_N1)}
    parts.update(zip((D_FFN, D_BRANCH, D_Q, D_K, D_V), list(low) + list(made[:3])))
    parts = {n: t.reshape(items * rows, t.shape[2]) for n, t in parts.items()}
    tab, long_back, glob_back = made[3:6]
    named = dict(zip(WEIGHTS, weights))
    if paired:
        cut, g_up, g_down, table = share_of(reduce_grads(parts, near, named, tab), width, hidden)
        g_b_up = jnp.concatenate([table[:, 128 + BIAS_LANE + k] for k in range(hidden // width)], 0)
    else:
        cut, g_up, g_down, table, g_b_up = sums_elsewhere(parts, named, tab)
    g_out, g_query, g_key, g_value = cut
    small = [table[:, 192 + n] for n in range(8)]
    g_bq, g_bv, g_bo, g_g1, g_s1, g_bd, g_g2, g_s2 = small
    grads = (g_query, g_bq, g_key, g_value, g_bv, g_out, g_bo, table[:, 12:12 + labels].T, g_g1, g_s1,
             g_up, g_b_up, g_down, g_bd, g_g2, g_s2)
    return tuple(t[None] for t in (outs[0], outs[1], long_back, glob_back) + grads)


def solution(mesh):
    part = P("section", "dp", None)
    vector = P("section", "dp")
    columns = P("section", None, "dp")
    matrix = P("section", None, None)
    row = P("section", None)
    items = P("dp", None)
    in_specs = (items, items, P("dp"), matrix, row, matrix, matrix, row, matrix, row, matrix, row, row,
                matrix, row, matrix, row, row, row, items, items)
    out_specs = (part, part, part, part, columns, vector, columns, columns, vector, columns, vector, columns,
                 vector, vector, columns, vector, part, vector, vector, vector)
    return jax.shard_map(per_device, mesh=mesh, in_specs=in_specs, out_specs=out_specs, check_vma=False)
```

```python
import functools
import math

import jax
import jax.numpy as jnp
from jax import lax
from jax.experimental import pallas as pl
from jax.experimental.pallas import tpu as pltpu
from jax.sharding import PartitionSpec as P

H = 12
F32 = jnp.float32
BF16 = jnp.bfloat16
ANY = pl.BlockSpec(memory_space=pl.ANY)
SMEM = pl.BlockSpec(memory_space=pltpu.SMEM)
NEG = -1e30
SHARDS = 16
BIAS_LANE = 72
(
    W_QUERY, W_KEY, W_VALUE, W_OUT, W_UP, W_DOWN, TABLE, BACK_TABLE, B_QUERY, B_VALUE, B_OUT, NORM1_GAIN, NORM1_BIAS, B_UP, B_DOWN, NORM2_GAIN, NORM2_BIAS,
    D_FFN, D_HIDDEN, D_BRANCH, D_Q, D_K, D_V, S_X, S_Q, S_K, S_V, S_ATT, S_N1, S_XH1, S_XH2, S_U, S_GP, S_P, S_RS1, S_RS2, S_TAB,
) = range(37)


def mm(a, b):
    return jnp.dot(a, b, preferred_element_type=F32)


def mm_t(a, b):
    return lax.dot_general(a, b, (((1,), (1,)), ((), ())), preferred_element_type=F32)


def mm_c(a, b):
    return lax.dot_general(a, b, (((0,), (0,)), ((), ())), preferred_element_type=F32)


class Copies:
    def __init__(self, sems):
        self.sems = sems
        self.used = 0

    def make(self, src, dst):
        copy = pltpu.make_async_copy(src, dst, self.sems.at[self.used])
        self.used += 1
        return copy

    def start(self, src, dst):
        copy = self.make(src, dst)
        copy.start()
        return copy

    def choose(self, first, src_a, src_b, dst):
        a = pltpu.make_async_copy(src_a, dst, self.sems.at[self.used])
        b = pltpu.make_async_copy(src_b, dst, self.sems.at[self.used])
        self.used += 1
        pl.when(first)(a.start)
        pl.when(jnp.logical_not(first))(b.start)
        return a


def normalize(rows):
    center = rows - jnp.mean(rows, axis=-1, keepdims=True)
    spread = jnp.mean(center * center, axis=-1, keepdims=True)
    rstd = lax.rsqrt(spread + 1e-05)
    return center * rstd, rstd


GELU_C = math.sqrt(2.0 / math.pi)


def gelu_parts(z):
    zz = z * z
    t = jnp.tanh(z * (GELU_C + (GELU_C * 0.044715) * zz))
    half = 0.5 + 0.5 * t
    slope = half + (0.5 * z) * (1.0 - t * t) * (GELU_C + (3.0 * GELU_C * 0.044715) * zz)
    return z * half, slope


WEIGHTS = (
    W_QUERY, W_KEY, W_VALUE, W_OUT, W_UP, W_DOWN, TABLE,
    B_QUERY, B_VALUE, B_OUT, NORM1_GAIN, NORM1_BIAS, B_UP, B_DOWN, NORM2_GAIN, NORM2_BIAS,
)
STATE = (S_X, S_Q, S_K, S_V, S_ATT, S_N1, S_XH1, S_XH2, S_GP, S_P, S_RS1, S_RS2)


def state_shapes(items, rows, width, hidden, keys):
    low = lambda *s: jax.ShapeDtypeStruct((items,) + s, BF16)
    shapes = {name: low(rows, width) for name in (S_X, S_Q, S_K, S_V, S_ATT, S_N1, S_XH1, S_XH2)}
    shapes[S_GP] = low(rows, hidden)
    shapes[S_P] = low(H, rows, keys)
    shapes[S_RS1] = shapes[S_RS2] = jax.ShapeDtypeStruct((items, rows, 128), F32)
    return [shapes[name] for name in STATE]


def head_masks():
    lane = lax.broadcasted_iota(jnp.int32, (1, 128), 1)
    return [lane < 64, lane >= 64]


def turn_of(counts, step_at, forward):
    section = lax.axis_index("section")
    first = (section == 0) if forward else (section == 1)
    turn = jnp.where(first, step_at, step_at - 1)
    item = jnp.clip(turn, 0, counts.shape[0] - 1)
    return item, counts[item], turn == item, first


def fwd_kernel(cfg, *refs):
    seq, slots, radius, first_call, step_at = cfg
    rows = seq + slots
    counts, x_long, x_glob, recv = refs[:4]
    w_hbm = dict(zip(WEIGHTS, refs[4:20]))
    refs = refs[20:]
    if not first_call:
        refs = refs[len(STATE) + 2:]
    st = dict(zip(STATE, refs[:len(STATE)]))
    long_out, glob_out, y_send = refs[len(STATE):len(STATE) + 3]
    refs = refs[len(STATE) + 3:]
    w = dict(zip(WEIGHTS, refs[:16]))
    sc = dict(zip(STATE, refs[16:16 + len(STATE)]))
    y_v, vc, bandm, ownm, sems = refs[16 + len(STATE):]
    item, count, active, fresh = turn_of(counts, step_at, True)

    @pl.when(active)
    def _():
        cp = Copies(sems)
        long_rows = pl.ds(pl.multiple_of(item * seq, seq), seq)
        glob_rows = pl.ds(pl.multiple_of(item * slots, slots), slots)
        c_x = cp.choose(fresh, x_long.at[long_rows], recv.at[0:seq], sc[S_X].at[0:seq])
        c_g = cp.choose(fresh, x_glob.at[glob_rows], recv.at[seq:rows], sc[S_X].at[seq:rows])
        loads = {}
        for name in (W_QUERY, B_QUERY, W_KEY, W_VALUE, B_VALUE, TABLE, W_OUT, B_OUT, NORM1_GAIN,
                     NORM1_BIAS, W_UP, B_UP, W_DOWN, B_DOWN, NORM2_GAIN, NORM2_BIAS):
            dst = w[name].at[0:w_hbm[name].shape[0]] if name == TABLE else w[name]
            loads[name] = cp.start(w_hbm[name], dst)
        outs = []

        def save(name):
            outs.append(cp.start(sc[name], st[name].at[item]))

        def vec(name):
            loads[name].wait()
            return w[name][...].astype(F32)

        row = lax.broadcasted_iota(jnp.int32, (seq, seq), 0)
        col = lax.broadcasted_iota(jnp.int32, (seq, seq), 1)
        bandm[...] = jnp.where(jnp.abs(col - row) <= radius, 0.0, NEG)
        key = lax.broadcasted_iota(jnp.int32, (slots, seq), 1)
        slot = lax.broadcasted_iota(jnp.int32, (slots, seq), 0)
        ownm[...] = jnp.where(lax.div(key * count, jnp.int32(seq)) == slot, 0.0, NEG)
        lane = lax.broadcasted_iota(jnp.int32, (1, 128), 1)
        globm = jnp.where((lane >= 64) & (lane < 64 + count), 0.0, NEG)
        vc[seq:, :] = jnp.zeros((128, vc.shape[1]), BF16)
        tab = w[TABLE]
        tab[192:, :] = jnp.zeros((tab.shape[0] - 192, tab.shape[1]), BF16)

        c_x.wait()
        c_g.wait()
        x = sc[S_X][...]
        save(S_X)
        loads[W_QUERY].wait()
        sc[S_Q][...] = (mm(x, w[W_QUERY][...]) + vec(B_QUERY)).astype(BF16)
        save(S_Q)
        loads[W_KEY].wait()
        k = mm(x, w[W_KEY][...]).astype(BF16)
        sc[S_K][...] = k
        save(S_K)
        loads[W_VALUE].wait()
        v = (mm(x, w[W_VALUE][...]) + vec(B_VALUE)).astype(BF16)
        sc[S_V][...] = v
        save(S_V)
        vc[0:seq, :] = v[0:seq]
        vc[seq + 64:seq + 64 + slots, :] = v[seq:rows]
        loads[TABLE].wait()
        tab[192:192 + slots, :] = k[seq:rows]
        halves = head_masks()

        ones_cols = jnp.ones((vc.shape[0], 128), BF16)
        live, done = {}, {}

        def scores(h):
            cols = slice(128 * (h // 2), 128 * (h // 2) + 128)
            qp = sc[S_Q][:, cols]
            qm = jnp.where(halves[h % 2], qp, jnp.zeros_like(qp)) * jnp.bfloat16(0.125)
            s1 = mm_t(qm, sc[S_K][0:seq, cols])
            s2 = mm_t(qm, tab[:, cols])
            band = pltpu.roll(s2[0:seq], (2 * seq - radius - 12) % seq, 1, stride=1, stride_axis=0)
            live[h] = (s1[0:seq] + band + bandm[...], s2[0:seq, 128:256] + globm,
                       s1[seq:rows] + ownm[...], s2[seq:rows, 128:256] + globm)

        def weigh(h):
            ll, lg, gl, gg = live.pop(h)
            parts = []
            for sl, sg in ((ll, lg), (gl, gg)):
                top = jnp.max(jnp.maximum(jnp.maximum(sl[:, 0:128], sl[:, 128:256]), sg), axis=-1, keepdims=True)
                parts.append(jnp.concatenate([jnp.exp(sl - top), jnp.exp(sg - top)], 1))
            live[h] = jnp.concatenate(parts, 0)

        def gather(h):
            cols = slice(128 * (h // 2), 128 * (h // 2) + 128)
            e = live.pop(h)
            got = mm(e.astype(BF16), jnp.concatenate([vc[:, cols], ones_cols], 1))
            inv = 1.0 / got[:, 128:]
            done[h] = got[:, 0:128] * inv
            for c in range(3):
                sc[S_P][h, :, 128 * c:128 * c + 128] = (e[:, 128 * c:128 * c + 128] * inv).astype(BF16)
            if h % 2:
                sc[S_ATT][:, cols] = jnp.where(halves[0], done.pop(h - 1), done.pop(h)).astype(BF16)

        for turn in range(H + 2):
            if turn < H:
                scores(turn)
            if 0 <= turn - 1 < H:
                weigh(turn - 1)
            if 0 <= turn - 2 < H:
                gather(turn - 2)
        save(S_P)
        save(S_ATT)
        loads[W_OUT].wait()
        r1 = x.astype(F32) + mm(sc[S_ATT][...], w[W_OUT][...]) + vec(B_OUT)
        xh1, rstd1 = normalize(r1)
        sc[S_XH1][...] = xh1.astype(BF16)
        save(S_XH1)
        sc[S_RS1][...] = jnp.broadcast_to(rstd1, (rows, 128))
        save(S_RS1)
        n1 = xh1 * vec(NORM1_GAIN) + vec(NORM1_BIAS)
        n1_low = n1.astype(BF16)
        sc[S_N1][...] = n1_low
        save(S_N1)
        hidden = w[W_UP].shape[1]
        step = 768
        loads[W_UP].wait()
        b_up = vec(B_UP)
        acc = n1 + vec(B_DOWN)
        for c in range(hidden // step):
            z = mm(n1_low, w[W_UP][:, c * step:(c + 1) * step]) + b_up[:, c * step:(c + 1) * step]
            act, slope = gelu_parts(z)
            act = act.astype(BF16)
            cols = slice(c * step, (c + 1) * step)
            sc[S_GP][:, cols] = slope.astype(BF16)
            outs.append(cp.start(sc[S_GP].at[:, cols], st[S_GP].at[item, :, cols]))
            if c == 0:
                loads[W_DOWN].wait()
            acc = acc + mm(act, w[W_DOWN][c * step:(c + 1) * step, :])
        xh2, rstd2 = normalize(acc)
        sc[S_XH2][...] = xh2.astype(BF16)
        save(S_XH2)
        sc[S_RS2][...] = jnp.broadcast_to(rstd2, (rows, 128))
        save(S_RS2)
        y = xh2 * vec(NORM2_GAIN) + vec(NORM2_BIAS)
        pos = lax.broadcasted_iota(jnp.int32, (rows, 1), 0)
        y = jnp.where(pos < seq + count, y, 0.0)
        y_v[...] = y.astype(BF16)
        outs.append(cp.start(y_v, y_send))
        outs.append(cp.start(y_v.at[0:seq], long_out.at[long_rows]))
        outs.append(cp.start(y_v.at[seq:rows], glob_out.at[glob_rows]))
        for copy in outs:
            copy.wait()


def vm(shape, dtype=BF16):
    return pltpu.VMEM(shape, dtype)


def run_forward(step_at, counts, x_long, x_glob, recv, weights, state, outs, seq, slots, radius):
    rows, width = seq + slots, x_long.shape[1]
    hidden = weights[4].shape[1]
    items = x_long.shape[0] // seq
    keys = seq + 128
    shapes = state_shapes(items, rows, width, hidden, keys)
    out_shape = shapes + [
        jax.ShapeDtypeStruct(x_long.shape, BF16),
        jax.ShapeDtypeStruct(x_glob.shape, BF16),
        jax.ShapeDtypeStruct((rows, width), BF16),
    ]
    first = state is None
    operands = [counts, x_long, x_glob, recv] + list(weights[:len(WEIGHTS)])
    aliases = {}
    if not first:
        base = len(operands)
        operands += list(state) + list(outs)
        aliases = {base + n: n for n in range(len(state) + 2)}
    scratch = []
    for name, t in zip(WEIGHTS, weights):
        scratch.append(vm((256, width)) if name == TABLE else vm(t.shape))
    scratch += [vm(s.shape[1:], s.dtype) for s in shapes]
    scratch += [vm((rows, width)), vm((keys, width)), vm((seq, seq), F32), vm((slots, seq), F32),
                pltpu.SemaphoreType.DMA((48,))]
    result = pl.pallas_call(
        functools.partial(fwd_kernel, (seq, slots, radius, first, step_at)),
        out_shape=out_shape,
        in_specs=[SMEM] + [ANY] * (len(operands) - 1),
        out_specs=[ANY] * len(out_shape),
        scratch_shapes=scratch,
        input_output_aliases=aliases,
        compiler_params=pltpu.CompilerParams(vmem_limit_bytes=60 << 20),
        cost_estimate=pl.CostEstimate(flops=20 * 10**9, bytes_accessed=20 * 10**6, transcendentals=0),
        name="layer_forward",
    )(*operands)
    n = len(STATE)
    return result[:n], result[n:n + 2], result[n + 2]


HIDDEN_USED = (S_XH1, S_XH2, S_GP, S_RS1, S_RS2)
HIDDEN_WEIGHTS = (W_UP, W_DOWN, NORM1_GAIN, NORM2_GAIN)
ATTENTION_USED = (S_Q, S_K, S_V, S_P)
ATTENTION_WEIGHTS = (W_QUERY, W_KEY, W_VALUE, W_OUT, BACK_TABLE)


def rows_of(ref, item, size):
    return ref.at[pl.ds(pl.multiple_of(item * size, size), size)]


def hidden_back_kernel(cfg, *refs):
    seq, slots, first_call, step_at, unread = cfg
    rows = seq + slots
    counts, c_long, c_glob, recv = refs[:4]
    w_hbm = dict(zip(HIDDEN_WEIGHTS, refs[4:8]))
    st = dict(zip(HIDDEN_USED, refs[8:13]))
    refs = refs[13:]
    if not first_call:
        refs = refs[2:]
    refs = refs[unread:]
    ffn_out, branch_out, ffn_now, first_out, small_out = refs[:5]
    refs = refs[5:]
    w = dict(zip(HIDDEN_WEIGHTS, refs[:4]))
    sc = dict(zip(HIDDEN_USED, refs[4:9]))
    dy, d_ffn_s, d_branch_s, d_first_s, small, small_t, sems = refs[9:]
    item, count, active, fresh = turn_of(counts, step_at, False)

    @pl.when(active)
    def _():
        cp = Copies(sems)
        c_y = cp.choose(fresh, rows_of(c_long, item, seq), recv.at[0:seq], dy.at[0:seq])
        c_g = cp.choose(fresh, rows_of(c_glob, item, slots), recv.at[seq:rows], dy.at[seq:rows])
        hidden, width = w[W_DOWN].shape
        step = width
        parts = [slice(c * step, (c + 1) * step) for c in range(hidden // step)]
        loads = {}
        for name in (S_RS2, S_XH2):
            loads[name] = cp.start(st[name].at[item], sc[name])
        loads[NORM2_GAIN] = cp.start(w_hbm[NORM2_GAIN], w[NORM2_GAIN])
        loads[S_GP] = cp.start(st[S_GP].at[item], sc[S_GP])
        for c, sl in enumerate(parts):
            loads[W_DOWN, c] = cp.start(w_hbm[W_DOWN].at[sl], w[W_DOWN].at[sl])
            loads[W_UP, c] = cp.start(w_hbm[W_UP].at[:, sl], w[W_UP].at[:, sl])
        for name in (S_RS1, S_XH1):
            loads[name] = cp.start(st[name].at[item], sc[name])
        loads[NORM1_GAIN] = cp.start(w_hbm[NORM1_GAIN], w[NORM1_GAIN])
        small[...] = jnp.zeros_like(small)
        pos = lax.broadcasted_iota(jnp.int32, (rows, 1), 0)
        lane = lax.broadcasted_iota(jnp.int32, (1, 128), 1)
        ones = jnp.ones((rows, 128), BF16)

        def norm_back(grad, xh, rstd, gain, at):
            small[at:at + 1, :] = jnp.sum(grad * xh, axis=0, keepdims=True)
            small[at + 1:at + 2, :] = jnp.sum(grad, axis=0, keepdims=True)
            dxh = grad * gain
            return rstd * (
                dxh - jnp.mean(dxh, axis=-1, keepdims=True) - xh * jnp.mean(dxh * xh, axis=-1, keepdims=True)
            )

        c_y.wait()
        c_g.wait()
        grad = jnp.where(pos < seq + count, dy[...].astype(F32), 0.0)
        for name in (NORM2_GAIN, S_XH2, S_RS2):
            loads[name].wait()
        d_second = norm_back(
            grad, sc[S_XH2][...].astype(F32), sc[S_RS2][:, 0:1], w[NORM2_GAIN][...].astype(F32), 70
        )
        d_ffn = d_second.astype(BF16)
        d_ffn_s[...] = d_ffn
        outs = [cp.start(d_ffn_s, ffn_out.at[item]), cp.start(d_ffn_s, ffn_now)]
        small[69:70, :] = jnp.sum(d_ffn.astype(F32), axis=0, keepdims=True)
        loads[S_GP].wait()
        d_normed = d_second
        wide, narrow = hidden // SHARDS, width // SHARDS
        for c, sl in enumerate(parts):
            loads[W_DOWN, c].wait()
            d_hid = (sc[S_GP][:, sl].astype(F32) * mm_t(d_ffn, w[W_DOWN][sl, :])).astype(BF16)
            loads[W_UP, c].wait()
            d_normed = d_normed + mm_t(d_hid, w[W_UP][:, sl])
            sums = mm_c(d_hid, ones)
            for shard in range(step // wide):
                block = jnp.zeros((narrow, 128), F32)
                for k in range(wide // narrow):
                    at = shard * wide + k * narrow
                    block = jnp.where(lane == BIAS_LANE + k, sums[at:at + narrow], block)
                at = (c * (step // wide) + shard) * narrow
                small_t[at:at + narrow, :] = block
        for name in (NORM1_GAIN, S_XH1, S_RS1):
            loads[name].wait()
        d_first = norm_back(
            d_normed, sc[S_XH1][...].astype(F32), sc[S_RS1][:, 0:1], w[NORM1_GAIN][...].astype(F32), 67
        )
        d_first_s[...] = d_first
        outs.append(cp.start(d_first_s, first_out))
        d_branch = d_first.astype(BF16)
        d_branch_s[...] = d_branch
        outs.append(cp.start(d_branch_s, branch_out.at[item]))
        small[66:67, :] = jnp.sum(d_branch.astype(F32), axis=0, keepdims=True)
        small_t[...] += small[...].T
        outs.append(cp.start(small_t, small_out))
        for copy in outs:
            copy.wait()


def run_hidden_back(step_at, counts, c_long, c_glob, recv, weights, state, made, arrived, seq, slots):
    rows, width = seq + slots, c_long.shape[1]
    named, kept = dict(zip(WEIGHTS + (BACK_TABLE,), weights)), dict(zip(STATE, state))
    items = c_long.shape[0] // seq
    low = jax.ShapeDtypeStruct((items, rows, width), BF16)
    out_shape = [low, low, jax.ShapeDtypeStruct((rows, width), BF16), jax.ShapeDtypeStruct((rows, width), F32),
                 jax.ShapeDtypeStruct((width, 128), F32)]
    operands = [counts, c_long, c_glob, recv] + [named[n] for n in HIDDEN_WEIGHTS] + [kept[n] for n in HIDDEN_USED]
    aliases = {}
    if made is not None:
        aliases = {len(operands): 0, len(operands) + 1: 1}
        operands += list(made)
    operands += list(arrived)
    scratch = [vm(named[n].shape) for n in HIDDEN_WEIGHTS]
    scratch += [vm(kept[n].shape[1:], kept[n].dtype) for n in HIDDEN_USED]
    scratch += [vm((rows, width)), vm((rows, width)), vm((rows, width)), vm((rows, width), F32),
                vm((128, width), F32), vm((width, 128), F32), pltpu.SemaphoreType.DMA((32,))]
    result = pl.pallas_call(
        functools.partial(hidden_back_kernel, (seq, slots, made is None, step_at, len(arrived))),
        out_shape=out_shape,
        in_specs=[SMEM] + [ANY] * (len(operands) - 1),
        out_specs=[ANY] * len(out_shape),
        scratch_shapes=scratch,
        input_output_aliases=aliases,
        compiler_params=pltpu.CompilerParams(vmem_limit_bytes=60 << 20),
        cost_estimate=pl.CostEstimate(flops=9 * 10**9, bytes_accessed=20 * 10**6, transcendentals=0),
        name="hidden_back",
    )(*operands)
    return result[:2], result[2], result[3], result[4]


def attention_back_kernel(cfg, *refs):
    seq, slots, radius, first_call, step_at = cfg
    rows = seq + slots
    counts, first_hbm, small_hbm = refs[:3]
    w_hbm = dict(zip(ATTENTION_WEIGHTS, refs[3:8]))
    st = dict(zip(ATTENTION_USED, refs[8:12]))
    refs = refs[12:]
    if not first_call:
        refs = refs[6:]
    fac = dict(zip((D_Q, D_K, D_V), refs[:3]))
    tab_out, long_back, glob_back, d_send = refs[3:7]
    refs = refs[7:]
    w = dict(zip(ATTENTION_WEIGHTS, refs[:5]))
    sc = dict(zip(ATTENTION_USED, refs[5:9]))
    fs = dict(zip((D_Q, D_K, D_V), refs[9:12]))
    da, dx, dx_low, tab_s, small, small_t, flip, vc, sems = refs[12:]
    item, _, active, _ = turn_of(counts, step_at, False)

    @pl.when(active)
    def _():
        cp = Copies(sems)
        loads = {S_X: cp.start(first_hbm, dx)}
        for name in (W_OUT, S_V, S_P, BACK_TABLE, S_K, S_Q):
            if name in w:
                dst = w[name].at[0:w_hbm[name].shape[0]] if name == BACK_TABLE else w[name]
                loads[name] = cp.start(w_hbm[name], dst)
            else:
                loads[name] = cp.start(st[name].at[item], sc[name])
        loads[S_TAB] = cp.start(small_hbm, small_t)
        for name in (W_QUERY, W_KEY, W_VALUE):
            loads[name] = cp.start(w_hbm[name], w[name])
        outs = []

        def save(name):
            outs.append(cp.start(fs[name], fac[name].at[item]))

        row = lax.broadcasted_iota(jnp.int32, (seq, seq), 0)
        col = lax.broadcasted_iota(jnp.int32, (seq, seq), 1)
        turn = (radius + 12) % seq
        flip[...] = jnp.where((row + col == turn) | (row + col == turn + seq), 1.0, 0.0).astype(BF16)
        vc[seq:, :] = jnp.zeros((128, vc.shape[1]), BF16)
        tab = w[BACK_TABLE]
        tab[192:, :] = jnp.zeros((tab.shape[0] - 192, tab.shape[1]), BF16)
        small[...] = jnp.zeros_like(small)
        loads[S_X].wait()
        loads[W_OUT].wait()
        da[...] = mm_t(dx[...].astype(BF16), w[W_OUT][...]).astype(BF16)
        for name in (S_Q, S_K, S_V, BACK_TABLE, S_P):
            loads[name].wait()
        vc[0:seq, :] = sc[S_V][0:seq, :]
        vc[seq + 64:seq + 64 + slots, :] = sc[S_V][seq:rows, :]
        tab[192:192 + slots, :] = sc[S_K][seq:rows, :]
        halves = head_masks()
        label = lax.broadcasted_iota(jnp.int32, (1, 256), 1)
        own_label = (label >= 12) & (label < 12 + 2 * radius + 1)

        def pair(p, carry):
            cols = pl.ds(pl.multiple_of(p * 128, 128), 128)
            qp = sc[S_Q][:, cols]
            kp = sc[S_K][0:seq, cols]
            rk = tab[:, cols]
            vp = vc[:, cols]
            dap = da[:, cols]
            q_t = qp.T
            da_t = dap.T
            dq, dk_t, dv_t = [], [], []
            for hh in range(2):
                h = p * 2 + hh
                dam = jnp.where(halves[hh], dap, jnp.zeros_like(dap))
                prob_low = sc[S_P][h]
                d_prob = mm_t(dam, vp)
                prob = [prob_low[:, 128 * c:128 * c + 128].astype(F32) for c in range(3)]
                d_prob = [d_prob[:, 128 * c:128 * c + 128] for c in range(3)]
                delta = jnp.sum(sum(a * b for a, b in zip(prob, d_prob)), axis=-1, keepdims=True)
                delta = delta / jnp.sum(sum(prob), axis=-1, keepdims=True)
                ds = jnp.concatenate([(a * (b - delta)).astype(BF16) for a, b in zip(prob, d_prob)], 1)
                ds1 = ds[:, 0:seq]
                rel = pltpu.roll(mm(ds1[0:seq], flip[...]).astype(BF16), 0, 1, stride=1, stride_axis=0)
                far = jnp.concatenate(
                    [
                        jnp.concatenate([rel[:, 0:128], rel[:, 128:256] + ds[0:seq, seq:]], 1),
                        jnp.concatenate([jnp.zeros((slots, 128), BF16), ds[seq:rows, seq:]], 1),
                    ],
                    0,
                )
                dq.append(mm(ds1, kp) + mm(far, rk))
                own = slice(64 * hh, 64 * hh + 64)
                dk_t.append(jnp.concatenate([mm(q_t[own], ds1), mm(q_t[own], far)], 1) * 0.125)
                dv_t.append(mm(da_t[own], prob_low).astype(BF16))
            fs[D_Q][:, cols] = (jnp.where(halves[0], dq[0], dq[1]) * 0.125).astype(BF16)
            dk_t = jnp.concatenate(dk_t, 0)
            dk_low = dk_t.astype(BF16)
            dv_t = jnp.concatenate(dv_t, 0)
            fs[D_K][0:seq, cols] = dk_low[:, 0:seq].T
            fs[D_K][seq:rows, cols] = dk_low[:, seq + 128:].T[64:64 + slots]
            fs[D_V][0:seq, cols] = dv_t[:, 0:seq].T
            fs[D_V][seq:rows, cols] = dv_t[:, seq:].T[64:64 + slots]
            tab_s[cols, :] = jnp.where(own_label, dk_t[:, seq:], 0.0)
            return carry

        lax.fori_loop(0, H // 2, pair, 0, unroll=True)
        save(D_Q)
        save(D_K)
        save(D_V)
        small[64:65, :] = jnp.sum(fs[D_Q][...].astype(F32), axis=0, keepdims=True)
        small[65:66, :] = jnp.sum(fs[D_V][...].astype(F32), axis=0, keepdims=True)
        for name in (W_QUERY, W_KEY, W_VALUE, S_TAB):
            loads[name].wait()
        d_rows = (
            dx[...]
            + mm_t(fs[D_Q][...], w[W_QUERY][...])
            + mm_t(fs[D_K][...], w[W_KEY][...])
            + mm_t(fs[D_V][...], w[W_VALUE][...])
        )
        dx_low[...] = d_rows.astype(BF16)
        outs.append(cp.start(dx_low, d_send))
        dx[...] = d_rows
        outs.append(cp.start(dx.at[0:seq], rows_of(long_back, item, seq)))
        outs.append(cp.start(dx.at[seq:rows], rows_of(glob_back, item, slots)))
        tab_s[:, 128:] += small[...].T + small_t[...]
        outs.append(cp.start(tab_s, tab_out.at[item]))
        for copy in outs:
            copy.wait()


def run_attention_back(step_at, counts, d_first, small, weights, state, made, seq, slots, radius):
    rows, width = d_first.shape
    named, kept = dict(zip(WEIGHTS + (BACK_TABLE,), weights)), dict(zip(STATE, state))
    items = kept[S_Q].shape[0]
    low = jax.ShapeDtypeStruct((items, rows, width), BF16)
    out_shape = [low, low, low, jax.ShapeDtypeStruct((items, width, 256), F32),
                 jax.ShapeDtypeStruct((items * seq, width), F32), jax.ShapeDtypeStruct((items * slots, width), F32),
                 jax.ShapeDtypeStruct((rows, width), BF16)]
    operands = [counts, d_first, small] + [named[n] for n in ATTENTION_WEIGHTS] + [kept[n] for n in ATTENTION_USED]
    aliases = {}
    if made is not None:
        aliases = {len(operands) + n: n for n in range(6)}
        operands += list(made)
    scratch = [vm((256, width)) if n == BACK_TABLE else vm(named[n].shape) for n in ATTENTION_WEIGHTS]
    scratch += [vm(kept[n].shape[1:], kept[n].dtype) for n in ATTENTION_USED]
    scratch += [vm((rows, width))] * 3
    scratch += [vm((rows, width)), vm((rows, width), F32), vm((rows, width)), vm((width, 256), F32), vm((128, width), F32),
                vm((width, 128), F32), vm((seq, seq)), vm((seq + 128, width)), pltpu.SemaphoreType.DMA((32,))]
    result = pl.pallas_call(
        functools.partial(attention_back_kernel, (seq, slots, radius, made is None, step_at)),
        out_shape=out_shape,
        in_specs=[SMEM] + [ANY] * (len(operands) - 1),
        out_specs=[ANY] * len(out_shape),
        scratch_shapes=scratch,
        input_output_aliases=aliases,
        compiler_params=pltpu.CompilerParams(vmem_limit_bytes=60 << 20),
        cost_estimate=pl.CostEstimate(flops=15 * 10**9, bytes_accessed=20 * 10**6, transcendentals=0),
        name="attention_back",
    )(*operands)
    return result[:6], result[6]


TILE = 16
MESH_ID = pl.DeviceIdType.MESH
NZ, NY, NX = 4, 2, 2
LOADED = (S_X, S_ATT, D_BRANCH, D_Q, D_K, D_V)
CHUNKS = ((1, 0), (0, 1)) * 6 + ((1, 0),)
ENTER = (0, 0, 1, 3, 4, 5, 6, 7, 8, 9, 10, 11, 12)
PIECES = 4
SPACING = 2
FFN_ORDER = (0, 3, 1, 2)
STAGES = 6
PER_CHUNK = 7
PER_FFN = 4


def reduce_kernel(cfg, *refs):
    rows, width, hidden = cfg
    wide, narrow = hidden // SHARDS, width // SHARDS
    ins = dict(zip(LOADED, refs[:6]))
    n1_hbm, n1_near, df_hbm, df_a, df_b, df_c, up_hbm, bias_hbm, down_hbm, tab_hbm, red = refs[6:17]
    refs = refs[17:]
    buf = dict(zip(LOADED, refs[:6]))
    n1, df, w_up, b_up, w_down, tab, ga, gf, ay, ax, az, by, bz, bx, fx, fz, u, d_hid = refs[6:24]
    load_sems, send_sems, recv_sems = refs[24:]
    section = lax.axis_index("section")
    me = lax.axis_index("dp")
    x, y, z = lax.rem(me, NX), lax.rem(lax.div(me, NX), NY), lax.div(me, NX * NY)
    half = rows // 2

    def at(zz, yy, xx):
        return (section, (zz * NY + yy) * NX + xx)

    across_x, across_y = at(z, y, 1 - x), at(z, 1 - y, x)
    above, below = at(z + 1, y, x), at(z - 1, y, x)

    cp = Copies(load_sems)
    loads = {}
    for name in (D_BRANCH, S_ATT):
        loads[name] = [cp.start(ins[name], buf[name])]
    loads[S_N1] = [cp.start(n1_hbm, n1.at[0:rows]), cp.start(n1_near, n1.at[rows:])]
    loads[D_FFN] = [cp.start(df_hbm, df.at[0:rows])]
    first_section = section == 0
    loads[D_FFN].append(cp.choose(first_section, df_b, df_a, df.at[rows:rows + half]))
    loads[D_FFN].append(cp.choose(first_section, df_c, df_b, df.at[rows + half:]))
    loads[B_UP] = [cp.start(bias_hbm, b_up)]
    for n in FFN_ORDER:
        units = pl.ds(pl.multiple_of((2 * n + y) * 2 * wide, 2 * wide), 2 * wide)
        loads[W_UP, n] = [cp.start(up_hbm.at[:, units], w_up.at[n]), cp.start(down_hbm.at[units], w_down.at[n])]
    for name in (S_X, D_Q, D_K, D_V):
        loads[name] = [cp.start(ins[name], buf[name])]
    loads[S_TAB] = [cp.start(tab_hbm, tab)]

    barrier = pltpu.get_barrier_semaphore()
    for other in (across_x, across_y):
        pl.semaphore_signal(barrier, inc=1, device_id=other, device_id_type=MESH_ID)

    @pl.when(z > 0)
    def _():
        pl.semaphore_signal(barrier, inc=1, device_id=below, device_id_type=MESH_ID)

    @pl.when(z < NZ - 1)
    def _():
        pl.semaphore_signal(barrier, inc=1, device_id=above, device_id_type=MESH_ID)

    def need(*names):
        for name in names:
            for copy in loads.pop(name, ()):
                copy.wait()

    def units_of(n):
        return pl.ds(pl.multiple_of((2 * n + y) * 2 * wide, 2 * wide), 2 * wide)

    def form_hidden(n):
        need(S_N1, D_FFN, B_UP, (W_UP, n))
        act, slope = gelu_parts(mm(n1[...], w_up[n]) + b_up[:, units_of(n)].astype(F32))
        u[...] = act.astype(BF16)
        d_hid[...] = (slope * mm_t(df[...], w_down[n])).astype(BF16)

    def form_down(n):
        part = mm_c(u[...], df[...]).astype(BF16)
        gf[n, 0, 0:wide, :] = part[0:wide]
        gf[n, 1, 0:wide, :] = part[wide:]

    def form_up(n):
        part = mm_c(d_hid[...], n1[...]).astype(BF16)
        gf[n, 0, wide:, :] = part[0:wide]
        gf[n, 1, wide:, :] = part[wide:]

    def form_narrow(left, right, at_row):
        need(left, right)

        def body(n, carry):
            cols = pl.ds(pl.multiple_of(n * 8 * narrow, 8 * narrow), 8 * narrow)
            part = mm_c(buf[left][:, cols], buf[right][...]).astype(BF16)
            for k in range(8):
                ga[2 * n + k // 4, (k // 2) % 2, k % 2, at_row:at_row + narrow, :] = part[k * narrow:(k + 1) * narrow]
            return carry

        lax.fori_loop(0, SHARDS // 8, body, 0)

    def form_table(at_row):
        need(S_TAB)

        def body(n, carry):
            for k in range(narrow // TILE):
                rows_k = pl.ds(pl.multiple_of(n * narrow + k * TILE, TILE), TILE)
                part = tab[0, rows_k, :] + tab[1, rows_k, :]
                shard = ga.at[lax.div(n, 4), lax.rem(lax.div(n, 2), 2), lax.rem(n, 2), at_row:at_row + TILE]
                shard[:, 256 * k:256 * k + 256] = part.astype(BF16)
            return carry

        lax.fori_loop(0, SHARDS, body, 0)

    first = [0]
    for counts in CHUNKS:
        first.append(first[-1] + sum(counts))

    def spans(chunk, route):
        counts = CHUNKS[chunk]
        start = first[chunk] + sum(counts[:route])
        own = sum(CHUNKS[n][route] for n in range(chunk))
        size = counts[route] * TILE
        return slice(start * TILE, start * TILE + size), slice(own * TILE, own * TILE + size), size

    pending = []

    def remote(src, dst, index, target):
        return pltpu.make_async_remote_copy(
            src_ref=src, dst_ref=dst, send_sem=send_sems.at[index], recv_sem=recv_sems.at[index],
            device_id=target, device_id_type=MESH_ID,
        )

    def send(src, dst, index, target):
        remote(src, dst, index, target).start()
        pending.append((None, lambda: remote(src, dst, index, target).wait_send()))

    def add(dst, src, lead):
        total = 1
        for n in lead:
            total *= n

        def body(n, carry):
            idx, rest = [], n
            for size in reversed(lead):
                idx.insert(0, lax.rem(rest, size))
                rest = lax.div(rest, size)
            d, s = dst(*idx), src(*idx)
            d[...] = (d[...].astype(F32) + s[...].astype(F32)).astype(BF16)
            return carry

        if total == 1:
            body(0, 0)
        else:
            lax.fori_loop(0, total, body, 0)

    def flow_z(stage, own, room, base, lead, shards=tuple(range(NZ))):
        def take(shard, slot, source):
            remote(own(shard), room(slot), base(slot), source).wait_recv()
            add(lambda *i: own(shard).at[i] if i else own(shard), lambda *i: room(slot).at[i] if i else room(slot), lead)

        def put(zz, shard, target):
            slot = NZ if (shard < zz and shard == zz - 1) else shard
            remote(own(shard), room(slot), base(slot), target).start()
            pending.append((zz, lambda: remote(own(shard), room(slot), base(slot), target).wait_send()))

        for zz in range(NZ):
            ups = [s for s in range(NZ - 1, zz - 1, -1) if s in shards]
            downs = [s for s in range(zz + 1) if s in shards]

            @pl.when(z == zz)
            def _():
                if stage == zz:
                    for shard in ups:
                        if zz > 0:
                            take(shard, shard, below)
                        if shard > zz:
                            put(zz, shard, above)
                if stage == NZ - 1 - zz:
                    for shard in downs:
                        if zz < NZ - 1:
                            take(shard, NZ if shard == zz else shard, above)
                        if shard < zz:
                            put(zz, shard, below)

    ffn_sems = len(CHUNKS) * PER_CHUNK

    def run(chunk, route, stage):
        rs, own, size = spans(chunk, route)
        if size == 0:
            return
        base = chunk * PER_CHUNK
        flow_base = lambda slot: base + 2 + slot
        out = slice(2 * wide + rs.start, 2 * wide + rs.stop)
        if stage == 0:
            room = ay if route == 0 else by
            send(ga.at[:, 1 - y, :, rs], room.at[:, :, own], base, across_y)
        if stage == 1:
            room = ay if route == 0 else by
            remote(ga.at[:, 1 - y, :, rs], room.at[:, :, own], base, across_y).wait_recv()
            add(lambda i, j: ga.at[i, y, j, rs], lambda i, j: room.at[i, j, own], (NZ, NX))
        if route == 0:
            if stage == 1:
                send(ga.at[:, y, 1 - x, rs], ax.at[:, own], base + 1, across_x)
            if stage == 2:
                remote(ga.at[:, y, 1 - x, rs], ax.at[:, own], base + 1, across_x).wait_recv()
                add(lambda i: ga.at[i, y, x, rs], lambda i: ax.at[i, own], (NZ,))
            if stage >= 2:
                flow_z(stage - 2, lambda s: ga.at[s, y, x, rs], lambda s: az.at[s, own], flow_base, ())
        else:
            if 1 <= stage <= 4:
                flow_z(stage - 1, lambda s: ga.at[s, y, :, rs], lambda s: bz.at[s, :, own], flow_base, (NX,))
            if stage == 4:
                send(ga.at[z, y, 1 - x, rs], bx.at[own], base + 1, across_x)
            if stage == 5:
                remote(ga.at[z, y, 1 - x, rs], bx.at[own], base + 1, across_x).wait_recv()
                add(lambda: ga.at[z, y, x, rs], lambda: bx.at[own], ())
        if stage == 5:
            red[out, :] = ga[z, y, x, rs, :].astype(F32)

    def run_ffn(n, piece, stage):
        base = ffn_sems + (n * PIECES + piece) * PER_FFN
        size = 2 * wide // PIECES
        rs = slice(piece * size, (piece + 1) * size)
        if stage == 0:
            send(gf.at[n, 1 - x, rs], fx.at[n, rs], base, across_x)
        if stage == 1:
            remote(gf.at[n, 1 - x, rs], fx.at[n, rs], base, across_x).wait_recv()
            add(lambda: gf.at[n, x, rs], lambda: fx.at[n, rs], ())
        if 1 <= stage <= 4:
            room = lambda slot: fz.at[1 if slot == NZ else 0, n, rs]
            flow_z(stage - 1, lambda s: gf.at[s, x, rs], room, lambda slot: base + (2 if slot == NZ else 1), (), (n,))
        if stage == 5:
            @pl.when(z == n)
            def _():
                red[rs, :] = gf[n, x, rs, :].astype(F32)

    def narrow_task(n):
        left, right = ((D_BRANCH, S_ATT), (D_Q, S_X), (D_K, S_X), (D_V, S_X))[n]
        return lambda: form_narrow(left, right, n * narrow)

    a, b, c, d = FFN_ORDER
    hidden_task = lambda n: lambda: form_hidden(n)
    down_task = lambda n: lambda: form_down(n)
    up_task = lambda n: lambda: form_up(n)
    tasks = [(up_task(a),), (narrow_task(1),), (hidden_task(b),), (down_task(b),), (narrow_task(2),), (up_task(b),),
             (hidden_task(c),), (down_task(c),), (narrow_task(3),), (up_task(c),),
             (hidden_task(d), lambda: form_table(4 * narrow)), (down_task(d),), (up_task(d),)]
    narrow_task(0)()

    @pl.when((z == 0) | (z == NZ - 1))
    def _():
        pl.semaphore_wait(barrier, 3)

    @pl.when((z > 0) & (z < NZ - 1))
    def _():
        pl.semaphore_wait(barrier, 4)

    starts = [(n, None, slot) for n, slot in enumerate(ENTER)]
    starts += [(FFN_ORDER[k // PIECES], k % PIECES, k) for k in range(NZ * PIECES)]
    last = max(slot for _, _, slot in starts) + SPACING * (STAGES - 1)
    for slot in range(last + 1):
        for stage in range(STAGES):
            for n, piece, enter in starts:
                if enter + stage * SPACING == slot:
                    if slot == 0 and piece == 0:
                        form_hidden(a)
                        form_down(a)
                    if piece is None:
                        run(n, 0, stage)
                        run(n, 1, stage)
                    else:
                        run_ffn(n, piece, stage)
            if stage == 0:
                for task in tasks.pop(0) if tasks else ():
                    task()
    for zz, wait in pending:
        if zz is None:
            wait()
        else:
            pl.when(z == zz)(wait)


def reduce_grads(parts, near, weights, tab):
    rows, width = parts[S_X].shape
    hidden = weights[W_UP].shape[1]
    wide, narrow = hidden // SHARDS, width // SHARDS
    share = 4 * narrow + TILE
    t = [sum(c[n] for c in CHUNKS) * TILE for n in range(2)]
    assert sum(t) == share
    n_sem = len(CHUNKS) * PER_CHUNK + NZ * PIECES * PER_FFN
    scratch = [vm(parts[n].shape) for n in LOADED]
    scratch += [
        vm((2 * rows, width)), vm((2 * rows, width)), vm((NZ, width, 2 * wide)), vm((1, hidden)), vm((NZ, 2 * wide, width)),
        vm(tab.shape, F32),
        vm((NZ, NY, NX, share, width)), vm((NZ, NX, 2 * wide, width)),
        vm((NZ, NX, t[0], width)), vm((NZ, t[0], width)), vm((NZ + 1, t[0], width)),
        vm((NZ, NX, t[1], width)), vm((NZ + 1, NX, t[1], width)), vm((t[1], width)),
        vm((NZ, 2 * wide, width)), vm((2, NZ, 2 * wide, width)), vm((2 * rows, 2 * wide)), vm((2 * rows, 2 * wide)),
        pltpu.SemaphoreType.DMA((32,)), pltpu.SemaphoreType.DMA((n_sem,)), pltpu.SemaphoreType.DMA((n_sem,)),
    ]
    operands = [parts[n] for n in LOADED]
    operands += [parts[S_N1], near[0], parts[D_FFN]] + list(near[1:])
    operands += [weights[W_UP], weights[B_UP], weights[W_DOWN], tab]
    return pl.pallas_call(
        functools.partial(reduce_kernel, (rows, width, hidden)),
        cost_estimate=pl.CostEstimate(flops=60 * 10**9, bytes_accessed=20 * 10**6, transcendentals=0),
        out_shape=jax.ShapeDtypeStruct((2 * wide + share, width), F32),
        in_specs=[ANY] * len(operands),
        out_specs=pl.BlockSpec(memory_space=pltpu.VMEM),
        scratch_shapes=scratch,
        compiler_params=pltpu.CompilerParams(collective_id=0, has_side_effects=True, vmem_limit_bytes=60 << 20),
        name="reduce_grads",
    )(*operands)


def share_of(red, width, hidden):
    wide, narrow = hidden // SHARDS, width // SHARDS
    low = 2 * wide
    cut = [red[low + n * narrow:low + (n + 1) * narrow].T for n in range(4)]
    packed = red[low + 4 * narrow:]
    table = jnp.concatenate([packed[:, 256 * k:256 * k + 256] for k in range(narrow // TILE)], 0)
    return cut, red[wide:low].T, red[0:wide], table


def sums_elsewhere(parts, weights, tab):
    def scatter(value, dim):
        return lax.psum_scatter(value, "dp", scatter_dimension=dim, tiled=True)

    cut = [scatter(mm_c(parts[a], parts[b]), 1)
           for a, b in ((S_ATT, D_BRANCH), (S_X, D_Q), (S_X, D_K), (S_X, D_V))]
    act, slope = gelu_parts(mm(parts[S_N1], weights[W_UP]) + weights[B_UP].astype(F32))
    d_hid = (slope * mm_t(parts[D_FFN], weights[W_DOWN])).astype(BF16)
    w_up = scatter(mm_c(parts[S_N1], d_hid), 1)
    w_down = scatter(mm_c(act.astype(BF16), parts[D_FFN]), 0)
    b_up = scatter(jnp.sum(d_hid.astype(F32), axis=0), 0)
    return cut, w_up, w_down, scatter(tab[0] + tab[1], 0), b_up


def per_device(
    long_input, global_input, counts, w_query, b_query, w_key, w_value, b_value, w_out, b_out, rel_table,
    norm1_gain, norm1_bias, w_up, b_up, w_down, b_down, norm2_gain, norm2_bias, long_cot, global_cot,
):
    items = counts.shape[0]
    seq, slots, width = long_input.shape[0] // items, global_input.shape[0] // items, long_input.shape[1]
    rows, hidden = seq + slots, w_up.shape[2]
    labels = rel_table.shape[1]
    radius = (labels - 1) // 2
    weights = [w_query[0], w_key[0], w_value[0], w_out[0], w_up[0], w_down[0],
               jnp.pad(rel_table[0], ((12, 192 - 12 - labels), (0, 0))),
               b_query, b_value, b_out, norm1_gain, norm1_bias, b_up, b_down, norm2_gain, norm2_bias,
               jnp.pad(rel_table[0, ::-1], ((12, 192 - 12 - labels), (0, 0)))]

    recv = long_input
    state = outs = None
    for step in range(items + 1):
        state, outs, sent = run_forward(
            step, counts, long_input, global_input, recv, weights, state, outs, seq, slots, radius)
        if step < items:
            recv = lax.ppermute(sent, "section", [(0, 1)])
    kept = dict(zip(STATE, state))
    shards = lax.axis_size("dp")
    paired = shards == SHARDS
    near = []
    if paired:
        near = [lax.ppermute(kept[S_N1], "dp", [(n, n ^ NX) for n in range(shards)]).reshape(items * rows, width)]
    low = made = None
    for step in range(items + 1):
        low, d_ffn, d_first, small = run_hidden_back(
            step, counts, long_cot, global_cot, recv, weights, state, low,
            near[0:1] if step == 1 else [], seq, slots)
        if paired:
            pairs = [(e * shards + n, e * shards + (n ^ NX)) for e in range(2) for n in range(shards)
                     if 0 <= step - (1 - e) < items]
            near.append(lax.ppermute(d_ffn, ("section", "dp"), pairs))
        made, sent = run_attention_back(
            step, counts, d_first, small, weights, state, made, seq, slots, radius)
        if step < items:
            if paired:
                sent, near[-1] = lax.optimization_barrier((sent, near[-1]))
            recv = lax.ppermute(sent, "section", [(1, 0)])
    parts = {n: kept[n] for n in (S_X, S_ATT, S_N1)}
    parts.update(zip((D_FFN, D_BRANCH, D_Q, D_K, D_V), list(low) + list(made[:3])))
    parts = {n: t.reshape(items * rows, t.shape[2]) for n, t in parts.items()}
    tab, long_back, glob_back = made[3:6]
    named = dict(zip(WEIGHTS, weights))
    if paired:
        cut, g_up, g_down, table = share_of(reduce_grads(parts, near, named, tab), width, hidden)
        g_b_up = jnp.concatenate([table[:, 128 + BIAS_LANE + k] for k in range(hidden // width)], 0)
    else:
        cut, g_up, g_down, table, g_b_up = sums_elsewhere(parts, named, tab)
    g_out, g_query, g_key, g_value = cut
    small = [table[:, 192 + n] for n in range(8)]
    g_bq, g_bv, g_bo, g_g1, g_s1, g_bd, g_g2, g_s2 = small
    grads = (g_query, g_bq, g_key, g_value, g_bv, g_out, g_bo, table[:, 12:12 + labels][:, ::-1].T, g_g1, g_s1,
             g_up, g_b_up, g_down, g_bd, g_g2, g_s2)
    return tuple(t[None] for t in (outs[0], outs[1], long_back, glob_back) + grads)


def solution(mesh):
    part = P("section", "dp", None)
    vector = P("section", "dp")
    columns = P("section", None, "dp")
    matrix = P("section", None, None)
    row = P("section", None)
    items = P("dp", None)
    in_specs = (items, items, P("dp"), matrix, row, matrix, matrix, row, matrix, row, matrix, row, row,
                matrix, row, matrix, row, row, row, items, items)
    out_specs = (part, part, part, part, columns, vector, columns, columns, vector, columns, vector, columns,
                 vector, vector, columns, vector, part, vector, vector, vector)
    return jax.shard_map(per_device, mesh=mesh, in_specs=in_specs, out_specs=out_specs, check_vma=False)
```

```python
import functools
import math

import jax
import jax.numpy as jnp
from jax import lax
from jax.experimental import pallas as pl
from jax.experimental.pallas import tpu as pltpu
from jax.sharding import PartitionSpec as P

H = 12
F32 = jnp.float32
BF16 = jnp.bfloat16
ANY = pl.BlockSpec(memory_space=pl.ANY)
SMEM = pl.BlockSpec(memory_space=pltpu.SMEM)
NEG = -1e30
SHARDS = 16
BIAS_LANE = 72
(
    W_QUERY, W_KEY, W_VALUE, W_OUT, W_UP, W_DOWN, TABLE, BACK_TABLE, B_QUERY, B_VALUE, B_OUT, NORM1_GAIN, NORM1_BIAS, B_UP, B_DOWN, NORM2_GAIN, NORM2_BIAS,
    D_FFN, D_HIDDEN, D_BRANCH, D_Q, D_K, D_V, S_X, S_Q, S_K, S_V, S_ATT, S_N1, S_XH1, S_XH2, S_U, S_GP, S_P, S_RS1, S_RS2, S_TAB,
) = range(37)


def mm(a, b):
    return jnp.dot(a, b, preferred_element_type=F32)


def mm_t(a, b):
    return lax.dot_general(a, b, (((1,), (1,)), ((), ())), preferred_element_type=F32)


def mm_c(a, b):
    return lax.dot_general(a, b, (((0,), (0,)), ((), ())), preferred_element_type=F32)


class Copies:
    def __init__(self, sems):
        self.sems = sems
        self.used = 0

    def make(self, src, dst):
        copy = pltpu.make_async_copy(src, dst, self.sems.at[self.used])
        self.used += 1
        return copy

    def start(self, src, dst):
        copy = self.make(src, dst)
        copy.start()
        return copy

    def choose(self, first, src_a, src_b, dst):
        a = pltpu.make_async_copy(src_a, dst, self.sems.at[self.used])
        b = pltpu.make_async_copy(src_b, dst, self.sems.at[self.used])
        self.used += 1
        pl.when(first)(a.start)
        pl.when(jnp.logical_not(first))(b.start)
        return a


def normalize(rows):
    center = rows - jnp.mean(rows, axis=-1, keepdims=True)
    spread = jnp.mean(center * center, axis=-1, keepdims=True)
    rstd = lax.rsqrt(spread + 1e-05)
    return center * rstd, rstd


GELU_C = math.sqrt(2.0 / math.pi)


def gelu_parts(z):
    zz = z * z
    t = jnp.tanh(z * (GELU_C + (GELU_C * 0.044715) * zz))
    half = 0.5 + 0.5 * t
    slope = half + (0.5 * z) * (1.0 - t * t) * (GELU_C + (3.0 * GELU_C * 0.044715) * zz)
    return z * half, slope


WEIGHTS = (
    W_QUERY, W_KEY, W_VALUE, W_OUT, W_UP, W_DOWN, TABLE,
    B_QUERY, B_VALUE, B_OUT, NORM1_GAIN, NORM1_BIAS, B_UP, B_DOWN, NORM2_GAIN, NORM2_BIAS,
)
STATE = (S_X, S_Q, S_K, S_V, S_ATT, S_N1, S_XH1, S_XH2, S_GP, S_P, S_RS1, S_RS2)


def state_shapes(items, rows, width, hidden, keys):
    low = lambda *s: jax.ShapeDtypeStruct((items,) + s, BF16)
    shapes = {name: low(rows, width) for name in (S_X, S_Q, S_K, S_V, S_ATT, S_N1, S_XH1, S_XH2)}
    shapes[S_GP] = low(rows, hidden)
    shapes[S_P] = low(H, rows, keys)
    shapes[S_RS1] = shapes[S_RS2] = jax.ShapeDtypeStruct((items, rows, 128), F32)
    return [shapes[name] for name in STATE]


def head_masks():
    lane = lax.broadcasted_iota(jnp.int32, (1, 128), 1)
    return [lane < 64, lane >= 64]


def turn_of(counts, step_at, forward):
    section = lax.axis_index("section")
    first = (section == 0) if forward else (section == 1)
    turn = jnp.where(first, step_at, step_at - 1)
    item = jnp.clip(turn, 0, counts.shape[0] - 1)
    return item, counts[item], turn == item, first


def fwd_kernel(cfg, *refs):
    seq, slots, radius, first_call, step_at = cfg
    rows = seq + slots
    counts, x_long, x_glob, recv = refs[:4]
    w_hbm = dict(zip(WEIGHTS, refs[4:20]))
    refs = refs[20:]
    if not first_call:
        refs = refs[len(STATE) + 2:]
    st = dict(zip(STATE, refs[:len(STATE)]))
    long_out, glob_out, y_send = refs[len(STATE):len(STATE) + 3]
    refs = refs[len(STATE) + 3:]
    w = dict(zip(WEIGHTS, refs[:16]))
    sc = dict(zip(STATE, refs[16:16 + len(STATE)]))
    y_v, vc, bandm, ownm, sems = refs[16 + len(STATE):]
    item, count, active, fresh = turn_of(counts, step_at, True)

    @pl.when(active)
    def _():
        cp = Copies(sems)
        long_rows = pl.ds(pl.multiple_of(item * seq, seq), seq)
        glob_rows = pl.ds(pl.multiple_of(item * slots, slots), slots)
        c_x = cp.choose(fresh, x_long.at[long_rows], recv.at[0:seq], sc[S_X].at[0:seq])
        c_g = cp.choose(fresh, x_glob.at[glob_rows], recv.at[seq:rows], sc[S_X].at[seq:rows])
        loads = {}
        for name in (W_QUERY, B_QUERY, W_KEY, W_VALUE, B_VALUE, TABLE, W_OUT, B_OUT, NORM1_GAIN,
                     NORM1_BIAS, W_UP, B_UP, W_DOWN, B_DOWN, NORM2_GAIN, NORM2_BIAS):
            dst = w[name].at[0:w_hbm[name].shape[0]] if name == TABLE else w[name]
            loads[name] = cp.start(w_hbm[name], dst)
        outs = []

        def save(name):
            outs.append(cp.start(sc[name], st[name].at[item]))

        def vec(name):
            loads[name].wait()
            return w[name][...].astype(F32)

        row = lax.broadcasted_iota(jnp.int32, (seq, seq), 0)
        col = lax.broadcasted_iota(jnp.int32, (seq, seq), 1)
        bandm[...] = jnp.where(jnp.abs(col - row) <= radius, 0.0, NEG)
        key = lax.broadcasted_iota(jnp.int32, (slots, seq), 1)
        slot = lax.broadcasted_iota(jnp.int32, (slots, seq), 0)
        ownm[...] = jnp.where(lax.div(key * count, jnp.int32(seq)) == slot, 0.0, NEG)
        lane = lax.broadcasted_iota(jnp.int32, (1, 128), 1)
        globm = jnp.where((lane >= 64) & (lane < 64 + count), 0.0, NEG)
        vc[seq:, :] = jnp.zeros((128, vc.shape[1]), BF16)
        tab = w[TABLE]
        tab[192:, :] = jnp.zeros((tab.shape[0] - 192, tab.shape[1]), BF16)

        c_x.wait()
        c_g.wait()
        x = sc[S_X][...]
        save(S_X)
        loads[W_QUERY].wait()
        sc[S_Q][...] = (mm(x, w[W_QUERY][...]) + vec(B_QUERY)).astype(BF16)
        save(S_Q)
        loads[W_KEY].wait()
        k = mm(x, w[W_KEY][...]).astype(BF16)
        sc[S_K][...] = k
        save(S_K)
        loads[W_VALUE].wait()
        v = (mm(x, w[W_VALUE][...]) + vec(B_VALUE)).astype(BF16)
        sc[S_V][...] = v
        save(S_V)
        vc[0:seq, :] = v[0:seq]
        vc[seq + 64:seq + 64 + slots, :] = v[seq:rows]
        loads[TABLE].wait()
        tab[192:192 + slots, :] = k[seq:rows]
        halves = head_masks()

        ones_cols = jnp.ones((vc.shape[0], 128), BF16)
        live, done = {}, {}

        def scores(h):
            cols = slice(128 * (h // 2), 128 * (h // 2) + 128)
            qp = sc[S_Q][:, cols]
            qm = jnp.where(halves[h % 2], qp, jnp.zeros_like(qp)) * jnp.bfloat16(0.125)
            s1 = mm_t(qm, sc[S_K][0:seq, cols])
            s2 = mm_t(qm, tab[:, cols])
            band = pltpu.roll(s2[0:seq], (2 * seq - radius - 12) % seq, 1, stride=1, stride_axis=0)
            live[h] = (s1[0:seq] + band + bandm[...], s2[0:seq, 128:256] + globm,
                       s1[seq:rows] + ownm[...], s2[seq:rows, 128:256] + globm)

        def weigh(h):
            ll, lg, gl, gg = live.pop(h)
            parts = []
            for sl, sg in ((ll, lg), (gl, gg)):
                top = jnp.max(jnp.maximum(jnp.maximum(sl[:, 0:128], sl[:, 128:256]), sg), axis=-1, keepdims=True)
                parts.append(jnp.concatenate([jnp.exp(sl - top), jnp.exp(sg - top)], 1))
            live[h] = jnp.concatenate(parts, 0)

        def gather(h):
            cols = slice(128 * (h // 2), 128 * (h // 2) + 128)
            e = live.pop(h)
            got = mm(e.astype(BF16), jnp.concatenate([vc[:, cols], ones_cols], 1))
            inv = 1.0 / got[:, 128:]
            done[h] = got[:, 0:128] * inv
            for c in range(3):
                sc[S_P][h, :, 128 * c:128 * c + 128] = (e[:, 128 * c:128 * c + 128] * inv).astype(BF16)
            if h % 2:
                sc[S_ATT][:, cols] = jnp.where(halves[0], done.pop(h - 1), done.pop(h)).astype(BF16)

        for turn in range(H + 2):
            if turn < H:
                scores(turn)
            if 0 <= turn - 1 < H:
                weigh(turn - 1)
            if 0 <= turn - 2 < H:
                gather(turn - 2)
        save(S_P)
        save(S_ATT)
        loads[W_OUT].wait()
        r1 = x.astype(F32) + mm(sc[S_ATT][...], w[W_OUT][...]) + vec(B_OUT)
        xh1, rstd1 = normalize(r1)
        sc[S_XH1][...] = xh1.astype(BF16)
        save(S_XH1)
        sc[S_RS1][...] = jnp.broadcast_to(rstd1, (rows, 128))
        save(S_RS1)
        n1 = xh1 * vec(NORM1_GAIN) + vec(NORM1_BIAS)
        n1_low = n1.astype(BF16)
        sc[S_N1][...] = n1_low
        save(S_N1)
        hidden = w[W_UP].shape[1]
        step = 768
        loads[W_UP].wait()
        b_up = vec(B_UP)
        acc = n1 + vec(B_DOWN)
        for c in range(hidden // step):
            z = mm(n1_low, w[W_UP][:, c * step:(c + 1) * step]) + b_up[:, c * step:(c + 1) * step]
            act, slope = gelu_parts(z)
            act = act.astype(BF16)
            cols = slice(c * step, (c + 1) * step)
            sc[S_GP][:, cols] = slope.astype(BF16)
            outs.append(cp.start(sc[S_GP].at[:, cols], st[S_GP].at[item, :, cols]))
            if c == 0:
                loads[W_DOWN].wait()
            acc = acc + mm(act, w[W_DOWN][c * step:(c + 1) * step, :])
        xh2, rstd2 = normalize(acc)
        sc[S_XH2][...] = xh2.astype(BF16)
        save(S_XH2)
        sc[S_RS2][...] = jnp.broadcast_to(rstd2, (rows, 128))
        save(S_RS2)
        y = xh2 * vec(NORM2_GAIN) + vec(NORM2_BIAS)
        pos = lax.broadcasted_iota(jnp.int32, (rows, 1), 0)
        y = jnp.where(pos < seq + count, y, 0.0)
        y_v[...] = y.astype(BF16)
        outs.append(cp.start(y_v, y_send))
        outs.append(cp.start(y_v.at[0:seq], long_out.at[long_rows]))
        outs.append(cp.start(y_v.at[seq:rows], glob_out.at[glob_rows]))
        for copy in outs:
            copy.wait()


def vm(shape, dtype=BF16):
    return pltpu.VMEM(shape, dtype)


def run_forward(step_at, counts, x_long, x_glob, recv, weights, state, outs, seq, slots, radius):
    rows, width = seq + slots, x_long.shape[1]
    hidden = weights[4].shape[1]
    items = x_long.shape[0] // seq
    keys = seq + 128
    shapes = state_shapes(items, rows, width, hidden, keys)
    out_shape = shapes + [
        jax.ShapeDtypeStruct(x_long.shape, BF16),
        jax.ShapeDtypeStruct(x_glob.shape, BF16),
        jax.ShapeDtypeStruct((rows, width), BF16),
    ]
    first = state is None
    operands = [counts, x_long, x_glob, recv] + list(weights[:len(WEIGHTS)])
    aliases = {}
    if not first:
        base = len(operands)
        operands += list(state) + list(outs)
        aliases = {base + n: n for n in range(len(state) + 2)}
    scratch = []
    for name, t in zip(WEIGHTS, weights):
        scratch.append(vm((256, width)) if name == TABLE else vm(t.shape))
    scratch += [vm(s.shape[1:], s.dtype) for s in shapes]
    scratch += [vm((rows, width)), vm((keys, width)), vm((seq, seq), F32), vm((slots, seq), F32),
                pltpu.SemaphoreType.DMA((48,))]
    result = pl.pallas_call(
        functools.partial(fwd_kernel, (seq, slots, radius, first, step_at)),
        out_shape=out_shape,
        in_specs=[SMEM] + [ANY] * (len(operands) - 1),
        out_specs=[ANY] * len(out_shape),
        scratch_shapes=scratch,
        input_output_aliases=aliases,
        compiler_params=pltpu.CompilerParams(vmem_limit_bytes=60 << 20),
        cost_estimate=pl.CostEstimate(flops=20 * 10**9, bytes_accessed=20 * 10**6, transcendentals=0),
        name="layer_forward",
    )(*operands)
    n = len(STATE)
    return result[:n], result[n:n + 2], result[n + 2]


HIDDEN_USED = (S_XH1, S_XH2, S_GP, S_RS1, S_RS2)
HIDDEN_WEIGHTS = (W_UP, W_DOWN, NORM1_GAIN, NORM2_GAIN)
ATTENTION_USED = (S_Q, S_K, S_V, S_P)
ATTENTION_WEIGHTS = (W_QUERY, W_KEY, W_VALUE, W_OUT, BACK_TABLE)


def rows_of(ref, item, size):
    return ref.at[pl.ds(pl.multiple_of(item * size, size), size)]


def hidden_back_kernel(cfg, *refs):
    seq, slots, first_call, step_at, unread = cfg
    rows = seq + slots
    counts, c_long, c_glob, recv = refs[:4]
    w_hbm = dict(zip(HIDDEN_WEIGHTS, refs[4:8]))
    st = dict(zip(HIDDEN_USED, refs[8:13]))
    refs = refs[13:]
    if not first_call:
        refs = refs[2:]
    refs = refs[unread:]
    ffn_out, branch_out, ffn_now, first_out, small_out = refs[:5]
    refs = refs[5:]
    w = dict(zip(HIDDEN_WEIGHTS, refs[:4]))
    sc = dict(zip(HIDDEN_USED, refs[4:9]))
    dy, d_ffn_s, d_branch_s, d_first_s, small, small_t, sems = refs[9:]
    item, count, active, fresh = turn_of(counts, step_at, False)

    @pl.when(active)
    def _():
        cp = Copies(sems)
        c_y = cp.choose(fresh, rows_of(c_long, item, seq), recv.at[0:seq], dy.at[0:seq])
        c_g = cp.choose(fresh, rows_of(c_glob, item, slots), recv.at[seq:rows], dy.at[seq:rows])
        hidden, width = w[W_DOWN].shape
        step = width
        parts = [slice(c * step, (c + 1) * step) for c in range(hidden // step)]
        loads = {}
        for name in (S_RS2, S_XH2):
            loads[name] = cp.start(st[name].at[item], sc[name])
        loads[NORM2_GAIN] = cp.start(w_hbm[NORM2_GAIN], w[NORM2_GAIN])
        loads[S_GP] = cp.start(st[S_GP].at[item], sc[S_GP])
        for c, sl in enumerate(parts):
            loads[W_DOWN, c] = cp.start(w_hbm[W_DOWN].at[sl], w[W_DOWN].at[sl])
            loads[W_UP, c] = cp.start(w_hbm[W_UP].at[:, sl], w[W_UP].at[:, sl])
        for name in (S_RS1, S_XH1):
            loads[name] = cp.start(st[name].at[item], sc[name])
        loads[NORM1_GAIN] = cp.start(w_hbm[NORM1_GAIN], w[NORM1_GAIN])
        small[...] = jnp.zeros_like(small)
        pos = lax.broadcasted_iota(jnp.int32, (rows, 1), 0)
        lane = lax.broadcasted_iota(jnp.int32, (1, 128), 1)
        ones = jnp.ones((rows, 128), BF16)

        def norm_back(grad, xh, rstd, gain, at):
            small[at:at + 1, :] = jnp.sum(grad * xh, axis=0, keepdims=True)
            small[at + 1:at + 2, :] = jnp.sum(grad, axis=0, keepdims=True)
            dxh = grad * gain
            return rstd * (
                dxh - jnp.mean(dxh, axis=-1, keepdims=True) - xh * jnp.mean(dxh * xh, axis=-1, keepdims=True)
            )

        c_y.wait()
        c_g.wait()
        grad = jnp.where(pos < seq + count, dy[...].astype(F32), 0.0)
        for name in (NORM2_GAIN, S_XH2, S_RS2):
            loads[name].wait()
        d_second = norm_back(
            grad, sc[S_XH2][...].astype(F32), sc[S_RS2][:, 0:1], w[NORM2_GAIN][...].astype(F32), 70
        )
        d_ffn = d_second.astype(BF16)
        d_ffn_s[...] = d_ffn
        outs = [cp.start(d_ffn_s, ffn_out.at[item]), cp.start(d_ffn_s, ffn_now)]
        small[69:70, :] = jnp.sum(d_ffn.astype(F32), axis=0, keepdims=True)
        loads[S_GP].wait()
        d_normed = d_second
        wide, narrow = hidden // SHARDS, width // SHARDS
        for c, sl in enumerate(parts):
            loads[W_DOWN, c].wait()
            d_hid = (sc[S_GP][:, sl].astype(F32) * mm_t(d_ffn, w[W_DOWN][sl, :])).astype(BF16)
            loads[W_UP, c].wait()
            d_normed = d_normed + mm_t(d_hid, w[W_UP][:, sl])
            sums = mm_c(d_hid, ones)
            for shard in range(step // wide):
                block = jnp.zeros((narrow, 128), F32)
                for k in range(wide // narrow):
                    at = shard * wide + k * narrow
                    block = jnp.where(lane == BIAS_LANE + k, sums[at:at + narrow], block)
                at = (c * (step // wide) + shard) * narrow
                small_t[at:at + narrow, :] = block
        for name in (NORM1_GAIN, S_XH1, S_RS1):
            loads[name].wait()
        d_first = norm_back(
            d_normed, sc[S_XH1][...].astype(F32), sc[S_RS1][:, 0:1], w[NORM1_GAIN][...].astype(F32), 67
        )
        d_first_s[...] = d_first
        outs.append(cp.start(d_first_s, first_out))
        d_branch = d_first.astype(BF16)
        d_branch_s[...] = d_branch
        outs.append(cp.start(d_branch_s, branch_out.at[item]))
        small[66:67, :] = jnp.sum(d_branch.astype(F32), axis=0, keepdims=True)
        small_t[...] += small[...].T
        outs.append(cp.start(small_t, small_out))
        for copy in outs:
            copy.wait()


def run_hidden_back(step_at, counts, c_long, c_glob, recv, weights, state, made, arrived, seq, slots):
    rows, width = seq + slots, c_long.shape[1]
    named, kept = dict(zip(WEIGHTS + (BACK_TABLE,), weights)), dict(zip(STATE, state))
    items = c_long.shape[0] // seq
    low = jax.ShapeDtypeStruct((items, rows, width), BF16)
    out_shape = [low, low, jax.ShapeDtypeStruct((rows, width), BF16), jax.ShapeDtypeStruct((rows, width), F32),
                 jax.ShapeDtypeStruct((width, 128), F32)]
    operands = [counts, c_long, c_glob, recv] + [named[n] for n in HIDDEN_WEIGHTS] + [kept[n] for n in HIDDEN_USED]
    aliases = {}
    if made is not None:
        aliases = {len(operands): 0, len(operands) + 1: 1}
        operands += list(made)
    operands += list(arrived)
    scratch = [vm(named[n].shape) for n in HIDDEN_WEIGHTS]
    scratch += [vm(kept[n].shape[1:], kept[n].dtype) for n in HIDDEN_USED]
    scratch += [vm((rows, width)), vm((rows, width)), vm((rows, width)), vm((rows, width), F32),
                vm((128, width), F32), vm((width, 128), F32), pltpu.SemaphoreType.DMA((32,))]
    result = pl.pallas_call(
        functools.partial(hidden_back_kernel, (seq, slots, made is None, step_at, len(arrived))),
        out_shape=out_shape,
        in_specs=[SMEM] + [ANY] * (len(operands) - 1),
        out_specs=[ANY] * len(out_shape),
        scratch_shapes=scratch,
        input_output_aliases=aliases,
        compiler_params=pltpu.CompilerParams(vmem_limit_bytes=60 << 20),
        cost_estimate=pl.CostEstimate(flops=9 * 10**9, bytes_accessed=20 * 10**6, transcendentals=0),
        name="hidden_back",
    )(*operands)
    return result[:2], result[2], result[3], result[4]


def attention_back_kernel(cfg, *refs):
    seq, slots, radius, first_call, step_at = cfg
    rows = seq + slots
    counts, first_hbm, small_hbm = refs[:3]
    w_hbm = dict(zip(ATTENTION_WEIGHTS, refs[3:8]))
    st = dict(zip(ATTENTION_USED, refs[8:12]))
    refs = refs[12:]
    if not first_call:
        refs = refs[6:]
    fac = dict(zip((D_Q, D_K, D_V), refs[:3]))
    tab_out, long_back, glob_back, d_send = refs[3:7]
    refs = refs[7:]
    w = dict(zip(ATTENTION_WEIGHTS, refs[:5]))
    sc = dict(zip(ATTENTION_USED, refs[5:9]))
    fs = dict(zip((D_Q, D_K, D_V), refs[9:12]))
    da, dx, dx_low, tab_s, small, small_t, flip, vc, sems = refs[12:]
    item, _, active, _ = turn_of(counts, step_at, False)

    @pl.when(active)
    def _():
        cp = Copies(sems)
        loads = {S_X: cp.start(first_hbm, dx)}
        for name in (W_OUT, S_V, S_P, BACK_TABLE, S_K, S_Q):
            if name in w:
                dst = w[name].at[0:w_hbm[name].shape[0]] if name == BACK_TABLE else w[name]
                loads[name] = cp.start(w_hbm[name], dst)
            else:
                loads[name] = cp.start(st[name].at[item], sc[name])
        loads[S_TAB] = cp.start(small_hbm, small_t)
        for name in (W_QUERY, W_KEY, W_VALUE):
            loads[name] = cp.start(w_hbm[name], w[name])
        outs = []

        def save(name):
            outs.append(cp.start(fs[name], fac[name].at[item]))

        row = lax.broadcasted_iota(jnp.int32, (seq, seq), 0)
        col = lax.broadcasted_iota(jnp.int32, (seq, seq), 1)
        turn = (radius + 12) % seq
        flip[...] = jnp.where((row + col == turn) | (row + col == turn + seq), 1.0, 0.0).astype(BF16)
        vc[seq:, :] = jnp.zeros((128, vc.shape[1]), BF16)
        tab = w[BACK_TABLE]
        tab[192:, :] = jnp.zeros((tab.shape[0] - 192, tab.shape[1]), BF16)
        small[...] = jnp.zeros_like(small)
        loads[S_X].wait()
        loads[W_OUT].wait()
        da[...] = mm_t(dx[...].astype(BF16), w[W_OUT][...]).astype(BF16)
        for name in (S_Q, S_K, S_V, BACK_TABLE, S_P):
            loads[name].wait()
        vc[0:seq, :] = sc[S_V][0:seq, :]
        vc[seq + 64:seq + 64 + slots, :] = sc[S_V][seq:rows, :]
        tab[192:192 + slots, :] = sc[S_K][seq:rows, :]
        halves = head_masks()
        label = lax.broadcasted_iota(jnp.int32, (1, 256), 1)
        own_label = (label >= 12) & (label < 12 + 2 * radius + 1)

        def pair(p, carry):
            cols = pl.ds(pl.multiple_of(p * 128, 128), 128)
            qp = sc[S_Q][:, cols]
            kp = sc[S_K][0:seq, cols]
            rk = tab[:, cols]
            vp = vc[:, cols]
            dap = da[:, cols]
            q_t = qp.T
            da_t = dap.T
            dq, dk_t, dv_t = [], [], []
            for hh in range(2):
                h = p * 2 + hh
                dam = jnp.where(halves[hh], dap, jnp.zeros_like(dap))
                prob_low = sc[S_P][h]
                d_prob = mm_t(dam, vp)
                prob = [prob_low[:, 128 * c:128 * c + 128].astype(F32) for c in range(3)]
                d_prob = [d_prob[:, 128 * c:128 * c + 128] for c in range(3)]
                delta = jnp.sum(sum(a * b for a, b in zip(prob, d_prob)), axis=-1, keepdims=True)
                delta = delta / jnp.sum(sum(prob), axis=-1, keepdims=True)
                ds = jnp.concatenate([(a * (b - delta)).astype(BF16) for a, b in zip(prob, d_prob)], 1)
                ds1 = ds[:, 0:seq]
                rel = pltpu.roll(mm(ds1[0:seq], flip[...]).astype(BF16), 0, 1, stride=1, stride_axis=0)
                far = jnp.concatenate(
                    [
                        jnp.concatenate([rel[:, 0:128], rel[:, 128:256] + ds[0:seq, seq:]], 1),
                        jnp.concatenate([jnp.zeros((slots, 128), BF16), ds[seq:rows, seq:]], 1),
                    ],
                    0,
                )
                dq.append(mm(ds1, kp) + mm(far, rk))
                own = slice(64 * hh, 64 * hh + 64)
                dk_t.append(jnp.concatenate([mm(q_t[own], ds1), mm(q_t[own], far)], 1) * 0.125)
                dv_t.append(mm(da_t[own], prob_low).astype(BF16))
            fs[D_Q][:, cols] = (jnp.where(halves[0], dq[0], dq[1]) * 0.125).astype(BF16)
            dk_t = jnp.concatenate(dk_t, 0)
            dk_low = dk_t.astype(BF16)
            dv_t = jnp.concatenate(dv_t, 0)
            fs[D_K][0:seq, cols] = dk_low[:, 0:seq].T
            fs[D_K][seq:rows, cols] = dk_low[:, seq + 128:].T[64:64 + slots]
            fs[D_V][0:seq, cols] = dv_t[:, 0:seq].T
            fs[D_V][seq:rows, cols] = dv_t[:, seq:].T[64:64 + slots]
            tab_s[cols, :] = jnp.where(own_label, dk_t[:, seq:], 0.0)
            return carry

        lax.fori_loop(0, H // 2, pair, 0, unroll=2)
        save(D_Q)
        save(D_K)
        save(D_V)
        small[64:65, :] = jnp.sum(fs[D_Q][...].astype(F32), axis=0, keepdims=True)
        small[65:66, :] = jnp.sum(fs[D_V][...].astype(F32), axis=0, keepdims=True)
        for name in (W_QUERY, W_KEY, W_VALUE, S_TAB):
            loads[name].wait()
        d_rows = (
            dx[...]
            + mm_t(fs[D_Q][...], w[W_QUERY][...])
            + mm_t(fs[D_K][...], w[W_KEY][...])
            + mm_t(fs[D_V][...], w[W_VALUE][...])
        )
        dx_low[...] = d_rows.astype(BF16)
        outs.append(cp.start(dx_low, d_send))
        dx[...] = d_rows
        outs.append(cp.start(dx.at[0:seq], rows_of(long_back, item, seq)))
        outs.append(cp.start(dx.at[seq:rows], rows_of(glob_back, item, slots)))
        tab_s[:, 128:] += small[...].T + small_t[...]
        outs.append(cp.start(tab_s, tab_out.at[item]))
        for copy in outs:
            copy.wait()


def run_attention_back(step_at, counts, d_first, small, weights, state, made, seq, slots, radius):
    rows, width = d_first.shape
    named, kept = dict(zip(WEIGHTS + (BACK_TABLE,), weights)), dict(zip(STATE, state))
    items = kept[S_Q].shape[0]
    low = jax.ShapeDtypeStruct((items, rows, width), BF16)
    out_shape = [low, low, low, jax.ShapeDtypeStruct((items, width, 256), F32),
                 jax.ShapeDtypeStruct((items * seq, width), F32), jax.ShapeDtypeStruct((items * slots, width), F32),
                 jax.ShapeDtypeStruct((rows, width), BF16)]
    operands = [counts, d_first, small] + [named[n] for n in ATTENTION_WEIGHTS] + [kept[n] for n in ATTENTION_USED]
    aliases = {}
    if made is not None:
        aliases = {len(operands) + n: n for n in range(6)}
        operands += list(made)
    scratch = [vm((256, width)) if n == BACK_TABLE else vm(named[n].shape) for n in ATTENTION_WEIGHTS]
    scratch += [vm(kept[n].shape[1:], kept[n].dtype) for n in ATTENTION_USED]
    scratch += [vm((rows, width))] * 3
    scratch += [vm((rows, width)), vm((rows, width), F32), vm((rows, width)), vm((width, 256), F32), vm((128, width), F32),
                vm((width, 128), F32), vm((seq, seq)), vm((seq + 128, width)), pltpu.SemaphoreType.DMA((32,))]
    result = pl.pallas_call(
        functools.partial(attention_back_kernel, (seq, slots, radius, made is None, step_at)),
        out_shape=out_shape,
        in_specs=[SMEM] + [ANY] * (len(operands) - 1),
        out_specs=[ANY] * len(out_shape),
        scratch_shapes=scratch,
        input_output_aliases=aliases,
        compiler_params=pltpu.CompilerParams(vmem_limit_bytes=60 << 20),
        cost_estimate=pl.CostEstimate(flops=15 * 10**9, bytes_accessed=20 * 10**6, transcendentals=0),
        name="attention_back",
    )(*operands)
    return result[:6], result[6]


TILE = 16
MESH_ID = pl.DeviceIdType.MESH
NZ, NY, NX = 4, 2, 2
LOADED = (S_X, S_ATT, D_BRANCH, D_Q, D_K, D_V)
CHUNKS = ((1, 0), (0, 1)) * 6 + ((1, 0),)
ENTER = (0, 0, 1, 3, 4, 5, 6, 7, 8, 9, 10, 11, 12)
PIECES = 4
SPACING = 2
FFN_ORDER = (0, 3, 1, 2)
STAGES = 6
PER_CHUNK = 7
PER_FFN = 4


def reduce_kernel(cfg, *refs):
    pl.when(lax.axis_index("section") == cfg[3])(lambda: reduce_turn(cfg, *refs))


def reduce_turn(cfg, *refs):
    rows, width, hidden, turn = cfg
    wide, narrow = hidden // SHARDS, width // SHARDS
    ins = dict(zip(LOADED, refs[:6]))
    n1_hbm, n1_near, df_hbm, df_a, df_b, up_hbm, bias_hbm, down_hbm, tab_hbm, red = refs[6:16]
    refs = refs[16:]
    buf = dict(zip(LOADED, refs[:6]))
    n1, df, w_up, b_up, w_down, tab, ga, gf, ay, ax, az, by, bz, bx, fx, fz, u, d_hid = refs[6:24]
    load_sems, send_sems, recv_sems = refs[24:]
    section = lax.axis_index("section")
    me = lax.axis_index("dp")
    x, y, z = lax.rem(me, NX), lax.rem(lax.div(me, NX), NY), lax.div(me, NX * NY)
    half = rows // 2

    def at(zz, yy, xx):
        return (section, (zz * NY + yy) * NX + xx)

    across_x, across_y = at(z, y, 1 - x), at(z, 1 - y, x)
    above, below = at(z + 1, y, x), at(z - 1, y, x)

    cp = Copies(load_sems)
    loads = {}
    for name in (D_BRANCH, S_ATT):
        loads[name] = [cp.start(ins[name], buf[name])]
    loads[S_N1] = [cp.start(n1_hbm, n1.at[0:rows]), cp.start(n1_near, n1.at[rows:])]
    loads[D_FFN] = [cp.start(df_hbm, df.at[0:rows])]
    loads[D_FFN] += [cp.start(df_a, df.at[rows:rows + half]), cp.start(df_b, df.at[rows + half:])]
    loads[B_UP] = [cp.start(bias_hbm, b_up)]
    for n in FFN_ORDER:
        units = pl.ds(pl.multiple_of((2 * n + y) * 2 * wide, 2 * wide), 2 * wide)
        loads[W_UP, n] = [cp.start(up_hbm.at[:, units], w_up.at[n]), cp.start(down_hbm.at[units], w_down.at[n])]
    for name in (S_X, D_Q, D_K, D_V):
        loads[name] = [cp.start(ins[name], buf[name])]
    loads[S_TAB] = [cp.start(tab_hbm, tab)]

    barrier = pltpu.get_barrier_semaphore()
    for other in (across_x, across_y):
        pl.semaphore_signal(barrier, inc=1, device_id=other, device_id_type=MESH_ID)

    @pl.when(z > 0)
    def _():
        pl.semaphore_signal(barrier, inc=1, device_id=below, device_id_type=MESH_ID)

    @pl.when(z < NZ - 1)
    def _():
        pl.semaphore_signal(barrier, inc=1, device_id=above, device_id_type=MESH_ID)

    def need(*names):
        for name in names:
            for copy in loads.pop(name, ()):
                copy.wait()

    def units_of(n):
        return pl.ds(pl.multiple_of((2 * n + y) * 2 * wide, 2 * wide), 2 * wide)

    def form_hidden(n):
        need(S_N1, D_FFN, B_UP, (W_UP, n))
        act, slope = gelu_parts(mm(n1[...], w_up[n]) + b_up[:, units_of(n)].astype(F32))
        u[...] = act.astype(BF16)
        d_hid[...] = (slope * mm_t(df[...], w_down[n])).astype(BF16)

    def form_down(n):
        part = mm_c(u[...], df[...]).astype(BF16)
        gf[n, 0, 0:wide, :] = part[0:wide]
        gf[n, 1, 0:wide, :] = part[wide:]

    def form_up(n):
        part = mm_c(d_hid[...], n1[...]).astype(BF16)
        gf[n, 0, wide:, :] = part[0:wide]
        gf[n, 1, wide:, :] = part[wide:]

    def form_narrow(left, right, at_row):
        need(left, right)

        def body(n, carry):
            cols = pl.ds(pl.multiple_of(n * 8 * narrow, 8 * narrow), 8 * narrow)
            part = mm_c(buf[left][:, cols], buf[right][...]).astype(BF16)
            for k in range(8):
                ga[2 * n + k // 4, (k // 2) % 2, k % 2, at_row:at_row + narrow, :] = part[k * narrow:(k + 1) * narrow]
            return carry

        lax.fori_loop(0, SHARDS // 8, body, 0)

    def form_table(at_row):
        need(S_TAB)

        def body(n, carry):
            for k in range(narrow // TILE):
                rows_k = pl.ds(pl.multiple_of(n * narrow + k * TILE, TILE), TILE)
                part = tab[0, rows_k, :] + tab[1, rows_k, :]
                shard = ga.at[lax.div(n, 4), lax.rem(lax.div(n, 2), 2), lax.rem(n, 2), at_row:at_row + TILE]
                shard[:, 256 * k:256 * k + 256] = part.astype(BF16)
            return carry

        lax.fori_loop(0, SHARDS, body, 0)

    first = [0]
    for counts in CHUNKS:
        first.append(first[-1] + sum(counts))

    def spans(chunk, route):
        counts = CHUNKS[chunk]
        start = first[chunk] + sum(counts[:route])
        own = sum(CHUNKS[n][route] for n in range(chunk))
        size = counts[route] * TILE
        return slice(start * TILE, start * TILE + size), slice(own * TILE, own * TILE + size), size

    pending = []

    def remote(src, dst, index, target):
        return pltpu.make_async_remote_copy(
            src_ref=src, dst_ref=dst, send_sem=send_sems.at[index], recv_sem=recv_sems.at[index],
            device_id=target, device_id_type=MESH_ID,
        )

    def send(src, dst, index, target):
        remote(src, dst, index, target).start()
        pending.append((None, lambda: remote(src, dst, index, target).wait_send()))

    def add(dst, src, lead):
        total = 1
        for n in lead:
            total *= n

        def body(n, carry):
            idx, rest = [], n
            for size in reversed(lead):
                idx.insert(0, lax.rem(rest, size))
                rest = lax.div(rest, size)
            d, s = dst(*idx), src(*idx)
            d[...] = (d[...].astype(F32) + s[...].astype(F32)).astype(BF16)
            return carry

        if total == 1:
            body(0, 0)
        else:
            lax.fori_loop(0, total, body, 0)

    def flow_z(stage, own, room, base, lead, shards=tuple(range(NZ))):
        def take(shard, slot, source):
            remote(own(shard), room(slot), base(slot), source).wait_recv()
            add(lambda *i: own(shard).at[i] if i else own(shard), lambda *i: room(slot).at[i] if i else room(slot), lead)

        def put(zz, shard, target):
            slot = NZ if (shard < zz and shard == zz - 1) else shard
            remote(own(shard), room(slot), base(slot), target).start()
            pending.append((zz, lambda: remote(own(shard), room(slot), base(slot), target).wait_send()))

        for zz in range(NZ):
            ups = [s for s in range(NZ - 1, zz - 1, -1) if s in shards]
            downs = [s for s in range(zz + 1) if s in shards]

            @pl.when(z == zz)
            def _():
                if stage == zz:
                    for shard in ups:
                        if zz > 0:
                            take(shard, shard, below)
                        if shard > zz:
                            put(zz, shard, above)
                if stage == NZ - 1 - zz:
                    for shard in downs:
                        if zz < NZ - 1:
                            take(shard, NZ if shard == zz else shard, above)
                        if shard < zz:
                            put(zz, shard, below)

    ffn_sems = len(CHUNKS) * PER_CHUNK

    def run(chunk, route, stage):
        rs, own, size = spans(chunk, route)
        if size == 0:
            return
        base = chunk * PER_CHUNK
        flow_base = lambda slot: base + 2 + slot
        out = slice(2 * wide + rs.start, 2 * wide + rs.stop)
        if stage == 0:
            room = ay if route == 0 else by
            send(ga.at[:, 1 - y, :, rs], room.at[:, :, own], base, across_y)
        if stage == 1:
            room = ay if route == 0 else by
            remote(ga.at[:, 1 - y, :, rs], room.at[:, :, own], base, across_y).wait_recv()
            add(lambda i, j: ga.at[i, y, j, rs], lambda i, j: room.at[i, j, own], (NZ, NX))
        if route == 0:
            if stage == 1:
                send(ga.at[:, y, 1 - x, rs], ax.at[:, own], base + 1, across_x)
            if stage == 2:
                remote(ga.at[:, y, 1 - x, rs], ax.at[:, own], base + 1, across_x).wait_recv()
                add(lambda i: ga.at[i, y, x, rs], lambda i: ax.at[i, own], (NZ,))
            if stage >= 2:
                flow_z(stage - 2, lambda s: ga.at[s, y, x, rs], lambda s: az.at[s, own], flow_base, ())
        else:
            if 1 <= stage <= 4:
                flow_z(stage - 1, lambda s: ga.at[s, y, :, rs], lambda s: bz.at[s, :, own], flow_base, (NX,))
            if stage == 4:
                send(ga.at[z, y, 1 - x, rs], bx.at[own], base + 1, across_x)
            if stage == 5:
                remote(ga.at[z, y, 1 - x, rs], bx.at[own], base + 1, across_x).wait_recv()
                add(lambda: ga.at[z, y, x, rs], lambda: bx.at[own], ())
        if stage == 5:
            red[out, :] = ga[z, y, x, rs, :].astype(F32)

    def run_ffn(n, piece, stage):
        base = ffn_sems + (n * PIECES + piece) * PER_FFN
        size = 2 * wide // PIECES
        rs = slice(piece * size, (piece + 1) * size)
        if stage == 0:
            send(gf.at[n, 1 - x, rs], fx.at[n, rs], base, across_x)
        if stage == 1:
            remote(gf.at[n, 1 - x, rs], fx.at[n, rs], base, across_x).wait_recv()
            add(lambda: gf.at[n, x, rs], lambda: fx.at[n, rs], ())
        if 1 <= stage <= 4:
            room = lambda slot: fz.at[1 if slot == NZ else 0, n, rs]
            flow_z(stage - 1, lambda s: gf.at[s, x, rs], room, lambda slot: base + (2 if slot == NZ else 1), (), (n,))
        if stage == 5:
            @pl.when(z == n)
            def _():
                red[rs, :] = gf[n, x, rs, :].astype(F32)

    def narrow_task(n):
        left, right = ((D_BRANCH, S_ATT), (D_Q, S_X), (D_K, S_X), (D_V, S_X))[n]
        return lambda: form_narrow(left, right, n * narrow)

    a, b, c, d = FFN_ORDER
    hidden_task = lambda n: lambda: form_hidden(n)
    down_task = lambda n: lambda: form_down(n)
    up_task = lambda n: lambda: form_up(n)
    tasks = [(up_task(a),), (narrow_task(1),), (hidden_task(b),), (down_task(b),), (narrow_task(2),), (up_task(b),),
             (hidden_task(c),), (down_task(c),), (narrow_task(3),), (up_task(c),),
             (hidden_task(d), lambda: form_table(4 * narrow)), (down_task(d),), (up_task(d),)]
    narrow_task(0)()

    @pl.when((z == 0) | (z == NZ - 1))
    def _():
        pl.semaphore_wait(barrier, 3)

    @pl.when((z > 0) & (z < NZ - 1))
    def _():
        pl.semaphore_wait(barrier, 4)

    starts = [(n, None, slot) for n, slot in enumerate(ENTER)]
    starts += [(FFN_ORDER[k // PIECES], k % PIECES, k) for k in range(NZ * PIECES)]
    last = max(slot for _, _, slot in starts) + SPACING * (STAGES - 1)
    for slot in range(last + 1):
        for stage in range(STAGES):
            for n, piece, enter in starts:
                if enter + stage * SPACING == slot:
                    if slot == 0 and piece == 0:
                        form_hidden(a)
                        form_down(a)
                    if piece is None:
                        run(n, 0, stage)
                        run(n, 1, stage)
                    else:
                        run_ffn(n, piece, stage)
            if stage == 0:
                for task in tasks.pop(0) if tasks else ():
                    task()
    for zz, wait in pending:
        if zz is None:
            wait()
        else:
            pl.when(z == zz)(wait)


def reduce_grads(turn, parts, near, weights, tab):
    rows, width = parts[S_X].shape
    hidden = weights[W_UP].shape[1]
    wide, narrow = hidden // SHARDS, width // SHARDS
    share = 4 * narrow + TILE
    t = [sum(c[n] for c in CHUNKS) * TILE for n in range(2)]
    assert sum(t) == share
    n_sem = len(CHUNKS) * PER_CHUNK + NZ * PIECES * PER_FFN
    scratch = [vm(parts[n].shape) for n in LOADED]
    scratch += [
        vm((2 * rows, width)), vm((2 * rows, width)), vm((NZ, width, 2 * wide)), vm((1, hidden)), vm((NZ, 2 * wide, width)),
        vm(tab.shape, F32),
        vm((NZ, NY, NX, share, width)), vm((NZ, NX, 2 * wide, width)),
        vm((NZ, NX, t[0], width)), vm((NZ, t[0], width)), vm((NZ + 1, t[0], width)),
        vm((NZ, NX, t[1], width)), vm((NZ + 1, NX, t[1], width)), vm((t[1], width)),
        vm((NZ, 2 * wide, width)), vm((2, NZ, 2 * wide, width)), vm((2 * rows, 2 * wide)), vm((2 * rows, 2 * wide)),
        pltpu.SemaphoreType.DMA((32,)), pltpu.SemaphoreType.DMA((n_sem,)), pltpu.SemaphoreType.DMA((n_sem,)),
    ]
    operands = [parts[n] for n in LOADED]
    operands += [parts[S_N1], near[0], parts[D_FFN]] + list(near[1:])
    operands += [weights[W_UP], weights[B_UP], weights[W_DOWN], tab]
    return pl.pallas_call(
        functools.partial(reduce_kernel, (rows, width, hidden, turn)),
        cost_estimate=pl.CostEstimate(flops=60 * 10**9, bytes_accessed=20 * 10**6, transcendentals=0),
        out_shape=jax.ShapeDtypeStruct((2 * wide + share, width), F32),
        in_specs=[ANY] * len(operands),
        out_specs=pl.BlockSpec(memory_space=pltpu.VMEM),
        scratch_shapes=scratch,
        compiler_params=pltpu.CompilerParams(collective_id=turn, has_side_effects=True, vmem_limit_bytes=60 << 20),
        name="reduce_grads",
    )(*operands)


def finish_kernel(labels, red_a, red_b, *refs):
    w_out, w_query, w_key, w_value, w_up, w_down, table = refs[:7]
    vectors, bias, red, turned, sem = refs[7:15], refs[15], refs[16], refs[17], refs[18]
    wide, narrow = w_up.shape[0], w_out.shape[0]
    cp = Copies(sem)
    cp.choose(lax.axis_index("section") == 0, red_a, red_b, red).wait()
    outs = [cp.start(red.at[0:wide], w_down), cp.start(red.at[wide:2 * wide], w_up)]
    for n, ref in enumerate((w_out, w_query, w_key, w_value)):
        at = 2 * wide + n * narrow
        outs.append(cp.start(red.at[at:at + narrow], ref))
    at = 2 * wide + 4 * narrow
    packed = jnp.concatenate([red[at:at + TILE, 256 * k:256 * k + 256] for k in range(narrow // TILE)], 0)
    turned[...] = packed.T
    row = lax.broadcasted_iota(jnp.int32, (256, labels), 0)
    col = lax.broadcasted_iota(jnp.int32, (256, labels), 1)
    back = jnp.where(row + col == labels + 11, 1.0, 0.0)
    table[...] = jnp.dot(packed, back, precision=lax.Precision.HIGHEST, preferred_element_type=F32)
    for n, ref in enumerate(vectors):
        ref[...] = turned[192 + n:193 + n, :]
    for k in range(wide // narrow):
        bias[:, k * narrow:(k + 1) * narrow] = turned[200 + k:201 + k, :]
    for copy in outs:
        copy.wait()


def finish(red_a, red_b, labels, hidden):
    width = red_a.shape[1]
    wide, narrow = hidden // SHARDS, width // SHARDS
    out = lambda *s: jax.ShapeDtypeStruct(s, F32)
    shapes = [out(narrow, width)] * 4 + [out(wide, width), out(wide, width), out(narrow, labels)]
    shapes += [out(1, narrow)] * 8 + [out(1, wide)]
    result = pl.pallas_call(
        functools.partial(finish_kernel, labels),
        out_shape=shapes,
        in_specs=[ANY, ANY],
        out_specs=[ANY] * 6 + [pl.BlockSpec(memory_space=pltpu.VMEM)] * (len(shapes) - 6),
        scratch_shapes=[vm(red_a.shape, F32), vm((256, narrow), F32), pltpu.SemaphoreType.DMA((8,))],
        compiler_params=pltpu.CompilerParams(vmem_limit_bytes=40 << 20),
        name="finish",
    )(red_a, red_b)
    mats = [t.T for t in result[:5]] + [result[5], result[6].T]
    return [t[None] for t in mats] + list(result[7:])


def sums_elsewhere(parts, weights, tab):
    def scatter(value, dim):
        return lax.psum_scatter(value, "dp", scatter_dimension=dim, tiled=True)

    cut = [scatter(mm_c(parts[a], parts[b]), 1)
           for a, b in ((S_ATT, D_BRANCH), (S_X, D_Q), (S_X, D_K), (S_X, D_V))]
    act, slope = gelu_parts(mm(parts[S_N1], weights[W_UP]) + weights[B_UP].astype(F32))
    d_hid = (slope * mm_t(parts[D_FFN], weights[W_DOWN])).astype(BF16)
    w_up = scatter(mm_c(parts[S_N1], d_hid), 1)
    w_down = scatter(mm_c(act.astype(BF16), parts[D_FFN]), 0)
    b_up = scatter(jnp.sum(d_hid.astype(F32), axis=0), 0)
    return cut, w_up, w_down, scatter(tab[0] + tab[1], 0), b_up


def per_device(
    long_input, global_input, counts, w_query, b_query, w_key, w_value, b_value, w_out, b_out, rel_table,
    norm1_gain, norm1_bias, w_up, b_up, w_down, b_down, norm2_gain, norm2_bias, long_cot, global_cot,
):
    items = counts.shape[0]
    seq, slots, width = long_input.shape[0] // items, global_input.shape[0] // items, long_input.shape[1]
    rows, hidden = seq + slots, w_up.shape[2]
    labels = rel_table.shape[1]
    radius = (labels - 1) // 2
    weights = [w_query[0], w_key[0], w_value[0], w_out[0], w_up[0], w_down[0],
               jnp.pad(rel_table[0], ((12, 192 - 12 - labels), (0, 0))),
               b_query, b_value, b_out, norm1_gain, norm1_bias, b_up, b_down, norm2_gain, norm2_bias,
               jnp.pad(rel_table[0, ::-1], ((12, 192 - 12 - labels), (0, 0)))]

    recv = long_input
    state = outs = None
    for step in range(items + 1):
        state, outs, sent = run_forward(
            step, counts, long_input, global_input, recv, weights, state, outs, seq, slots, radius)
        if step < items:
            recv = lax.ppermute(sent, "section", [(0, 1)])
    kept = dict(zip(STATE, state))
    shards = lax.axis_size("dp")
    paired = shards == SHARDS
    near = []
    if paired:
        near = [lax.ppermute(kept[S_N1], "dp", [(n, n ^ NX) for n in range(shards)]).reshape(items * rows, width)]
    named = dict(zip(WEIGHTS, weights))

    def parts_of():
        parts = {n: kept[n] for n in (S_X, S_ATT, S_N1)}
        parts.update(zip((D_FFN, D_BRANCH, D_Q, D_K, D_V), list(low) + list(made[:3])))
        return {n: t.reshape(items * rows, t.shape[2]) for n, t in parts.items()}

    low = made = None
    summed, awaited = [], near[0:1]
    for step in range(items + 1):
        low, d_ffn, d_first, small = run_hidden_back(
            step, counts, long_cot, global_cot, recv, weights, state, low, awaited if step else [], seq, slots)
        if paired:
            pairs = [(e * shards + n, e * shards + (n ^ NX)) for e in range(2) for n in range(shards)
                     if 0 <= step - (1 - e) < items]
            near.append(lax.ppermute(d_ffn, ("section", "dp"), pairs))
        made, sent = run_attention_back(
            step, counts, d_first, small, weights, state, made, seq, slots, radius)
        if step < items:
            if paired:
                sent, near[-1] = lax.optimization_barrier((sent, near[-1]))
            recv = lax.ppermute(sent, "section", [(1, 0)])
        if paired and step >= items - 1:
            turn = items - step
            awaited = [reduce_grads(turn, parts_of(), [near[0]] + near[step:step + 2], named, made[3])]
            summed += awaited
    long_back, glob_back = made[4:6]
    if paired:
        final = finish(summed[1], summed[0], labels, hidden)
        g_out, g_query, g_key, g_value, g_up, g_down, g_table = final[:7]
        g_bq, g_bv, g_bo, g_g1, g_s1, g_bd, g_g2, g_s2, g_b_up = final[7:]
    else:
        cut, g_up, g_down, table, g_b_up = [jax.tree.map(lambda t: t[None], t)
                                            for t in sums_elsewhere(parts_of(), named, made[3])]
        g_out, g_query, g_key, g_value = cut
        g_bq, g_bv, g_bo, g_g1, g_s1, g_bd, g_g2, g_s2 = [table[:, :, 192 + n] for n in range(8)]
        g_table = table[0, :, 12:12 + labels][:, ::-1].T[None]
    grads = (g_query, g_bq, g_key, g_value, g_bv, g_out, g_bo, g_table, g_g1, g_s1, g_up, g_b_up, g_down, g_bd, g_g2, g_s2)
    return tuple(t[None] for t in (outs[0], outs[1], long_back, glob_back)) + grads


def solution(mesh):
    part = P("section", "dp", None)
    vector = P("section", "dp")
    columns = P("section", None, "dp")
    matrix = P("section", None, None)
    row = P("section", None)
    items = P("dp", None)
    in_specs = (items, items, P("dp"), matrix, row, matrix, matrix, row, matrix, row, matrix, row, row,
                matrix, row, matrix, row, row, row, items, items)
    out_specs = (part, part, part, part, columns, vector, columns, columns, vector, columns, vector, columns,
                 vector, vector, columns, vector, part, vector, vector, vector)
    return jax.shard_map(per_device, mesh=mesh, in_specs=in_specs, out_specs=out_specs, check_vma=False)
```

```python
import functools
import math

import jax
import jax.numpy as jnp
from jax import lax
from jax.experimental import pallas as pl
from jax.experimental.pallas import tpu as pltpu
from jax.sharding import PartitionSpec as P

H = 12
F32 = jnp.float32
BF16 = jnp.bfloat16
ANY = pl.BlockSpec(memory_space=pl.ANY)
SMEM = pl.BlockSpec(memory_space=pltpu.SMEM)
NEG = -1e30
SHARDS = 16
BIAS_LANE = 72
(
    W_QUERY, W_KEY, W_VALUE, W_OUT, W_UP, W_DOWN, TABLE, B_QUERY, B_VALUE, B_OUT, NORM1_GAIN, NORM1_BIAS, B_UP, B_DOWN, NORM2_GAIN, NORM2_BIAS,
    D_FFN, D_HIDDEN, D_BRANCH, D_Q, D_K, D_V, S_X, S_Q, S_K, S_V, S_ATT, S_N1, S_XH1, S_XH2, S_U, S_GP, S_P, S_RS1, S_RS2, S_TAB,
) = range(36)


def mm(a, b):
    return jnp.dot(a, b, preferred_element_type=F32)


def mm_t(a, b):
    return lax.dot_general(a, b, (((1,), (1,)), ((), ())), preferred_element_type=F32)


def mm_c(a, b):
    return lax.dot_general(a, b, (((0,), (0,)), ((), ())), preferred_element_type=F32)


class Copies:
    def __init__(self, sems):
        self.sems = sems
        self.used = 0

    def make(self, src, dst):
        copy = pltpu.make_async_copy(src, dst, self.sems.at[self.used])
        self.used += 1
        return copy

    def start(self, src, dst):
        copy = self.make(src, dst)
        copy.start()
        return copy

    def choose(self, first, src_a, src_b, dst):
        a = pltpu.make_async_copy(src_a, dst, self.sems.at[self.used])
        b = pltpu.make_async_copy(src_b, dst, self.sems.at[self.used])
        self.used += 1
        pl.when(first)(a.start)
        pl.when(jnp.logical_not(first))(b.start)
        return a


def normalize(rows):
    center = rows - jnp.mean(rows, axis=-1, keepdims=True)
    spread = jnp.mean(center * center, axis=-1, keepdims=True)
    rstd = lax.rsqrt(spread + 1e-05)
    return center * rstd, rstd


GELU_C = math.sqrt(2.0 / math.pi)


def gelu_parts(z):
    zz = z * z
    t = jnp.tanh(z * (GELU_C + (GELU_C * 0.044715) * zz))
    half = 0.5 + 0.5 * t
    slope = half + (0.5 * z) * (1.0 - t * t) * (GELU_C + (3.0 * GELU_C * 0.044715) * zz)
    return z * half, slope


WEIGHTS = (
    W_QUERY, W_KEY, W_VALUE, W_OUT, W_UP, W_DOWN, TABLE,
    B_QUERY, B_VALUE, B_OUT, NORM1_GAIN, NORM1_BIAS, B_UP, B_DOWN, NORM2_GAIN, NORM2_BIAS,
)
STATE = (S_X, S_Q, S_K, S_V, S_ATT, S_N1, S_XH1, S_XH2, S_GP, S_P, S_RS1, S_RS2)


def state_shapes(items, rows, width, hidden, keys):
    low = lambda *s: jax.ShapeDtypeStruct((items,) + s, BF16)
    shapes = {name: low(rows, width) for name in (S_X, S_Q, S_K, S_V, S_ATT, S_N1, S_XH1, S_XH2)}
    shapes[S_GP] = low(rows, hidden)
    shapes[S_P] = low(H, rows, keys)
    shapes[S_RS1] = shapes[S_RS2] = jax.ShapeDtypeStruct((items, rows, 128), F32)
    return [shapes[name] for name in STATE]


def head_masks():
    lane = lax.broadcasted_iota(jnp.int32, (1, 128), 1)
    return [lane < 64, lane >= 64]


def turn_of(counts, step_at, forward):
    section = lax.axis_index("section")
    first = (section == 0) if forward else (section == 1)
    turn = jnp.where(first, step_at, step_at - 1)
    item = jnp.clip(turn, 0, counts.shape[0] - 1)
    return item, counts[item], turn == item, first


def fwd_kernel(cfg, *refs):
    seq, slots, radius, first_call, step_at = cfg
    rows = seq + slots
    counts, x_long, x_glob, recv = refs[:4]
    w_hbm = dict(zip(WEIGHTS, refs[4:20]))
    refs = refs[20:]
    if not first_call:
        refs = refs[len(STATE) + 2:]
    st = dict(zip(STATE, refs[:len(STATE)]))
    long_out, glob_out, y_send = refs[len(STATE):len(STATE) + 3]
    refs = refs[len(STATE) + 3:]
    w = dict(zip(WEIGHTS, refs[:16]))
    sc = dict(zip(STATE, refs[16:16 + len(STATE)]))
    y_v, vc, bandm, ownm, sems = refs[16 + len(STATE):]
    item, count, active, fresh = turn_of(counts, step_at, True)

    @pl.when(active)
    def _():
        cp = Copies(sems)
        long_rows = pl.ds(pl.multiple_of(item * seq, seq), seq)
        glob_rows = pl.ds(pl.multiple_of(item * slots, slots), slots)
        c_x = cp.choose(fresh, x_long.at[long_rows], recv.at[0:seq], sc[S_X].at[0:seq])
        c_g = cp.choose(fresh, x_glob.at[glob_rows], recv.at[seq:rows], sc[S_X].at[seq:rows])
        loads = {}
        for name in (W_QUERY, B_QUERY, W_KEY, W_VALUE, B_VALUE, TABLE, W_OUT, B_OUT, NORM1_GAIN,
                     NORM1_BIAS, W_UP, B_UP, W_DOWN, B_DOWN, NORM2_GAIN, NORM2_BIAS):
            dst = w[name].at[0:w_hbm[name].shape[0]] if name == TABLE else w[name]
            loads[name] = cp.start(w_hbm[name], dst)
        outs = []

        def save(name):
            outs.append(cp.start(sc[name], st[name].at[item]))

        def vec(name):
            loads[name].wait()
            return w[name][...].astype(F32)

        row = lax.broadcasted_iota(jnp.int32, (seq, seq), 0)
        col = lax.broadcasted_iota(jnp.int32, (seq, seq), 1)
        bandm[...] = jnp.where(jnp.abs(col - row) <= radius, 0.0, NEG)
        key = lax.broadcasted_iota(jnp.int32, (slots, seq), 1)
        slot = lax.broadcasted_iota(jnp.int32, (slots, seq), 0)
        ownm[...] = jnp.where(lax.div(key * count, jnp.int32(seq)) == slot, 0.0, NEG)
        lane = lax.broadcasted_iota(jnp.int32, (1, 128), 1)
        globm = jnp.where((lane >= 64) & (lane < 64 + count), 0.0, NEG)
        vc[seq:, :] = jnp.zeros((128, vc.shape[1]), BF16)
        tab = w[TABLE]
        tab[192:, :] = jnp.zeros((tab.shape[0] - 192, tab.shape[1]), BF16)

        c_x.wait()
        c_g.wait()
        x = sc[S_X][...]
        save(S_X)
        loads[W_QUERY].wait()
        sc[S_Q][...] = (mm(x, w[W_QUERY][...]) + vec(B_QUERY)).astype(BF16)
        save(S_Q)
        loads[W_KEY].wait()
        k = mm(x, w[W_KEY][...]).astype(BF16)
        sc[S_K][...] = k
        save(S_K)
        loads[W_VALUE].wait()
        v = (mm(x, w[W_VALUE][...]) + vec(B_VALUE)).astype(BF16)
        sc[S_V][...] = v
        save(S_V)
        vc[0:seq, :] = v[0:seq]
        vc[seq + 64:seq + 64 + slots, :] = v[seq:rows]
        loads[TABLE].wait()
        tab[192:192 + slots, :] = k[seq:rows]
        halves = head_masks()

        ones_cols = jnp.ones((vc.shape[0], 128), BF16)
        live, done = {}, {}

        def scores(h):
            cols = slice(128 * (h // 2), 128 * (h // 2) + 128)
            qp = sc[S_Q][:, cols]
            qm = jnp.where(halves[h % 2], qp, jnp.zeros_like(qp)) * jnp.bfloat16(0.125)
            s1 = mm_t(qm, sc[S_K][0:seq, cols])
            s2 = mm_t(qm, tab[:, cols])
            band = pltpu.roll(s2[0:seq], (2 * seq - radius - 12) % seq, 1, stride=1, stride_axis=0)
            live[h] = (s1[0:seq] + band + bandm[...], s2[0:seq, 128:256] + globm,
                       s1[seq:rows] + ownm[...], s2[seq:rows, 128:256] + globm)

        def weigh(h):
            ll, lg, gl, gg = live.pop(h)
            parts = []
            for sl, sg in ((ll, lg), (gl, gg)):
                top = jnp.max(jnp.maximum(jnp.maximum(sl[:, 0:128], sl[:, 128:256]), sg), axis=-1, keepdims=True)
                parts.append(jnp.concatenate([jnp.exp(sl - top), jnp.exp(sg - top)], 1))
            live[h] = jnp.concatenate(parts, 0)

        def gather(h):
            cols = slice(128 * (h // 2), 128 * (h // 2) + 128)
            e = live.pop(h)
            got = mm(e.astype(BF16), jnp.concatenate([vc[:, cols], ones_cols], 1))
            inv = 1.0 / got[:, 128:]
            done[h] = got[:, 0:128] * inv
            for c in range(3):
                sc[S_P][h, :, 128 * c:128 * c + 128] = (e[:, 128 * c:128 * c + 128] * inv).astype(BF16)
            if h % 2:
                sc[S_ATT][:, cols] = jnp.where(halves[0], done.pop(h - 1), done.pop(h)).astype(BF16)

        for turn in range(H + 2):
            if turn < H:
                scores(turn)
            if 0 <= turn - 1 < H:
                weigh(turn - 1)
            if 0 <= turn - 2 < H:
                gather(turn - 2)
        save(S_P)
        save(S_ATT)
        loads[W_OUT].wait()
        r1 = x.astype(F32) + mm(sc[S_ATT][...], w[W_OUT][...]) + vec(B_OUT)
        xh1, rstd1 = normalize(r1)
        sc[S_XH1][...] = xh1.astype(BF16)
        save(S_XH1)
        sc[S_RS1][...] = jnp.broadcast_to(rstd1, (rows, 128))
        save(S_RS1)
        n1 = xh1 * vec(NORM1_GAIN) + vec(NORM1_BIAS)
        n1_low = n1.astype(BF16)
        sc[S_N1][...] = n1_low
        save(S_N1)
        hidden = w[W_UP].shape[1]
        step = 768
        loads[W_UP].wait()
        b_up = vec(B_UP)
        acc = n1 + vec(B_DOWN)
        for c in range(hidden // step):
            z = mm(n1_low, w[W_UP][:, c * step:(c + 1) * step]) + b_up[:, c * step:(c + 1) * step]
            act, slope = gelu_parts(z)
            act = act.astype(BF16)
            cols = slice(c * step, (c + 1) * step)
            sc[S_GP][:, cols] = slope.astype(BF16)
            outs.append(cp.start(sc[S_GP].at[:, cols], st[S_GP].at[item, :, cols]))
            if c == 0:
                loads[W_DOWN].wait()
            acc = acc + mm(act, w[W_DOWN][c * step:(c + 1) * step, :])
        xh2, rstd2 = normalize(acc)
        sc[S_XH2][...] = xh2.astype(BF16)
        save(S_XH2)
        sc[S_RS2][...] = jnp.broadcast_to(rstd2, (rows, 128))
        save(S_RS2)
        y = xh2 * vec(NORM2_GAIN) + vec(NORM2_BIAS)
        pos = lax.broadcasted_iota(jnp.int32, (rows, 1), 0)
        y = jnp.where(pos < seq + count, y, 0.0)
        y_v[...] = y.astype(BF16)
        outs.append(cp.start(y_v, y_send))
        outs.append(cp.start(y_v.at[0:seq], long_out.at[long_rows]))
        outs.append(cp.start(y_v.at[seq:rows], glob_out.at[glob_rows]))
        for copy in outs:
            copy.wait()


def vm(shape, dtype=BF16):
    return pltpu.VMEM(shape, dtype)


def run_forward(step_at, counts, x_long, x_glob, recv, weights, state, outs, seq, slots, radius):
    rows, width = seq + slots, x_long.shape[1]
    hidden = weights[4].shape[1]
    items = x_long.shape[0] // seq
    keys = seq + 128
    shapes = state_shapes(items, rows, width, hidden, keys)
    out_shape = shapes + [
        jax.ShapeDtypeStruct(x_long.shape, BF16),
        jax.ShapeDtypeStruct(x_glob.shape, BF16),
        jax.ShapeDtypeStruct((rows, width), BF16),
    ]
    first = state is None
    operands = [counts, x_long, x_glob, recv] + list(weights)
    aliases = {}
    if not first:
        base = len(operands)
        operands += list(state) + list(outs)
        aliases = {base + n: n for n in range(len(state) + 2)}
    scratch = []
    for name, t in zip(WEIGHTS, weights):
        scratch.append(vm((256, width)) if name == TABLE else vm(t.shape))
    scratch += [vm(s.shape[1:], s.dtype) for s in shapes]
    scratch += [vm((rows, width)), vm((keys, width)), vm((seq, seq), F32), vm((slots, seq), F32),
                pltpu.SemaphoreType.DMA((48,))]
    result = pl.pallas_call(
        functools.partial(fwd_kernel, (seq, slots, radius, first, step_at)),
        out_shape=out_shape,
        in_specs=[SMEM] + [ANY] * (len(operands) - 1),
        out_specs=[ANY] * len(out_shape),
        scratch_shapes=scratch,
        input_output_aliases=aliases,
        compiler_params=pltpu.CompilerParams(vmem_limit_bytes=60 << 20),
        cost_estimate=pl.CostEstimate(flops=20 * 10**9, bytes_accessed=20 * 10**6, transcendentals=0),
        name="layer_forward",
    )(*operands)
    n = len(STATE)
    return result[:n], result[n:n + 2], result[n + 2]


HIDDEN_USED = (S_XH1, S_XH2, S_GP, S_RS1, S_RS2)
HIDDEN_WEIGHTS = (W_UP, W_DOWN, NORM1_GAIN, NORM2_GAIN)
ATTENTION_USED = (S_Q, S_K, S_V, S_P)
ATTENTION_WEIGHTS = (W_QUERY, W_KEY, W_VALUE, W_OUT, TABLE)


def rows_of(ref, item, size):
    return ref.at[pl.ds(pl.multiple_of(item * size, size), size)]


def hidden_back_kernel(cfg, *refs):
    seq, slots, first_call, step_at, unread = cfg
    rows = seq + slots
    counts, c_long, c_glob, recv = refs[:4]
    w_hbm = dict(zip(HIDDEN_WEIGHTS, refs[4:8]))
    st = dict(zip(HIDDEN_USED, refs[8:13]))
    refs = refs[13:]
    if not first_call:
        refs = refs[2:]
    refs = refs[unread:]
    ffn_out, branch_out, ffn_now, small_out = refs[:4]
    refs = refs[4:]
    w = dict(zip(HIDDEN_WEIGHTS, refs[:4]))
    sc = dict(zip(HIDDEN_USED, refs[4:9]))
    dy, d_ffn_s, d_branch_s, small, small_t, sems = refs[9:]
    item, count, active, fresh = turn_of(counts, step_at, False)

    @pl.when(active)
    def _():
        cp = Copies(sems)
        c_y = cp.choose(fresh, rows_of(c_long, item, seq), recv.at[0:seq], dy.at[0:seq])
        c_g = cp.choose(fresh, rows_of(c_glob, item, slots), recv.at[seq:rows], dy.at[seq:rows])
        hidden, width = w[W_DOWN].shape
        step = width
        parts = [slice(c * step, (c + 1) * step) for c in range(hidden // step)]
        loads = {}
        for name in (S_RS2, S_XH2):
            loads[name] = cp.start(st[name].at[item], sc[name])
        loads[NORM2_GAIN] = cp.start(w_hbm[NORM2_GAIN], w[NORM2_GAIN])
        loads[S_GP] = cp.start(st[S_GP].at[item], sc[S_GP])
        for c, sl in enumerate(parts):
            loads[W_DOWN, c] = cp.start(w_hbm[W_DOWN].at[sl], w[W_DOWN].at[sl])
            loads[W_UP, c] = cp.start(w_hbm[W_UP].at[:, sl], w[W_UP].at[:, sl])
        for name in (S_RS1, S_XH1):
            loads[name] = cp.start(st[name].at[item], sc[name])
        loads[NORM1_GAIN] = cp.start(w_hbm[NORM1_GAIN], w[NORM1_GAIN])
        small[...] = jnp.zeros_like(small)
        pos = lax.broadcasted_iota(jnp.int32, (rows, 1), 0)
        lane = lax.broadcasted_iota(jnp.int32, (1, 128), 1)
        ones = jnp.ones((rows, 128), BF16)

        def norm_back(grad, xh, rstd, gain, at):
            small[at:at + 1, :] = jnp.sum(grad * xh, axis=0, keepdims=True)
            small[at + 1:at + 2, :] = jnp.sum(grad, axis=0, keepdims=True)
            dxh = grad * gain
            return rstd * (
                dxh - jnp.mean(dxh, axis=-1, keepdims=True) - xh * jnp.mean(dxh * xh, axis=-1, keepdims=True)
            )

        c_y.wait()
        c_g.wait()
        grad = jnp.where(pos < seq + count, dy[...].astype(F32), 0.0)
        for name in (NORM2_GAIN, S_XH2, S_RS2):
            loads[name].wait()
        d_second = norm_back(
            grad, sc[S_XH2][...].astype(F32), sc[S_RS2][:, 0:1], w[NORM2_GAIN][...].astype(F32), 70
        )
        d_ffn = d_second.astype(BF16)
        d_ffn_s[...] = d_ffn
        outs = [cp.start(d_ffn_s, ffn_out.at[item]), cp.start(d_ffn_s, ffn_now)]
        small[69:70, :] = jnp.sum(d_ffn.astype(F32), axis=0, keepdims=True)
        loads[S_GP].wait()
        d_normed = d_second
        wide, narrow = hidden // SHARDS, width // SHARDS
        for c, sl in enumerate(parts):
            loads[W_DOWN, c].wait()
            d_hid = (sc[S_GP][:, sl].astype(F32) * mm_t(d_ffn, w[W_DOWN][sl, :])).astype(BF16)
            loads[W_UP, c].wait()
            d_normed = d_normed + mm_t(d_hid, w[W_UP][:, sl])
            sums = mm_c(d_hid, ones)
            for shard in range(step // wide):
                block = jnp.zeros((narrow, 128), F32)
                for k in range(wide // narrow):
                    at = shard * wide + k * narrow
                    block = jnp.where(lane == BIAS_LANE + k, sums[at:at + narrow], block)
                at = (c * (step // wide) + shard) * narrow
                small_t[at:at + narrow, :] = block
        for name in (NORM1_GAIN, S_XH1, S_RS1):
            loads[name].wait()
        d_first = norm_back(
            d_normed, sc[S_XH1][...].astype(F32), sc[S_RS1][:, 0:1], w[NORM1_GAIN][...].astype(F32), 67
        )
        d_branch = d_first.astype(BF16)
        d_branch_s[...] = d_branch
        outs.append(cp.start(d_branch_s, branch_out.at[item]))
        small[66:67, :] = jnp.sum(d_branch.astype(F32), axis=0, keepdims=True)
        small_t[...] += small[...].T
        outs.append(cp.start(small_t, small_out))
        for copy in outs:
            copy.wait()


def run_hidden_back(step_at, counts, c_long, c_glob, recv, weights, state, made, arrived, seq, slots):
    rows, width = seq + slots, c_long.shape[1]
    named, kept = dict(zip(WEIGHTS, weights)), dict(zip(STATE, state))
    items = c_long.shape[0] // seq
    low = jax.ShapeDtypeStruct((items, rows, width), BF16)
    out_shape = [low, low, jax.ShapeDtypeStruct((rows, width), BF16), jax.ShapeDtypeStruct((width, 128), F32)]
    operands = [counts, c_long, c_glob, recv] + [named[n] for n in HIDDEN_WEIGHTS] + [kept[n] for n in HIDDEN_USED]
    aliases = {}
    if made is not None:
        aliases = {len(operands): 0, len(operands) + 1: 1}
        operands += list(made)
    operands += list(arrived)
    scratch = [vm(named[n].shape) for n in HIDDEN_WEIGHTS]
    scratch += [vm(kept[n].shape[1:], kept[n].dtype) for n in HIDDEN_USED]
    scratch += [vm((rows, width)), vm((rows, width)), vm((rows, width)),
                vm((128, width), F32), vm((width, 128), F32), pltpu.SemaphoreType.DMA((32,))]
    result = pl.pallas_call(
        functools.partial(hidden_back_kernel, (seq, slots, made is None, step_at, len(arrived))),
        out_shape=out_shape,
        in_specs=[SMEM] + [ANY] * (len(operands) - 1),
        out_specs=[ANY] * len(out_shape),
        scratch_shapes=scratch,
        input_output_aliases=aliases,
        compiler_params=pltpu.CompilerParams(vmem_limit_bytes=60 << 20),
        cost_estimate=pl.CostEstimate(flops=9 * 10**9, bytes_accessed=20 * 10**6, transcendentals=0),
        name="hidden_back",
    )(*operands)
    return result[:2], result[2], result[3]


def attention_back_kernel(cfg, *refs):
    seq, slots, radius, first_call, step_at = cfg
    rows = seq + slots
    counts, branch_hbm, small_hbm = refs[:3]
    w_hbm = dict(zip(ATTENTION_WEIGHTS, refs[3:8]))
    st = dict(zip(ATTENTION_USED, refs[8:12]))
    refs = refs[12:]
    if not first_call:
        refs = refs[6:]
    fac = dict(zip((D_Q, D_K, D_V), refs[:3]))
    tab_out, long_back, glob_back, d_send = refs[3:7]
    refs = refs[7:]
    w = dict(zip(ATTENTION_WEIGHTS, refs[:5]))
    sc = dict(zip(ATTENTION_USED, refs[5:9]))
    fs = dict(zip((D_Q, D_K, D_V), refs[9:12]))
    d_branch, da, dx, dx_low, tab_s, small, small_t, flip, vc, sems = refs[12:]
    item, _, active, _ = turn_of(counts, step_at, False)

    @pl.when(active)
    def _():
        cp = Copies(sems)
        loads = {D_BRANCH: cp.start(branch_hbm.at[item], d_branch)}
        for name in (W_OUT, S_V, S_P, TABLE, S_K, S_Q):
            if name in w:
                dst = w[name].at[0:w_hbm[name].shape[0]] if name == TABLE else w[name]
                loads[name] = cp.start(w_hbm[name], dst)
            else:
                loads[name] = cp.start(st[name].at[item], sc[name])
        loads[S_TAB] = cp.start(small_hbm, small_t)
        for name in (W_QUERY, W_KEY, W_VALUE):
            loads[name] = cp.start(w_hbm[name], w[name])
        outs = []

        def save(name):
            outs.append(cp.start(fs[name], fac[name].at[item]))

        row = lax.broadcasted_iota(jnp.int32, (seq, seq), 0)
        col = lax.broadcasted_iota(jnp.int32, (seq, seq), 1)
        turn = (radius + 12) % seq
        flip[...] = jnp.where((row + col == turn) | (row + col == turn + seq), 1.0, 0.0).astype(BF16)
        vc[seq:, :] = jnp.zeros((128, vc.shape[1]), BF16)
        tab = w[TABLE]
        tab[192:, :] = jnp.zeros((tab.shape[0] - 192, tab.shape[1]), BF16)
        small[...] = jnp.zeros_like(small)
        loads[D_BRANCH].wait()
        loads[W_OUT].wait()
        da[...] = mm_t(d_branch[...], w[W_OUT][...]).astype(BF16)
        for name in (S_Q, S_K, S_V, TABLE, S_P):
            loads[name].wait()
        row = lax.broadcasted_iota(jnp.int32, (192, 192), 0)
        col = lax.broadcasted_iota(jnp.int32, (192, 192), 1)
        tab[0:192, :] = mm(jnp.where(row + col == 192, 1.0, 0.0).astype(BF16), tab[0:192, :]).astype(BF16)
        vc[0:seq, :] = sc[S_V][0:seq, :]
        vc[seq + 64:seq + 64 + slots, :] = sc[S_V][seq:rows, :]
        tab[192:192 + slots, :] = sc[S_K][seq:rows, :]
        halves = head_masks()
        label = lax.broadcasted_iota(jnp.int32, (1, 256), 1)
        own_label = (label >= 12) & (label < 12 + 2 * radius + 1)

        def pair(p, carry):
            cols = pl.ds(pl.multiple_of(p * 128, 128), 128)
            qp = sc[S_Q][:, cols]
            kp = sc[S_K][0:seq, cols]
            rk = tab[:, cols]
            vp = vc[:, cols]
            dap = da[:, cols]
            q_t = qp.T
            da_t = dap.T
            dq, dk_t, dv_t = [], [], []
            for hh in range(2):
                h = p * 2 + hh
                dam = jnp.where(halves[hh], dap, jnp.zeros_like(dap))
                prob_low = sc[S_P][h]
                d_prob = mm_t(dam, vp)
                prob = [prob_low[:, 128 * c:128 * c + 128].astype(F32) for c in range(3)]
                d_prob = [d_prob[:, 128 * c:128 * c + 128] for c in range(3)]
                delta = jnp.sum(sum(a * b for a, b in zip(prob, d_prob)), axis=-1, keepdims=True)
                delta = delta / jnp.sum(sum(prob), axis=-1, keepdims=True)
                ds = jnp.concatenate([(a * (b - delta)).astype(BF16) for a, b in zip(prob, d_prob)], 1)
                ds1 = ds[:, 0:seq]
                rel = pltpu.roll(mm(ds1[0:seq], flip[...]).astype(BF16), 0, 1, stride=1, stride_axis=0)
                far = jnp.concatenate(
                    [
                        jnp.concatenate([rel[:, 0:128], rel[:, 128:256] + ds[0:seq, seq:]], 1),
                        jnp.concatenate([jnp.zeros((slots, 128), BF16), ds[seq:rows, seq:]], 1),
                    ],
                    0,
                )
                dq.append(mm(ds1, kp) + mm(far, rk))
                own = slice(64 * hh, 64 * hh + 64)
                dk_t.append(jnp.concatenate([mm(q_t[own], ds1), mm(q_t[own], far)], 1) * 0.125)
                dv_t.append(mm(da_t[own], prob_low).astype(BF16))
            fs[D_Q][:, cols] = (jnp.where(halves[0], dq[0], dq[1]) * 0.125).astype(BF16)
            dk_t = jnp.concatenate(dk_t, 0)
            dk_low = dk_t.astype(BF16)
            dv_t = jnp.concatenate(dv_t, 0)
            fs[D_K][0:seq, cols] = dk_low[:, 0:seq].T
            fs[D_K][seq:rows, cols] = dk_low[:, seq + 128:].T[64:64 + slots]
            fs[D_V][0:seq, cols] = dv_t[:, 0:seq].T
            fs[D_V][seq:rows, cols] = dv_t[:, seq:].T[64:64 + slots]
            tab_s[cols, :] = jnp.where(own_label, dk_t[:, seq:], 0.0)
            return carry

        lax.fori_loop(0, H // 2, pair, 0, unroll=2)
        save(D_Q)
        save(D_K)
        save(D_V)
        small[64:65, :] = jnp.sum(fs[D_Q][...].astype(F32), axis=0, keepdims=True)
        small[65:66, :] = jnp.sum(fs[D_V][...].astype(F32), axis=0, keepdims=True)
        for name in (W_QUERY, W_KEY, W_VALUE, S_TAB):
            loads[name].wait()
        d_rows = (
            d_branch[...].astype(F32)
            + mm_t(fs[D_Q][...], w[W_QUERY][...])
            + mm_t(fs[D_K][...], w[W_KEY][...])
            + mm_t(fs[D_V][...], w[W_VALUE][...])
        )
        dx_low[...] = d_rows.astype(BF16)
        outs.append(cp.start(dx_low, d_send))
        dx[...] = d_rows
        outs.append(cp.start(dx.at[0:seq], rows_of(long_back, item, seq)))
        outs.append(cp.start(dx.at[seq:rows], rows_of(glob_back, item, slots)))
        tab_s[:, 128:] += small[...].T + small_t[...]
        outs.append(cp.start(tab_s, tab_out.at[item]))
        for copy in outs:
            copy.wait()


def run_attention_back(step_at, counts, d_branch, small, weights, state, made, seq, slots, radius):
    rows, width = d_branch.shape[1:]
    named, kept = dict(zip(WEIGHTS, weights)), dict(zip(STATE, state))
    items = kept[S_Q].shape[0]
    low = jax.ShapeDtypeStruct((items, rows, width), BF16)
    out_shape = [low, low, low, jax.ShapeDtypeStruct((items, width, 256), F32),
                 jax.ShapeDtypeStruct((items * seq, width), F32), jax.ShapeDtypeStruct((items * slots, width), F32),
                 jax.ShapeDtypeStruct((rows, width), BF16)]
    operands = [counts, d_branch, small] + [named[n] for n in ATTENTION_WEIGHTS] + [kept[n] for n in ATTENTION_USED]
    aliases = {}
    if made is not None:
        aliases = {len(operands) + n: n for n in range(6)}
        operands += list(made)
    scratch = [vm((256, width)) if n == TABLE else vm(named[n].shape) for n in ATTENTION_WEIGHTS]
    scratch += [vm(kept[n].shape[1:], kept[n].dtype) for n in ATTENTION_USED]
    scratch += [vm((rows, width))] * 3
    scratch += [vm((rows, width)), vm((rows, width)), vm((rows, width), F32), vm((rows, width)), vm((width, 256), F32), vm((128, width), F32),
                vm((width, 128), F32), vm((seq, seq)), vm((seq + 128, width)), pltpu.SemaphoreType.DMA((32,))]
    result = pl.pallas_call(
        functools.partial(attention_back_kernel, (seq, slots, radius, made is None, step_at)),
        out_shape=out_shape,
        in_specs=[SMEM] + [ANY] * (len(operands) - 1),
        out_specs=[ANY] * len(out_shape),
        scratch_shapes=scratch,
        input_output_aliases=aliases,
        compiler_params=pltpu.CompilerParams(vmem_limit_bytes=60 << 20),
        cost_estimate=pl.CostEstimate(flops=15 * 10**9, bytes_accessed=20 * 10**6, transcendentals=0),
        name="attention_back",
    )(*operands)
    return result[:6], result[6]


TILE = 16
MESH_ID = pl.DeviceIdType.MESH
NZ, NY, NX = 4, 2, 2
LOADED = (S_X, S_ATT, D_BRANCH, D_Q, D_K, D_V)
CHUNKS = ((2, 0), (0, 2)) * 3 + ((1, 0),)
ENTER = (0, 2, 4, 6, 8, 10, 11)
PIECES = 4
SPACING = 2
FFN_ORDER = (0, 3, 1, 2)
STAGES = 6
PER_CHUNK = 7
PER_FFN = 4


def reduce_kernel(cfg, *refs):
    pl.when(lax.axis_index("section") == cfg[3])(lambda: reduce_turn(cfg, *refs))


def reduce_turn(cfg, *refs):
    rows, width, hidden, turn = cfg
    wide, narrow = hidden // SHARDS, width // SHARDS
    ins = dict(zip(LOADED, refs[:6]))
    n1_hbm, n1_near, df_hbm, df_a, df_b, up_hbm, bias_hbm, down_hbm, tab_hbm, red_hbm = refs[6:16]
    refs = refs[16:]
    buf = dict(zip(LOADED, refs[:6]))
    n1, df, w_up, b_up, w_down, tab, ga, gf, ay, ax, az, by, bz, bx, fx, fz, u, d_hid, red = refs[6:25]
    load_sems, send_sems, recv_sems = refs[25:]
    section = lax.axis_index("section")
    me = lax.axis_index("dp")
    x, y, z = lax.rem(me, NX), lax.rem(lax.div(me, NX), NY), lax.div(me, NX * NY)
    half = rows // 2

    def at(zz, yy, xx):
        return (section, (zz * NY + yy) * NX + xx)

    across_x, across_y = at(z, y, 1 - x), at(z, 1 - y, x)
    above, below = at(z + 1, y, x), at(z - 1, y, x)

    cp = Copies(load_sems)
    loads = {}
    for name in (D_BRANCH, S_ATT):
        loads[name] = [cp.start(ins[name], buf[name])]
    loads[S_N1] = [cp.start(n1_hbm, n1.at[0:rows]), cp.start(n1_near, n1.at[rows:])]
    loads[D_FFN] = [cp.start(df_hbm, df.at[0:rows])]
    loads[D_FFN] += [cp.start(df_a, df.at[rows:rows + half]), cp.start(df_b, df.at[rows + half:])]
    loads[B_UP] = [cp.start(bias_hbm, b_up)]
    for n in FFN_ORDER:
        units = pl.ds(pl.multiple_of((2 * n + y) * 2 * wide, 2 * wide), 2 * wide)
        loads[W_UP, n] = [cp.start(up_hbm.at[:, units], w_up.at[n]), cp.start(down_hbm.at[units], w_down.at[n])]
    for name in (S_X, D_Q, D_K, D_V):
        loads[name] = [cp.start(ins[name], buf[name])]
    loads[S_TAB] = [cp.start(tab_hbm, tab)]

    barrier = pltpu.get_barrier_semaphore()
    for other in (across_x, across_y):
        pl.semaphore_signal(barrier, inc=1, device_id=other, device_id_type=MESH_ID)

    @pl.when(z > 0)
    def _():
        pl.semaphore_signal(barrier, inc=1, device_id=below, device_id_type=MESH_ID)

    @pl.when(z < NZ - 1)
    def _():
        pl.semaphore_signal(barrier, inc=1, device_id=above, device_id_type=MESH_ID)

    def need(*names):
        for name in names:
            for copy in loads.pop(name, ()):
                copy.wait()

    def units_of(n):
        return pl.ds(pl.multiple_of((2 * n + y) * 2 * wide, 2 * wide), 2 * wide)

    def form_hidden(n):
        need(S_N1, D_FFN, B_UP, (W_UP, n))
        bias = b_up[:, units_of(n)].astype(F32)

        def body(k, carry):
            some = pl.ds(pl.multiple_of(k * half, half), half)
            act, slope = gelu_parts(mm(n1[some, :], w_up[n]) + bias)
            u[some, :] = act.astype(BF16)
            d_hid[some, :] = (slope * mm_t(df[some, :], w_down[n])).astype(BF16)
            return carry

        lax.fori_loop(0, 4, body, 0)

    def form_down(n):
        part = mm_c(u[...], df[...]).astype(BF16)
        gf[n, 0, 0:wide, :] = part[0:wide]
        gf[n, 1, 0:wide, :] = part[wide:]

    def form_up(n):
        part = mm_c(d_hid[...], n1[...]).astype(BF16)
        gf[n, 0, wide:, :] = part[0:wide]
        gf[n, 1, wide:, :] = part[wide:]

    def form_narrow(left, right, at_row):
        need(left, right)

        def body(n, carry):
            cols = pl.ds(pl.multiple_of(n * 8 * narrow, 8 * narrow), 8 * narrow)
            part = mm_c(buf[left][:, cols], buf[right][...]).astype(BF16)
            for k in range(8):
                ga[2 * n + k // 4, (k // 2) % 2, k % 2, at_row:at_row + narrow, :] = part[k * narrow:(k + 1) * narrow]
            return carry

        lax.fori_loop(0, SHARDS // 8, body, 0)

    def form_table(at_row):
        need(S_TAB)

        def body(n, carry):
            for k in range(narrow // TILE):
                rows_k = pl.ds(pl.multiple_of(n * narrow + k * TILE, TILE), TILE)
                part = tab[0, rows_k, :] + tab[1, rows_k, :]
                shard = ga.at[lax.div(n, 4), lax.rem(lax.div(n, 2), 2), lax.rem(n, 2), at_row:at_row + TILE]
                shard[:, 256 * k:256 * k + 256] = part.astype(BF16)
            return carry

        lax.fori_loop(0, SHARDS, body, 0)

    first = [0]
    for counts in CHUNKS:
        first.append(first[-1] + sum(counts))

    def spans(chunk, route):
        counts = CHUNKS[chunk]
        start = first[chunk] + sum(counts[:route])
        own = sum(CHUNKS[n][route] for n in range(chunk))
        size = counts[route] * TILE
        return slice(start * TILE, start * TILE + size), slice(own * TILE, own * TILE + size), size

    pending = []

    def remote(src, dst, index, target):
        return pltpu.make_async_remote_copy(
            src_ref=src, dst_ref=dst, send_sem=send_sems.at[index], recv_sem=recv_sems.at[index],
            device_id=target, device_id_type=MESH_ID,
        )

    def send(src, dst, index, target):
        remote(src, dst, index, target).start()
        pending.append((None, lambda: remote(src, dst, index, target).wait_send()))

    def add(dst, src, lead, size):
        part = 48 if size % 48 == 0 else 32 if size % 32 == 0 else TILE
        steps = size // part
        for n in lead:
            steps *= n

        def body(n, carry):
            some = pl.ds(pl.multiple_of(lax.rem(n, size // part) * part, part), part)
            idx, rest = [], lax.div(n, size // part)
            for count in reversed(lead):
                idx.insert(0, lax.rem(rest, count))
                rest = lax.div(rest, count)
            d, s = dst(*idx).at[some], src(*idx).at[some]
            d[...] = (d[...].astype(F32) + s[...].astype(F32)).astype(BF16)
            return carry

        lax.fori_loop(0, steps, body, 0)

    def flow_z(stage, own, room, base, lead, size, shards=tuple(range(NZ))):
        def take(shard, slot, source):
            remote(own(shard), room(slot), base(slot), source).wait_recv()
            add(lambda *i: own(shard).at[i] if i else own(shard), lambda *i: room(slot).at[i] if i else room(slot), lead, size)

        def put(zz, shard, target):
            slot = NZ if (shard < zz and shard == zz - 1) else shard
            remote(own(shard), room(slot), base(slot), target).start()
            pending.append((zz, lambda: remote(own(shard), room(slot), base(slot), target).wait_send()))

        for zz in range(NZ):
            ups = [s for s in range(NZ - 1, zz - 1, -1) if s in shards]
            downs = [s for s in range(zz + 1) if s in shards]

            @pl.when(z == zz)
            def _():
                if stage == zz:
                    for shard in ups:
                        if zz > 0:
                            take(shard, shard, below)
                        if shard > zz:
                            put(zz, shard, above)
                if stage == NZ - 1 - zz:
                    for shard in downs:
                        if zz < NZ - 1:
                            take(shard, NZ if shard == zz else shard, above)
                        if shard < zz:
                            put(zz, shard, below)

    ffn_sems = len(CHUNKS) * PER_CHUNK

    def run(chunk, route, stage):
        rs, own, size = spans(chunk, route)
        if size == 0:
            return
        base = chunk * PER_CHUNK
        flow_base = lambda slot: base + 2 + slot
        out = slice(2 * wide + rs.start, 2 * wide + rs.stop)
        if stage == 0:
            room = ay if route == 0 else by
            send(ga.at[:, 1 - y, :, rs], room.at[:, :, own], base, across_y)
        if stage == 1:
            room = ay if route == 0 else by
            remote(ga.at[:, 1 - y, :, rs], room.at[:, :, own], base, across_y).wait_recv()
            add(lambda i, j: ga.at[i, y, j, rs], lambda i, j: room.at[i, j, own], (NZ, NX), size)
        if route == 0:
            if stage == 1:
                send(ga.at[:, y, 1 - x, rs], ax.at[:, own], base + 1, across_x)
            if stage == 2:
                remote(ga.at[:, y, 1 - x, rs], ax.at[:, own], base + 1, across_x).wait_recv()
                add(lambda i: ga.at[i, y, x, rs], lambda i: ax.at[i, own], (NZ,), size)
            if stage >= 2:
                flow_z(stage - 2, lambda s: ga.at[s, y, x, rs], lambda s: az.at[s, own], flow_base, (), size)
        else:
            if 1 <= stage <= 4:
                flow_z(stage - 1, lambda s: ga.at[s, y, :, rs], lambda s: bz.at[s, :, own], flow_base, (NX,), size)
            if stage == 4:
                send(ga.at[z, y, 1 - x, rs], bx.at[own], base + 1, across_x)
            if stage == 5:
                remote(ga.at[z, y, 1 - x, rs], bx.at[own], base + 1, across_x).wait_recv()
                add(lambda: ga.at[z, y, x, rs], lambda: bx.at[own], (), size)
        if stage == 5:
            red[out, :] = ga[z, y, x, rs, :].astype(F32)

    def run_ffn(n, piece, stage):
        base = ffn_sems + (n * PIECES + piece) * PER_FFN
        size = 2 * wide // PIECES
        rs = slice(piece * size, (piece + 1) * size)
        if stage == 0:
            send(gf.at[n, 1 - x, rs], fx.at[n, rs], base, across_x)
        if stage == 1:
            remote(gf.at[n, 1 - x, rs], fx.at[n, rs], base, across_x).wait_recv()
            add(lambda: gf.at[n, x, rs], lambda: fx.at[n, rs], (), size)
        if 1 <= stage <= 4:
            room = lambda slot: fz.at[1 if slot == NZ else 0, n, rs]
            flow_z(stage - 1, lambda s: gf.at[s, x, rs], room, lambda slot: base + (2 if slot == NZ else 1), (), size, (n,))
        if stage == 5:
            @pl.when(z == n)
            def _():
                red[rs, :] = gf[n, x, rs, :].astype(F32)

    def narrow_task(n):
        left, right = ((D_BRANCH, S_ATT), (D_Q, S_X), (D_K, S_X), (D_V, S_X))[n]
        return lambda: form_narrow(left, right, n * narrow)

    a, b, c, d = FFN_ORDER
    hidden_task = lambda n: lambda: form_hidden(n)
    down_task = lambda n: lambda: form_down(n)
    up_task = lambda n: lambda: form_up(n)
    tasks = [(narrow_task(1),), (up_task(a),), (hidden_task(b),), (down_task(b),), (narrow_task(2),), (up_task(b),),
             (hidden_task(c), narrow_task(3)), (down_task(c),), (), (up_task(c),),
             (hidden_task(d), lambda: form_table(4 * narrow)), (down_task(d),), (up_task(d),)]
    narrow_task(0)()

    @pl.when((z == 0) | (z == NZ - 1))
    def _():
        pl.semaphore_wait(barrier, 3)

    @pl.when((z > 0) & (z < NZ - 1))
    def _():
        pl.semaphore_wait(barrier, 4)

    starts = [(n, None, slot) for n, slot in enumerate(ENTER)]
    starts += [(FFN_ORDER[k // PIECES], k % PIECES, k) for k in range(NZ * PIECES)]
    last = max(slot for _, _, slot in starts) + SPACING * (STAGES - 1)
    for slot in range(last + 1):
        for stage in range(STAGES):
            for n, piece, enter in starts:
                if enter + stage * SPACING == slot:
                    if slot == 0 and piece == 0:
                        form_hidden(a)
                        form_down(a)
                    if piece is None:
                        run(n, 0, stage)
                        run(n, 1, stage)
                    else:
                        run_ffn(n, piece, stage)
            if stage == 0:
                for task in tasks.pop(0) if tasks else ():
                    task()
    result = cp.start(red, red_hbm)
    for zz, wait in pending:
        if zz is None:
            wait()
        else:
            pl.when(z == zz)(wait)
    result.wait()


def reduce_grads(turn, parts, near, weights, tab):
    rows, width = parts[S_X].shape
    hidden = weights[W_UP].shape[1]
    wide, narrow = hidden // SHARDS, width // SHARDS
    share = 4 * narrow + TILE
    t = [sum(c[n] for c in CHUNKS) * TILE for n in range(2)]
    assert sum(t) == share
    n_sem = len(CHUNKS) * PER_CHUNK + NZ * PIECES * PER_FFN
    scratch = [vm(parts[n].shape) for n in LOADED]
    scratch += [
        vm((2 * rows, width)), vm((2 * rows, width)), vm((NZ, width, 2 * wide)), vm((1, hidden)), vm((NZ, 2 * wide, width)),
        vm(tab.shape, F32),
        vm((NZ, NY, NX, share, width)), vm((NZ, NX, 2 * wide, width)),
        vm((NZ, NX, t[0], width)), vm((NZ, t[0], width)), vm((NZ + 1, t[0], width)),
        vm((NZ, NX, t[1], width)), vm((NZ + 1, NX, t[1], width)), vm((t[1], width)),
        vm((NZ, 2 * wide, width)), vm((2, NZ, 2 * wide, width)), vm((2 * rows, 2 * wide)), vm((2 * rows, 2 * wide)),
        vm((2 * wide + share, width), F32),
        pltpu.SemaphoreType.DMA((32,)), pltpu.SemaphoreType.DMA((n_sem,)), pltpu.SemaphoreType.DMA((n_sem,)),
    ]
    operands = [parts[n] for n in LOADED]
    operands += [parts[S_N1], near[0], parts[D_FFN]] + list(near[1:])
    operands += [weights[W_UP], weights[B_UP], weights[W_DOWN], tab]
    return pl.pallas_call(
        functools.partial(reduce_kernel, (rows, width, hidden, turn)),
        cost_estimate=pl.CostEstimate(flops=60 * 10**9, bytes_accessed=20 * 10**6, transcendentals=0),
        out_shape=jax.ShapeDtypeStruct((2 * wide + share, width), F32),
        in_specs=[ANY] * len(operands),
        out_specs=ANY,
        scratch_shapes=scratch,
        compiler_params=pltpu.CompilerParams(collective_id=turn, has_side_effects=True, vmem_limit_bytes=60 << 20),
        name="reduce_grads",
    )(*operands)


def finish_kernel(labels, red_a, red_b, *refs):
    w_out, w_query, w_key, w_value, w_up, w_down, table = refs[:7]
    vectors, bias, red, turned, sem = refs[7:15], refs[15], refs[16], refs[17], refs[18]
    wide, narrow = w_up.shape[0], w_out.shape[0]
    cp = Copies(sem)
    cp.choose(lax.axis_index("section") == 0, red_a, red_b, red).wait()
    outs = [cp.start(red.at[0:wide], w_down), cp.start(red.at[wide:2 * wide], w_up)]
    for n, ref in enumerate((w_out, w_query, w_key, w_value)):
        at = 2 * wide + n * narrow
        outs.append(cp.start(red.at[at:at + narrow], ref))
    at = 2 * wide + 4 * narrow
    packed = jnp.concatenate([red[at:at + TILE, 256 * k:256 * k + 256] for k in range(narrow // TILE)], 0)
    turned[...] = packed.T
    row = lax.broadcasted_iota(jnp.int32, (256, labels), 0)
    col = lax.broadcasted_iota(jnp.int32, (256, labels), 1)
    back = jnp.where(row + col == labels + 11, 1.0, 0.0)
    table[...] = jnp.dot(packed, back, precision=lax.Precision.HIGHEST, preferred_element_type=F32)
    for n, ref in enumerate(vectors):
        ref[...] = turned[192 + n:193 + n, :]
    for k in range(wide // narrow):
        bias[:, k * narrow:(k + 1) * narrow] = turned[200 + k:201 + k, :]
    for copy in outs:
        copy.wait()


def finish(red_a, red_b, labels, hidden):
    width = red_a.shape[1]
    wide, narrow = hidden // SHARDS, width // SHARDS
    out = lambda *s: jax.ShapeDtypeStruct(s, F32)
    shapes = [out(narrow, width)] * 4 + [out(wide, width), out(wide, width), out(narrow, labels)]
    shapes += [out(1, narrow)] * 8 + [out(1, wide)]
    result = pl.pallas_call(
        functools.partial(finish_kernel, labels),
        out_shape=shapes,
        in_specs=[ANY, ANY],
        out_specs=[ANY] * 6 + [pl.BlockSpec(memory_space=pltpu.VMEM)] * (len(shapes) - 6),
        scratch_shapes=[vm(red_a.shape, F32), vm((256, narrow), F32), pltpu.SemaphoreType.DMA((8,))],
        compiler_params=pltpu.CompilerParams(vmem_limit_bytes=40 << 20),
        name="finish",
    )(red_a, red_b)
    mats = [t.T for t in result[:5]] + [result[5], result[6].T]
    return [t[None] for t in mats] + list(result[7:])


def sums_elsewhere(parts, weights, tab):
    def scatter(value, dim):
        return lax.psum_scatter(value, "dp", scatter_dimension=dim, tiled=True)

    cut = [scatter(mm_c(parts[a], parts[b]), 1)
           for a, b in ((S_ATT, D_BRANCH), (S_X, D_Q), (S_X, D_K), (S_X, D_V))]
    act, slope = gelu_parts(mm(parts[S_N1], weights[W_UP]) + weights[B_UP].astype(F32))
    d_hid = (slope * mm_t(parts[D_FFN], weights[W_DOWN])).astype(BF16)
    w_up = scatter(mm_c(parts[S_N1], d_hid), 1)
    w_down = scatter(mm_c(act.astype(BF16), parts[D_FFN]), 0)
    b_up = scatter(jnp.sum(d_hid.astype(F32), axis=0), 0)
    return cut, w_up, w_down, scatter(tab[0] + tab[1], 0), b_up


def per_device(
    long_input, global_input, counts, w_query, b_query, w_key, w_value, b_value, w_out, b_out, rel_table,
    norm1_gain, norm1_bias, w_up, b_up, w_down, b_down, norm2_gain, norm2_bias, long_cot, global_cot,
):
    items = counts.shape[0]
    seq, slots, width = long_input.shape[0] // items, global_input.shape[0] // items, long_input.shape[1]
    rows, hidden = seq + slots, w_up.shape[2]
    labels = rel_table.shape[1]
    radius = (labels - 1) // 2
    weights = [w_query[0], w_key[0], w_value[0], w_out[0], w_up[0], w_down[0],
               jnp.pad(rel_table[0], ((12, 192 - 12 - labels), (0, 0))),
               b_query, b_value, b_out, norm1_gain, norm1_bias, b_up, b_down, norm2_gain, norm2_bias]

    recv = long_input
    state = outs = None
    for step in range(items + 1):
        state, outs, sent = run_forward(
            step, counts, long_input, global_input, recv, weights, state, outs, seq, slots, radius)
        if step < items:
            recv = lax.ppermute(sent, "section", [(0, 1)])
    kept = dict(zip(STATE, state))
    shards = lax.axis_size("dp")
    paired = shards == SHARDS
    near = []
    if paired:
        near = [lax.ppermute(kept[S_N1], "dp", [(n, n ^ NX) for n in range(shards)]).reshape(items * rows, width)]
    named = dict(zip(WEIGHTS, weights))

    def parts_of():
        parts = {n: kept[n] for n in (S_X, S_ATT, S_N1)}
        parts.update(zip((D_FFN, D_BRANCH, D_Q, D_K, D_V), list(low) + list(made[:3])))
        return {n: t.reshape(items * rows, t.shape[2]) for n, t in parts.items()}

    low = made = None
    summed, awaited = [], near[0:1]
    for step in range(items + 1):
        low, d_ffn, small = run_hidden_back(
            step, counts, long_cot, global_cot, recv, weights, state, low, awaited if step else [], seq, slots)
        if paired:
            pairs = [(e * shards + n, e * shards + (n ^ NX)) for e in range(2) for n in range(shards)
                     if 0 <= step - (1 - e) < items]
            near.append(lax.ppermute(d_ffn, ("section", "dp"), pairs))
        made, sent = run_attention_back(
            step, counts, low[1], small, weights, state, made, seq, slots, radius)
        if step < items:
            if paired:
                sent, near[-1] = lax.optimization_barrier((sent, near[-1]))
            recv = lax.ppermute(sent, "section", [(1, 0)])
        if paired and step >= items - 1:
            turn = items - step
            awaited = [reduce_grads(turn, parts_of(), [near[0]] + near[step:step + 2], named, made[3])]
            summed += awaited
    long_back, glob_back = made[4:6]
    if paired:
        final = finish(summed[1], summed[0], labels, hidden)
        g_out, g_query, g_key, g_value, g_up, g_down, g_table = final[:7]
        g_bq, g_bv, g_bo, g_g1, g_s1, g_bd, g_g2, g_s2, g_b_up = final[7:]
    else:
        cut, g_up, g_down, table, g_b_up = [jax.tree.map(lambda t: t[None], t)
                                            for t in sums_elsewhere(parts_of(), named, made[3])]
        g_out, g_query, g_key, g_value = cut
        g_bq, g_bv, g_bo, g_g1, g_s1, g_bd, g_g2, g_s2 = [table[:, :, 192 + n] for n in range(8)]
        g_table = table[0, :, 12:12 + labels][:, ::-1].T[None]
    grads = (g_query, g_bq, g_key, g_value, g_bv, g_out, g_bo, g_table, g_g1, g_s1, g_up, g_b_up, g_down, g_bd, g_g2, g_s2)
    return tuple(t[None] for t in (outs[0], outs[1], long_back, glob_back)) + grads


def solution(mesh):
    part = P("section", "dp", None)
    vector = P("section", "dp")
    columns = P("section", None, "dp")
    matrix = P("section", None, None)
    row = P("section", None)
    items = P("dp", None)
    in_specs = (items, items, P("dp"), matrix, row, matrix, matrix, row, matrix, row, matrix, row, row,
                matrix, row, matrix, row, row, row, items, items)
    out_specs = (part, part, part, part, columns, vector, columns, columns, vector, columns, vector, columns,
                 vector, vector, columns, vector, part, vector, vector, vector)
    return jax.shard_map(per_device, mesh=mesh, in_specs=in_specs, out_specs=out_specs, check_vma=False)
```

```python
import functools
import math

import jax
import jax.numpy as jnp
from jax import lax
from jax.experimental import pallas as pl
from jax.experimental.pallas import tpu as pltpu
from jax.sharding import PartitionSpec as P

H = 12
F32 = jnp.float32
BF16 = jnp.bfloat16
ANY = pl.BlockSpec(memory_space=pl.ANY)
SMEM = pl.BlockSpec(memory_space=pltpu.SMEM)
NEG = -1e30
SHARDS = 16
BIAS_LANE = 72
(
    W_QUERY, W_KEY, W_VALUE, W_OUT, W_UP, W_DOWN, TABLE, B_QUERY, B_VALUE, B_OUT, NORM1_GAIN, NORM1_BIAS, B_UP, B_DOWN, NORM2_GAIN, NORM2_BIAS,
    D_FFN, D_HIDDEN, D_BRANCH, D_Q, D_K, D_V, S_X, S_Q, S_K, S_V, S_ATT, S_N1, S_XH1, S_XH2, S_U, S_GP, S_P, S_RS1, S_RS2, S_TAB,
) = range(36)


def mm(a, b):
    return jnp.dot(a, b, preferred_element_type=F32)


def mm_t(a, b):
    return lax.dot_general(a, b, (((1,), (1,)), ((), ())), preferred_element_type=F32)


def mm_c(a, b):
    return lax.dot_general(a, b, (((0,), (0,)), ((), ())), preferred_element_type=F32)


class Copies:
    def __init__(self, sems):
        self.sems = sems
        self.used = 0

    def make(self, src, dst):
        copy = pltpu.make_async_copy(src, dst, self.sems.at[self.used])
        self.used += 1
        return copy

    def start(self, src, dst):
        copy = self.make(src, dst)
        copy.start()
        return copy

    def choose(self, first, src_a, src_b, dst):
        a = pltpu.make_async_copy(src_a, dst, self.sems.at[self.used])
        b = pltpu.make_async_copy(src_b, dst, self.sems.at[self.used])
        self.used += 1
        pl.when(first)(a.start)
        pl.when(jnp.logical_not(first))(b.start)
        return a


def normalize(rows):
    center = rows - jnp.mean(rows, axis=-1, keepdims=True)
    spread = jnp.mean(center * center, axis=-1, keepdims=True)
    rstd = lax.rsqrt(spread + 1e-05)
    return center * rstd, rstd


GELU_C = math.sqrt(2.0 / math.pi)


def gelu_parts(z):
    zz = z * z
    t = jnp.tanh(z * (GELU_C + (GELU_C * 0.044715) * zz))
    half = 0.5 + 0.5 * t
    slope = half + (0.5 * z) * (1.0 - t * t) * (GELU_C + (3.0 * GELU_C * 0.044715) * zz)
    return z * half, slope


WEIGHTS = (
    W_QUERY, W_KEY, W_VALUE, W_OUT, W_UP, W_DOWN, TABLE,
    B_QUERY, B_VALUE, B_OUT, NORM1_GAIN, NORM1_BIAS, B_UP, B_DOWN, NORM2_GAIN, NORM2_BIAS,
)
STATE = (S_X, S_Q, S_K, S_V, S_ATT, S_N1, S_XH1, S_XH2, S_GP, S_P, S_RS1, S_RS2)


def state_shapes(items, rows, width, hidden, keys):
    low = lambda *s: jax.ShapeDtypeStruct((items,) + s, BF16)
    shapes = {name: low(rows, width) for name in (S_X, S_Q, S_K, S_V, S_ATT, S_N1, S_XH1, S_XH2)}
    shapes[S_GP] = low(rows, hidden)
    shapes[S_P] = low(H, rows, keys)
    shapes[S_RS1] = shapes[S_RS2] = jax.ShapeDtypeStruct((items, rows, 128), F32)
    return [shapes[name] for name in STATE]


def place_labels(table, turned):
    labels = table.shape[0]
    row = lax.broadcasted_iota(jnp.int32, (192, labels), 0)
    col = lax.broadcasted_iota(jnp.int32, (192, labels), 1)
    hit = row + col == labels + 11 if turned else row == col + 12
    return mm(jnp.where(hit, 1.0, 0.0).astype(BF16), table[...]).astype(BF16)


def head_masks():
    lane = lax.broadcasted_iota(jnp.int32, (1, 128), 1)
    return [lane < 64, lane >= 64]


def turn_of(counts, step_at, forward):
    section = lax.axis_index("section")
    first = (section == 0) if forward else (section == 1)
    turn = jnp.where(first, step_at, step_at - 1)
    item = jnp.clip(turn, 0, counts.shape[0] - 1)
    return item, counts[item], turn == item, first


def fwd_kernel(cfg, *refs):
    seq, slots, radius, first_call, step_at = cfg
    rows = seq + slots
    counts, x_long, x_glob, recv = refs[:4]
    w_hbm = dict(zip(WEIGHTS, refs[4:20]))
    refs = refs[20:]
    if not first_call:
        refs = refs[len(STATE) + 2:]
    st = dict(zip(STATE, refs[:len(STATE)]))
    long_out, glob_out, y_send = refs[len(STATE):len(STATE) + 3]
    refs = refs[len(STATE) + 3:]
    w = dict(zip(WEIGHTS, refs[:16]))
    sc = dict(zip(STATE, refs[16:16 + len(STATE)]))
    y_v, tab, vc, bandm, ownm, sems = refs[16 + len(STATE):]
    item, count, active, fresh = turn_of(counts, step_at, True)

    @pl.when(active)
    def _():
        cp = Copies(sems)
        long_rows = pl.ds(pl.multiple_of(item * seq, seq), seq)
        glob_rows = pl.ds(pl.multiple_of(item * slots, slots), slots)
        c_x = cp.choose(fresh, x_long.at[long_rows], recv.at[0:seq], sc[S_X].at[0:seq])
        c_g = cp.choose(fresh, x_glob.at[glob_rows], recv.at[seq:rows], sc[S_X].at[seq:rows])
        loads = {}
        for name in (W_QUERY, B_QUERY, W_KEY, W_VALUE, B_VALUE, TABLE, W_OUT, B_OUT, NORM1_GAIN,
                     NORM1_BIAS, W_UP, B_UP, W_DOWN, B_DOWN, NORM2_GAIN, NORM2_BIAS):
            loads[name] = cp.start(w_hbm[name], w[name])
        outs = []

        def save(name):
            outs.append(cp.start(sc[name], st[name].at[item]))

        def vec(name):
            loads[name].wait()
            return w[name][...].astype(F32)

        row = lax.broadcasted_iota(jnp.int32, (seq, seq), 0)
        col = lax.broadcasted_iota(jnp.int32, (seq, seq), 1)
        bandm[...] = jnp.where(jnp.abs(col - row) <= radius, 0.0, NEG)
        key = lax.broadcasted_iota(jnp.int32, (slots, seq), 1)
        slot = lax.broadcasted_iota(jnp.int32, (slots, seq), 0)
        ownm[...] = jnp.where(lax.div(key * count, jnp.int32(seq)) == slot, 0.0, NEG)
        lane = lax.broadcasted_iota(jnp.int32, (1, 128), 1)
        globm = jnp.where((lane >= 64) & (lane < 64 + count), 0.0, NEG)
        vc[seq:, :] = jnp.zeros((128, vc.shape[1]), BF16)
        tab[192:, :] = jnp.zeros((tab.shape[0] - 192, tab.shape[1]), BF16)

        c_x.wait()
        c_g.wait()
        x = sc[S_X][...]
        save(S_X)
        loads[W_QUERY].wait()
        sc[S_Q][...] = (mm(x, w[W_QUERY][...]) + vec(B_QUERY)).astype(BF16)
        save(S_Q)
        loads[W_KEY].wait()
        k = mm(x, w[W_KEY][...]).astype(BF16)
        sc[S_K][...] = k
        save(S_K)
        loads[W_VALUE].wait()
        v = (mm(x, w[W_VALUE][...]) + vec(B_VALUE)).astype(BF16)
        sc[S_V][...] = v
        save(S_V)
        vc[0:seq, :] = v[0:seq]
        vc[seq + 64:seq + 64 + slots, :] = v[seq:rows]
        loads[TABLE].wait()
        tab[0:192, :] = place_labels(w[TABLE], False)
        tab[192:192 + slots, :] = k[seq:rows]
        halves = head_masks()

        ones_cols = jnp.ones((vc.shape[0], 128), BF16)
        live, done = {}, {}

        def scores(h):
            cols = slice(128 * (h // 2), 128 * (h // 2) + 128)
            qp = sc[S_Q][:, cols]
            qm = jnp.where(halves[h % 2], qp, jnp.zeros_like(qp)) * jnp.bfloat16(0.125)
            s1 = mm_t(qm, sc[S_K][0:seq, cols])
            s2 = mm_t(qm, tab[:, cols])
            band = pltpu.roll(s2[0:seq], (2 * seq - radius - 12) % seq, 1, stride=1, stride_axis=0)
            live[h] = (s1[0:seq] + band + bandm[...], s2[0:seq, 128:256] + globm,
                       s1[seq:rows] + ownm[...], s2[seq:rows, 128:256] + globm)

        def weigh(h):
            ll, lg, gl, gg = live.pop(h)
            parts = []
            for sl, sg in ((ll, lg), (gl, gg)):
                top = jnp.max(jnp.maximum(jnp.maximum(sl[:, 0:128], sl[:, 128:256]), sg), axis=-1, keepdims=True)
                parts.append(jnp.concatenate([jnp.exp(sl - top), jnp.exp(sg - top)], 1))
            live[h] = jnp.concatenate(parts, 0)

        def gather(h):
            cols = slice(128 * (h // 2), 128 * (h // 2) + 128)
            e = live.pop(h)
            got = mm(e.astype(BF16), jnp.concatenate([vc[:, cols], ones_cols], 1))
            inv = 1.0 / got[:, 128:]
            done[h] = got[:, 0:128] * inv
            for c in range(3):
                sc[S_P][h, :, 128 * c:128 * c + 128] = (e[:, 128 * c:128 * c + 128] * inv).astype(BF16)
            if h % 2:
                sc[S_ATT][:, cols] = jnp.where(halves[0], done.pop(h - 1), done.pop(h)).astype(BF16)

        for turn in range(H + 2):
            if turn < H:
                scores(turn)
            if 0 <= turn - 1 < H:
                weigh(turn - 1)
            if 0 <= turn - 2 < H:
                gather(turn - 2)
        save(S_P)
        save(S_ATT)
        loads[W_OUT].wait()
        r1 = x.astype(F32) + mm(sc[S_ATT][...], w[W_OUT][...]) + vec(B_OUT)
        xh1, rstd1 = normalize(r1)
        sc[S_XH1][...] = xh1.astype(BF16)
        save(S_XH1)
        sc[S_RS1][...] = jnp.broadcast_to(rstd1, (rows, 128))
        save(S_RS1)
        n1 = xh1 * vec(NORM1_GAIN) + vec(NORM1_BIAS)
        n1_low = n1.astype(BF16)
        sc[S_N1][...] = n1_low
        save(S_N1)
        hidden = w[W_UP].shape[1]
        step = 768
        loads[W_UP].wait()
        b_up = vec(B_UP)
        acc = n1 + vec(B_DOWN)
        for c in range(hidden // step):
            z = mm(n1_low, w[W_UP][:, c * step:(c + 1) * step]) + b_up[:, c * step:(c + 1) * step]
            act, slope = gelu_parts(z)
            act = act.astype(BF16)
            cols = slice(c * step, (c + 1) * step)
            sc[S_GP][:, cols] = slope.astype(BF16)
            outs.append(cp.start(sc[S_GP].at[:, cols], st[S_GP].at[item, :, cols]))
            if c == 0:
                loads[W_DOWN].wait()
            acc = acc + mm(act, w[W_DOWN][c * step:(c + 1) * step, :])
        xh2, rstd2 = normalize(acc)
        sc[S_XH2][...] = xh2.astype(BF16)
        save(S_XH2)
        sc[S_RS2][...] = jnp.broadcast_to(rstd2, (rows, 128))
        save(S_RS2)
        y = xh2 * vec(NORM2_GAIN) + vec(NORM2_BIAS)
        pos = lax.broadcasted_iota(jnp.int32, (rows, 1), 0)
        y = jnp.where(pos < seq + count, y, 0.0)
        y_v[...] = y.astype(BF16)
        outs.append(cp.start(y_v, y_send))
        outs.append(cp.start(y_v.at[0:seq], long_out.at[long_rows]))
        outs.append(cp.start(y_v.at[seq:rows], glob_out.at[glob_rows]))
        for copy in outs:
            copy.wait()


def vm(shape, dtype=BF16):
    return pltpu.VMEM(shape, dtype)


def run_forward(step_at, counts, x_long, x_glob, recv, weights, state, outs, seq, slots, radius):
    rows, width = seq + slots, x_long.shape[1]
    hidden = weights[4].shape[1]
    items = x_long.shape[0] // seq
    keys = seq + 128
    shapes = state_shapes(items, rows, width, hidden, keys)
    out_shape = shapes + [
        jax.ShapeDtypeStruct(x_long.shape, BF16),
        jax.ShapeDtypeStruct(x_glob.shape, BF16),
        jax.ShapeDtypeStruct((rows, width), BF16),
    ]
    first = state is None
    operands = [counts, x_long, x_glob, recv] + list(weights)
    aliases = {}
    if not first:
        base = len(operands)
        operands += list(state) + list(outs)
        aliases = {base + n: n for n in range(len(state) + 2)}
    scratch = []
    for name, t in zip(WEIGHTS, weights):
        scratch.append(vm(t.shape))
    scratch += [vm(s.shape[1:], s.dtype) for s in shapes]
    scratch += [vm((rows, width)), vm((256, width)), vm((keys, width)), vm((seq, seq), F32), vm((slots, seq), F32),
                pltpu.SemaphoreType.DMA((48,))]
    result = pl.pallas_call(
        functools.partial(fwd_kernel, (seq, slots, radius, first, step_at)),
        out_shape=out_shape,
        in_specs=[SMEM] + [ANY] * (len(operands) - 1),
        out_specs=[ANY] * len(out_shape),
        scratch_shapes=scratch,
        input_output_aliases=aliases,
        compiler_params=pltpu.CompilerParams(vmem_limit_bytes=60 << 20),
        cost_estimate=pl.CostEstimate(flops=20 * 10**9, bytes_accessed=20 * 10**6, transcendentals=0),
        name="layer_forward",
    )(*operands)
    n = len(STATE)
    return result[:n], result[n:n + 2], result[n + 2]


HIDDEN_USED = (S_XH1, S_XH2, S_GP, S_RS1, S_RS2)
HIDDEN_WEIGHTS = (W_UP, W_DOWN, NORM1_GAIN, NORM2_GAIN)
ATTENTION_USED = (S_Q, S_K, S_V, S_P)
ATTENTION_WEIGHTS = (W_QUERY, W_KEY, W_VALUE, W_OUT, TABLE)


def rows_of(ref, item, size):
    return ref.at[pl.ds(pl.multiple_of(item * size, size), size)]


def hidden_back_kernel(cfg, *refs):
    seq, slots, first_call, step_at, unread = cfg
    rows = seq + slots
    counts, c_long, c_glob, recv = refs[:4]
    w_hbm = dict(zip(HIDDEN_WEIGHTS, refs[4:8]))
    st = dict(zip(HIDDEN_USED, refs[8:13]))
    refs = refs[13:]
    if not first_call:
        refs = refs[2:]
    refs = refs[unread:]
    ffn_out, branch_out, ffn_now, small_out = refs[:4]
    refs = refs[4:]
    w = dict(zip(HIDDEN_WEIGHTS, refs[:4]))
    sc = dict(zip(HIDDEN_USED, refs[4:9]))
    dy, d_ffn_s, d_branch_s, small, small_t, sems = refs[9:]
    item, count, active, fresh = turn_of(counts, step_at, False)

    @pl.when(active)
    def _():
        cp = Copies(sems)
        c_y = cp.choose(fresh, rows_of(c_long, item, seq), recv.at[0:seq], dy.at[0:seq])
        c_g = cp.choose(fresh, rows_of(c_glob, item, slots), recv.at[seq:rows], dy.at[seq:rows])
        hidden, width = w[W_DOWN].shape
        step = width
        parts = [slice(c * step, (c + 1) * step) for c in range(hidden // step)]
        loads = {}
        for name in (S_RS2, S_XH2):
            loads[name] = cp.start(st[name].at[item], sc[name])
        loads[NORM2_GAIN] = cp.start(w_hbm[NORM2_GAIN], w[NORM2_GAIN])
        loads[S_GP] = cp.start(st[S_GP].at[item], sc[S_GP])
        for c, sl in enumerate(parts):
            loads[W_DOWN, c] = cp.start(w_hbm[W_DOWN].at[sl], w[W_DOWN].at[sl])
            loads[W_UP, c] = cp.start(w_hbm[W_UP].at[:, sl], w[W_UP].at[:, sl])
        for name in (S_RS1, S_XH1):
            loads[name] = cp.start(st[name].at[item], sc[name])
        loads[NORM1_GAIN] = cp.start(w_hbm[NORM1_GAIN], w[NORM1_GAIN])
        small[...] = jnp.zeros_like(small)
        pos = lax.broadcasted_iota(jnp.int32, (rows, 1), 0)
        lane = lax.broadcasted_iota(jnp.int32, (1, 128), 1)
        ones = jnp.ones((rows, 128), BF16)

        def norm_back(grad, xh, rstd, gain, at):
            small[at:at + 1, :] = jnp.sum(grad * xh, axis=0, keepdims=True)
            small[at + 1:at + 2, :] = jnp.sum(grad, axis=0, keepdims=True)
            dxh = grad * gain
            return rstd * (
                dxh - jnp.mean(dxh, axis=-1, keepdims=True) - xh * jnp.mean(dxh * xh, axis=-1, keepdims=True)
            )

        c_y.wait()
        c_g.wait()
        grad = jnp.where(pos < seq + count, dy[...].astype(F32), 0.0)
        for name in (NORM2_GAIN, S_XH2, S_RS2):
            loads[name].wait()
        d_second = norm_back(
            grad, sc[S_XH2][...].astype(F32), sc[S_RS2][:, 0:1], w[NORM2_GAIN][...].astype(F32), 70
        )
        d_ffn = d_second.astype(BF16)
        d_ffn_s[...] = d_ffn
        outs = [cp.start(d_ffn_s, ffn_out.at[item]), cp.start(d_ffn_s, ffn_now)]
        small[69:70, :] = jnp.sum(d_ffn.astype(F32), axis=0, keepdims=True)
        loads[S_GP].wait()
        d_normed = d_second
        wide, narrow = hidden // SHARDS, width // SHARDS
        for c, sl in enumerate(parts):
            loads[W_DOWN, c].wait()
            d_hid = (sc[S_GP][:, sl].astype(F32) * mm_t(d_ffn, w[W_DOWN][sl, :])).astype(BF16)
            loads[W_UP, c].wait()
            d_normed = d_normed + mm_t(d_hid, w[W_UP][:, sl])
            sums = mm_c(d_hid, ones)
            for shard in range(step // wide):
                block = jnp.zeros((narrow, 128), F32)
                for k in range(wide // narrow):
                    at = shard * wide + k * narrow
                    block = jnp.where(lane == BIAS_LANE + k, sums[at:at + narrow], block)
                at = (c * (step // wide) + shard) * narrow
                small_t[at:at + narrow, :] = block
        for name in (NORM1_GAIN, S_XH1, S_RS1):
            loads[name].wait()
        d_first = norm_back(
            d_normed, sc[S_XH1][...].astype(F32), sc[S_RS1][:, 0:1], w[NORM1_GAIN][...].astype(F32), 67
        )
        d_branch = d_first.astype(BF16)
        d_branch_s[...] = d_branch
        outs.append(cp.start(d_branch_s, branch_out.at[item]))
        small[66:67, :] = jnp.sum(d_branch.astype(F32), axis=0, keepdims=True)
        small_t[...] += small[...].T
        outs.append(cp.start(small_t, small_out))
        for copy in outs:
            copy.wait()


def run_hidden_back(step_at, counts, c_long, c_glob, recv, weights, state, made, arrived, seq, slots):
    rows, width = seq + slots, c_long.shape[1]
    named, kept = dict(zip(WEIGHTS, weights)), dict(zip(STATE, state))
    items = c_long.shape[0] // seq
    low = jax.ShapeDtypeStruct((items, rows, width), BF16)
    out_shape = [low, low, jax.ShapeDtypeStruct((rows, width), BF16), jax.ShapeDtypeStruct((width, 128), F32)]
    operands = [counts, c_long, c_glob, recv] + [named[n] for n in HIDDEN_WEIGHTS] + [kept[n] for n in HIDDEN_USED]
    aliases = {}
    if made is not None:
        aliases = {len(operands): 0, len(operands) + 1: 1}
        operands += list(made)
    operands += list(arrived)
    scratch = [vm(named[n].shape) for n in HIDDEN_WEIGHTS]
    scratch += [vm(kept[n].shape[1:], kept[n].dtype) for n in HIDDEN_USED]
    scratch += [vm((rows, width)), vm((rows, width)), vm((rows, width)),
                vm((128, width), F32), vm((width, 128), F32), pltpu.SemaphoreType.DMA((32,))]
    result = pl.pallas_call(
        functools.partial(hidden_back_kernel, (seq, slots, made is None, step_at, len(arrived))),
        out_shape=out_shape,
        in_specs=[SMEM] + [ANY] * (len(operands) - 1),
        out_specs=[ANY] * len(out_shape),
        scratch_shapes=scratch,
        input_output_aliases=aliases,
        compiler_params=pltpu.CompilerParams(vmem_limit_bytes=60 << 20),
        cost_estimate=pl.CostEstimate(flops=9 * 10**9, bytes_accessed=20 * 10**6, transcendentals=0),
        name="hidden_back",
    )(*operands)
    return result[:2], result[2], result[3]


def attention_back_kernel(cfg, *refs):
    seq, slots, radius, first_call, step_at = cfg
    rows = seq + slots
    counts, branch_hbm, small_hbm = refs[:3]
    w_hbm = dict(zip(ATTENTION_WEIGHTS, refs[3:8]))
    st = dict(zip(ATTENTION_USED, refs[8:12]))
    refs = refs[12:]
    if not first_call:
        refs = refs[6:]
    fac = dict(zip((D_Q, D_K, D_V), refs[:3]))
    tab_out, long_back, glob_back, d_send = refs[3:7]
    refs = refs[7:]
    w = dict(zip(ATTENTION_WEIGHTS, refs[:5]))
    sc = dict(zip(ATTENTION_USED, refs[5:9]))
    fs = dict(zip((D_Q, D_K, D_V), refs[9:12]))
    d_branch, da, dx, dx_low, tab_s, small, small_t, flip, tab, vc, sems = refs[12:]
    item, _, active, _ = turn_of(counts, step_at, False)

    @pl.when(active)
    def _():
        cp = Copies(sems)
        loads = {D_BRANCH: cp.start(branch_hbm.at[item], d_branch)}
        for name in (W_OUT, S_V, S_P, TABLE, S_K, S_Q):
            if name in w:
                loads[name] = cp.start(w_hbm[name], w[name])
            else:
                loads[name] = cp.start(st[name].at[item], sc[name])
        loads[S_TAB] = cp.start(small_hbm, small_t)
        for name in (W_QUERY, W_KEY, W_VALUE):
            loads[name] = cp.start(w_hbm[name], w[name])
        outs = []

        def save(name):
            outs.append(cp.start(fs[name], fac[name].at[item]))

        row = lax.broadcasted_iota(jnp.int32, (seq, seq), 0)
        col = lax.broadcasted_iota(jnp.int32, (seq, seq), 1)
        turn = (radius + 12) % seq
        flip[...] = jnp.where((row + col == turn) | (row + col == turn + seq), 1.0, 0.0).astype(BF16)
        vc[seq:, :] = jnp.zeros((128, vc.shape[1]), BF16)
        tab[192:, :] = jnp.zeros((tab.shape[0] - 192, tab.shape[1]), BF16)
        small[...] = jnp.zeros_like(small)
        loads[D_BRANCH].wait()
        loads[W_OUT].wait()
        da[...] = mm_t(d_branch[...], w[W_OUT][...]).astype(BF16)
        for name in (S_Q, S_K, S_V, TABLE, S_P):
            loads[name].wait()
        tab[0:192, :] = place_labels(w[TABLE], True)
        vc[0:seq, :] = sc[S_V][0:seq, :]
        vc[seq + 64:seq + 64 + slots, :] = sc[S_V][seq:rows, :]
        tab[192:192 + slots, :] = sc[S_K][seq:rows, :]
        halves = head_masks()
        label = lax.broadcasted_iota(jnp.int32, (1, 256), 1)
        own_label = (label >= 12) & (label < 12 + 2 * radius + 1)

        def pair(p, carry):
            cols = pl.ds(pl.multiple_of(p * 128, 128), 128)
            qp = sc[S_Q][:, cols]
            kp = sc[S_K][0:seq, cols]
            rk = tab[:, cols]
            vp = vc[:, cols]
            dap = da[:, cols]
            q_t = qp.T
            da_t = dap.T
            dq, dk_t, dv_t = [], [], []
            for hh in range(2):
                h = p * 2 + hh
                dam = jnp.where(halves[hh], dap, jnp.zeros_like(dap))
                prob_low = sc[S_P][h]
                d_prob = mm_t(dam, vp)
                prob = [prob_low[:, 128 * c:128 * c + 128].astype(F32) for c in range(3)]
                d_prob = [d_prob[:, 128 * c:128 * c + 128] for c in range(3)]
                delta = jnp.sum(sum(a * b for a, b in zip(prob, d_prob)), axis=-1, keepdims=True)
                delta = delta / jnp.sum(sum(prob), axis=-1, keepdims=True)
                ds = jnp.concatenate([(a * (b - delta)).astype(BF16) for a, b in zip(prob, d_prob)], 1)
                ds1 = ds[:, 0:seq]
                rel = pltpu.roll(mm(ds1[0:seq], flip[...]).astype(BF16), 0, 1, stride=1, stride_axis=0)
                far = jnp.concatenate(
                    [
                        jnp.concatenate([rel[:, 0:128], rel[:, 128:256] + ds[0:seq, seq:]], 1),
                        jnp.concatenate([jnp.zeros((slots, 128), BF16), ds[seq:rows, seq:]], 1),
                    ],
                    0,
                )
                dq.append(mm(ds1, kp) + mm(far, rk))
                own = slice(64 * hh, 64 * hh + 64)
                dk_t.append(jnp.concatenate([mm(q_t[own], ds1), mm(q_t[own], far)], 1) * 0.125)
                dv_t.append(mm(da_t[own], prob_low).astype(BF16))
            fs[D_Q][:, cols] = (jnp.where(halves[0], dq[0], dq[1]) * 0.125).astype(BF16)
            dk_t = jnp.concatenate(dk_t, 0)
            dk_low = dk_t.astype(BF16)
            dv_t = jnp.concatenate(dv_t, 0)
            fs[D_K][0:seq, cols] = dk_low[:, 0:seq].T
            fs[D_K][seq:rows, cols] = dk_low[:, seq + 128:].T[64:64 + slots]
            fs[D_V][0:seq, cols] = dv_t[:, 0:seq].T
            fs[D_V][seq:rows, cols] = dv_t[:, seq:].T[64:64 + slots]
            tab_s[cols, :] = jnp.where(own_label, dk_t[:, seq:], 0.0)
            return carry

        lax.fori_loop(0, H // 2, pair, 0, unroll=2)
        save(D_Q)
        save(D_K)
        save(D_V)
        small[64:65, :] = jnp.sum(fs[D_Q][...].astype(F32), axis=0, keepdims=True)
        small[65:66, :] = jnp.sum(fs[D_V][...].astype(F32), axis=0, keepdims=True)
        for name in (W_QUERY, W_KEY, W_VALUE, S_TAB):
            loads[name].wait()
        d_rows = (
            d_branch[...].astype(F32)
            + mm_t(fs[D_Q][...], w[W_QUERY][...])
            + mm_t(fs[D_K][...], w[W_KEY][...])
            + mm_t(fs[D_V][...], w[W_VALUE][...])
        )
        dx_low[...] = d_rows.astype(BF16)
        outs.append(cp.start(dx_low, d_send))
        dx[...] = d_rows
        outs.append(cp.start(dx.at[0:seq], rows_of(long_back, item, seq)))
        outs.append(cp.start(dx.at[seq:rows], rows_of(glob_back, item, slots)))
        tab_s[:, 128:] += small[...].T + small_t[...]
        outs.append(cp.start(tab_s, tab_out.at[item]))
        for copy in outs:
            copy.wait()


def run_attention_back(step_at, counts, d_branch, small, weights, state, made, seq, slots, radius):
    rows, width = d_branch.shape[1:]
    named, kept = dict(zip(WEIGHTS, weights)), dict(zip(STATE, state))
    items = kept[S_Q].shape[0]
    low = jax.ShapeDtypeStruct((items, rows, width), BF16)
    out_shape = [low, low, low, jax.ShapeDtypeStruct((items, width, 256), F32),
                 jax.ShapeDtypeStruct((items * seq, width), F32), jax.ShapeDtypeStruct((items * slots, width), F32),
                 jax.ShapeDtypeStruct((rows, width), BF16)]
    operands = [counts, d_branch, small] + [named[n] for n in ATTENTION_WEIGHTS] + [kept[n] for n in ATTENTION_USED]
    aliases = {}
    if made is not None:
        aliases = {len(operands) + n: n for n in range(6)}
        operands += list(made)
    scratch = [vm(named[n].shape) for n in ATTENTION_WEIGHTS]
    scratch += [vm(kept[n].shape[1:], kept[n].dtype) for n in ATTENTION_USED]
    scratch += [vm((rows, width))] * 3
    scratch += [vm((rows, width)), vm((rows, width)), vm((rows, width), F32), vm((rows, width)), vm((width, 256), F32), vm((128, width), F32),
                vm((width, 128), F32), vm((seq, seq)), vm((256, width)), vm((seq + 128, width)), pltpu.SemaphoreType.DMA((32,))]
    result = pl.pallas_call(
        functools.partial(attention_back_kernel, (seq, slots, radius, made is None, step_at)),
        out_shape=out_shape,
        in_specs=[SMEM] + [ANY] * (len(operands) - 1),
        out_specs=[ANY] * len(out_shape),
        scratch_shapes=scratch,
        input_output_aliases=aliases,
        compiler_params=pltpu.CompilerParams(vmem_limit_bytes=60 << 20),
        cost_estimate=pl.CostEstimate(flops=15 * 10**9, bytes_accessed=20 * 10**6, transcendentals=0),
        name="attention_back",
    )(*operands)
    return result[:6], result[6]


TILE = 16
MESH_ID = pl.DeviceIdType.MESH
NZ, NY, NX = 4, 2, 2
LOADED = (S_X, S_ATT, D_BRANCH, D_Q, D_K, D_V)
CHUNKS = ((2, 0), (0, 2)) * 3 + ((1, 0),)
ENTER = (0, 2, 4, 6, 8, 10, 11)
PIECES = 4
SPACING = 2
FFN_ORDER = (0, 3, 1, 2)
STAGES = 6
PER_CHUNK = 7
PER_FFN = 4


def reduce_kernel(cfg, *refs):
    pl.when(lax.axis_index("section") == cfg[3])(lambda: reduce_turn(cfg, *refs))


def reduce_turn(cfg, *refs):
    rows, width, hidden, turn = cfg
    wide, narrow = hidden // SHARDS, width // SHARDS
    ins = dict(zip(LOADED, refs[:6]))
    n1_hbm, n1_near, df_hbm, df_a, df_b, up_hbm, bias_hbm, down_hbm, tab_hbm, red_hbm = refs[6:16]
    refs = refs[16:]
    buf = dict(zip(LOADED, refs[:6]))
    n1, df, w_up, b_up, w_down, tab, ga, gf, ay, ax, az, by, bz, bx, fx, fz, u, d_hid, red = refs[6:25]
    load_sems, send_sems, recv_sems = refs[25:]
    section = lax.axis_index("section")
    me = lax.axis_index("dp")
    x, y, z = lax.rem(me, NX), lax.rem(lax.div(me, NX), NY), lax.div(me, NX * NY)
    half = rows // 2

    def at(zz, yy, xx):
        return (section, (zz * NY + yy) * NX + xx)

    across_x, across_y = at(z, y, 1 - x), at(z, 1 - y, x)
    above, below = at(z + 1, y, x), at(z - 1, y, x)

    cp = Copies(load_sems)
    loads = {}
    for name in (D_BRANCH, S_ATT):
        loads[name] = [cp.start(ins[name], buf[name])]
    loads[S_N1] = [cp.start(n1_hbm, n1.at[0:rows]), cp.start(n1_near, n1.at[rows:])]
    loads[D_FFN] = [cp.start(df_hbm, df.at[0:rows])]
    loads[D_FFN] += [cp.start(df_a, df.at[rows:rows + half]), cp.start(df_b, df.at[rows + half:])]
    loads[B_UP] = [cp.start(bias_hbm, b_up)]
    for n in FFN_ORDER:
        units = pl.ds(pl.multiple_of((2 * n + y) * 2 * wide, 2 * wide), 2 * wide)
        loads[W_UP, n] = [cp.start(up_hbm.at[:, units], w_up.at[n]), cp.start(down_hbm.at[units], w_down.at[n])]
    for name in (S_X, D_Q, D_K, D_V):
        loads[name] = [cp.start(ins[name], buf[name])]
    loads[S_TAB] = [cp.start(tab_hbm, tab)]

    barrier = pltpu.get_barrier_semaphore()
    for other in (across_x, across_y):
        pl.semaphore_signal(barrier, inc=1, device_id=other, device_id_type=MESH_ID)

    @pl.when(z > 0)
    def _():
        pl.semaphore_signal(barrier, inc=1, device_id=below, device_id_type=MESH_ID)

    @pl.when(z < NZ - 1)
    def _():
        pl.semaphore_signal(barrier, inc=1, device_id=above, device_id_type=MESH_ID)

    def need(*names):
        for name in names:
            for copy in loads.pop(name, ()):
                copy.wait()

    def units_of(n):
        return pl.ds(pl.multiple_of((2 * n + y) * 2 * wide, 2 * wide), 2 * wide)

    def form_hidden(n):
        need(S_N1, D_FFN, B_UP, (W_UP, n))
        bias = b_up[:, units_of(n)].astype(F32)

        def body(k, carry):
            some = pl.ds(pl.multiple_of(k * half, half), half)
            act, slope = gelu_parts(mm(n1[some, :], w_up[n]) + bias)
            u[some, :] = act.astype(BF16)
            d_hid[some, :] = (slope * mm_t(df[some, :], w_down[n])).astype(BF16)
            return carry

        lax.fori_loop(0, 4, body, 0)

    def form_down(n):
        part = mm_c(u[...], df[...]).astype(BF16)
        gf[n, 0, 0:wide, :] = part[0:wide]
        gf[n, 1, 0:wide, :] = part[wide:]

    def form_up(n):
        part = mm_c(d_hid[...], n1[...]).astype(BF16)
        gf[n, 0, wide:, :] = part[0:wide]
        gf[n, 1, wide:, :] = part[wide:]

    def form_narrow(left, right, at_row):
        need(left, right)

        def body(n, carry):
            cols = pl.ds(pl.multiple_of(n * 8 * narrow, 8 * narrow), 8 * narrow)
            part = mm_c(buf[left][:, cols], buf[right][...]).astype(BF16)
            for k in range(8):
                ga[2 * n + k // 4, (k // 2) % 2, k % 2, at_row:at_row + narrow, :] = part[k * narrow:(k + 1) * narrow]
            return carry

        lax.fori_loop(0, SHARDS // 8, body, 0)

    def form_table(at_row):
        need(S_TAB)

        def body(n, carry):
            for k in range(narrow // TILE):
                rows_k = pl.ds(pl.multiple_of(n * narrow + k * TILE, TILE), TILE)
                part = tab[0, rows_k, :] + tab[1, rows_k, :]
                shard = ga.at[lax.div(n, 4), lax.rem(lax.div(n, 2), 2), lax.rem(n, 2), at_row:at_row + TILE]
                shard[:, 256 * k:256 * k + 256] = part.astype(BF16)
            return carry

        lax.fori_loop(0, SHARDS, body, 0)

    first = [0]
    for counts in CHUNKS:
        first.append(first[-1] + sum(counts))

    def spans(chunk, route):
        counts = CHUNKS[chunk]
        start = first[chunk] + sum(counts[:route])
        own = sum(CHUNKS[n][route] for n in range(chunk))
        size = counts[route] * TILE
        return slice(start * TILE, start * TILE + size), slice(own * TILE, own * TILE + size), size

    pending = []

    def remote(src, dst, index, target):
        return pltpu.make_async_remote_copy(
            src_ref=src, dst_ref=dst, send_sem=send_sems.at[index], recv_sem=recv_sems.at[index],
            device_id=target, device_id_type=MESH_ID,
        )

    def send(src, dst, index, target):
        remote(src, dst, index, target).start()
        pending.append((None, lambda: remote(src, dst, index, target).wait_send()))

    def add(dst, src, lead, size):
        part = 48 if size % 48 == 0 else 32 if size % 32 == 0 else TILE
        steps = size // part
        for n in lead:
            steps *= n

        def body(n, carry):
            some = pl.ds(pl.multiple_of(lax.rem(n, size // part) * part, part), part)
            idx, rest = [], lax.div(n, size // part)
            for count in reversed(lead):
                idx.insert(0, lax.rem(rest, count))
                rest = lax.div(rest, count)
            d, s = dst(*idx).at[some], src(*idx).at[some]
            d[...] = (d[...].astype(F32) + s[...].astype(F32)).astype(BF16)
            return carry

        lax.fori_loop(0, steps, body, 0)

    def flow_z(stage, own, room, base, lead, size, shards=tuple(range(NZ))):
        def take(shard, slot, source):
            remote(own(shard), room(slot), base(slot), source).wait_recv()
            add(lambda *i: own(shard).at[i] if i else own(shard), lambda *i: room(slot).at[i] if i else room(slot), lead, size)

        def put(zz, shard, target):
            slot = NZ if (shard < zz and shard == zz - 1) else shard
            remote(own(shard), room(slot), base(slot), target).start()
            pending.append((zz, lambda: remote(own(shard), room(slot), base(slot), target).wait_send()))

        for zz in range(NZ):
            ups = [s for s in range(NZ - 1, zz - 1, -1) if s in shards]
            downs = [s for s in range(zz + 1) if s in shards]

            @pl.when(z == zz)
            def _():
                if stage == zz:
                    for shard in ups:
                        if zz > 0:
                            take(shard, shard, below)
                        if shard > zz:
                            put(zz, shard, above)
                if stage == NZ - 1 - zz:
                    for shard in downs:
                        if zz < NZ - 1:
                            take(shard, NZ if shard == zz else shard, above)
                        if shard < zz:
                            put(zz, shard, below)

    ffn_sems = len(CHUNKS) * PER_CHUNK

    def run(chunk, route, stage):
        rs, own, size = spans(chunk, route)
        if size == 0:
            return
        base = chunk * PER_CHUNK
        flow_base = lambda slot: base + 2 + slot
        out = slice(2 * wide + rs.start, 2 * wide + rs.stop)
        if stage == 0:
            room = ay if route == 0 else by
            send(ga.at[:, 1 - y, :, rs], room.at[:, :, own], base, across_y)
        if stage == 1:
            room = ay if route == 0 else by
            remote(ga.at[:, 1 - y, :, rs], room.at[:, :, own], base, across_y).wait_recv()
            add(lambda i, j: ga.at[i, y, j, rs], lambda i, j: room.at[i, j, own], (NZ, NX), size)
        if route == 0:
            if stage == 1:
                send(ga.at[:, y, 1 - x, rs], ax.at[:, own], base + 1, across_x)
            if stage == 2:
                remote(ga.at[:, y, 1 - x, rs], ax.at[:, own], base + 1, across_x).wait_recv()
                add(lambda i: ga.at[i, y, x, rs], lambda i: ax.at[i, own], (NZ,), size)
            if stage >= 2:
                flow_z(stage - 2, lambda s: ga.at[s, y, x, rs], lambda s: az.at[s, own], flow_base, (), size)
        else:
            if 1 <= stage <= 4:
                flow_z(stage - 1, lambda s: ga.at[s, y, :, rs], lambda s: bz.at[s, :, own], flow_base, (NX,), size)
            if stage == 4:
                send(ga.at[z, y, 1 - x, rs], bx.at[own], base + 1, across_x)
            if stage == 5:
                remote(ga.at[z, y, 1 - x, rs], bx.at[own], base + 1, across_x).wait_recv()
                add(lambda: ga.at[z, y, x, rs], lambda: bx.at[own], (), size)
        if stage == 5:
            red[out, :] = ga[z, y, x, rs, :].astype(F32)

    def run_ffn(n, piece, stage):
        base = ffn_sems + (n * PIECES + piece) * PER_FFN
        size = 2 * wide // PIECES
        rs = slice(piece * size, (piece + 1) * size)
        if stage == 0:
            send(gf.at[n, 1 - x, rs], fx.at[n, rs], base, across_x)
        if stage == 1:
            remote(gf.at[n, 1 - x, rs], fx.at[n, rs], base, across_x).wait_recv()
            add(lambda: gf.at[n, x, rs], lambda: fx.at[n, rs], (), size)
        if 1 <= stage <= 4:
            room = lambda slot: fz.at[1 if slot == NZ else 0, n, rs]
            flow_z(stage - 1, lambda s: gf.at[s, x, rs], room, lambda slot: base + (2 if slot == NZ else 1), (), size, (n,))
        if stage == 5:
            @pl.when(z == n)
            def _():
                red[rs, :] = gf[n, x, rs, :].astype(F32)

    def narrow_task(n):
        left, right = ((D_BRANCH, S_ATT), (D_Q, S_X), (D_K, S_X), (D_V, S_X))[n]
        return lambda: form_narrow(left, right, n * narrow)

    a, b, c, d = FFN_ORDER
    hidden_task = lambda n: lambda: form_hidden(n)
    down_task = lambda n: lambda: form_down(n)
    up_task = lambda n: lambda: form_up(n)
    tasks = [(narrow_task(1),), (up_task(a),), (hidden_task(b),), (down_task(b),), (narrow_task(2),), (up_task(b),),
             (hidden_task(c), narrow_task(3)), (down_task(c),), (), (up_task(c),),
             (hidden_task(d), lambda: form_table(4 * narrow)), (down_task(d),), (up_task(d),)]
    narrow_task(0)()

    @pl.when((z == 0) | (z == NZ - 1))
    def _():
        pl.semaphore_wait(barrier, 3)

    @pl.when((z > 0) & (z < NZ - 1))
    def _():
        pl.semaphore_wait(barrier, 4)

    starts = [(n, None, slot) for n, slot in enumerate(ENTER)]
    starts += [(FFN_ORDER[k // PIECES], k % PIECES, k) for k in range(NZ * PIECES)]
    last = max(slot for _, _, slot in starts) + SPACING * (STAGES - 1)
    for slot in range(last + 1):
        for stage in range(STAGES):
            for n, piece, enter in starts:
                if enter + stage * SPACING == slot:
                    if slot == 0 and piece == 0:
                        form_hidden(a)
                        form_down(a)
                    if piece is None:
                        run(n, 0, stage)
                        run(n, 1, stage)
                    else:
                        run_ffn(n, piece, stage)
            if stage == 0:
                for task in tasks.pop(0) if tasks else ():
                    task()
    result = cp.start(red, red_hbm)
    for zz, wait in pending:
        if zz is None:
            wait()
        else:
            pl.when(z == zz)(wait)
    result.wait()


def reduce_grads(turn, parts, near, weights, tab):
    rows, width = parts[S_X].shape
    hidden = weights[W_UP].shape[1]
    wide, narrow = hidden // SHARDS, width // SHARDS
    share = 4 * narrow + TILE
    t = [sum(c[n] for c in CHUNKS) * TILE for n in range(2)]
    assert sum(t) == share
    n_sem = len(CHUNKS) * PER_CHUNK + NZ * PIECES * PER_FFN
    scratch = [vm(parts[n].shape) for n in LOADED]
    scratch += [
        vm((2 * rows, width)), vm((2 * rows, width)), vm((NZ, width, 2 * wide)), vm((1, hidden)), vm((NZ, 2 * wide, width)),
        vm(tab.shape, F32),
        vm((NZ, NY, NX, share, width)), vm((NZ, NX, 2 * wide, width)),
        vm((NZ, NX, t[0], width)), vm((NZ, t[0], width)), vm((NZ + 1, t[0], width)),
        vm((NZ, NX, t[1], width)), vm((NZ + 1, NX, t[1], width)), vm((t[1], width)),
        vm((NZ, 2 * wide, width)), vm((2, NZ, 2 * wide, width)), vm((2 * rows, 2 * wide)), vm((2 * rows, 2 * wide)),
        vm((2 * wide + share, width), F32),
        pltpu.SemaphoreType.DMA((32,)), pltpu.SemaphoreType.DMA((n_sem,)), pltpu.SemaphoreType.DMA((n_sem,)),
    ]
    operands = [parts[n] for n in LOADED]
    operands += [parts[S_N1], near[0], parts[D_FFN]] + list(near[1:])
    operands += [weights[W_UP], weights[B_UP], weights[W_DOWN], tab]
    return pl.pallas_call(
        functools.partial(reduce_kernel, (rows, width, hidden, turn)),
        cost_estimate=pl.CostEstimate(flops=60 * 10**9, bytes_accessed=20 * 10**6, transcendentals=0),
        out_shape=jax.ShapeDtypeStruct((2 * wide + share, width), F32),
        in_specs=[ANY] * len(operands),
        out_specs=ANY,
        scratch_shapes=scratch,
        compiler_params=pltpu.CompilerParams(collective_id=turn, has_side_effects=True, vmem_limit_bytes=60 << 20),
        name="reduce_grads",
    )(*operands)


def finish_kernel(labels, red_a, red_b, *refs):
    w_out, w_query, w_key, w_value, w_up, w_down, table = refs[:7]
    vectors, bias, red, turned, sem = refs[7:15], refs[15], refs[16], refs[17], refs[18]
    wide, narrow = w_up.shape[0], w_out.shape[0]
    cp = Copies(sem)
    cp.choose(lax.axis_index("section") == 0, red_a, red_b, red).wait()
    outs = [cp.start(red.at[0:wide], w_down), cp.start(red.at[wide:2 * wide], w_up)]
    for n, ref in enumerate((w_out, w_query, w_key, w_value)):
        at = 2 * wide + n * narrow
        outs.append(cp.start(red.at[at:at + narrow], ref))
    at = 2 * wide + 4 * narrow
    packed = jnp.concatenate([red[at:at + TILE, 256 * k:256 * k + 256] for k in range(narrow // TILE)], 0)
    turned[...] = packed.T
    row = lax.broadcasted_iota(jnp.int32, (256, labels), 0)
    col = lax.broadcasted_iota(jnp.int32, (256, labels), 1)
    back = jnp.where(row + col == labels + 11, 1.0, 0.0)
    table[...] = jnp.dot(packed, back, precision=lax.Precision.HIGHEST, preferred_element_type=F32)
    for n, ref in enumerate(vectors):
        ref[...] = turned[192 + n:193 + n, :]
    for k in range(wide // narrow):
        bias[:, k * narrow:(k + 1) * narrow] = turned[200 + k:201 + k, :]
    for copy in outs:
        copy.wait()


def finish(red_a, red_b, labels, hidden):
    width = red_a.shape[1]
    wide, narrow = hidden // SHARDS, width // SHARDS
    out = lambda *s: jax.ShapeDtypeStruct(s, F32)
    shapes = [out(narrow, width)] * 4 + [out(wide, width), out(wide, width), out(narrow, labels)]
    shapes += [out(1, narrow)] * 8 + [out(1, wide)]
    result = pl.pallas_call(
        functools.partial(finish_kernel, labels),
        out_shape=shapes,
        in_specs=[ANY, ANY],
        out_specs=[ANY] * 6 + [pl.BlockSpec(memory_space=pltpu.VMEM)] * (len(shapes) - 6),
        scratch_shapes=[vm(red_a.shape, F32), vm((256, narrow), F32), pltpu.SemaphoreType.DMA((8,))],
        compiler_params=pltpu.CompilerParams(vmem_limit_bytes=40 << 20),
        name="finish",
    )(red_a, red_b)
    mats = [t.T for t in result[:5]] + [result[5], result[6].T]
    return [t[None] for t in mats] + list(result[7:])


def sums_elsewhere(parts, weights, tab):
    def scatter(value, dim):
        return lax.psum_scatter(value, "dp", scatter_dimension=dim, tiled=True)

    cut = [scatter(mm_c(parts[a], parts[b]), 1)
           for a, b in ((S_ATT, D_BRANCH), (S_X, D_Q), (S_X, D_K), (S_X, D_V))]
    act, slope = gelu_parts(mm(parts[S_N1], weights[W_UP]) + weights[B_UP].astype(F32))
    d_hid = (slope * mm_t(parts[D_FFN], weights[W_DOWN])).astype(BF16)
    w_up = scatter(mm_c(parts[S_N1], d_hid), 1)
    w_down = scatter(mm_c(act.astype(BF16), parts[D_FFN]), 0)
    b_up = scatter(jnp.sum(d_hid.astype(F32), axis=0), 0)
    return cut, w_up, w_down, scatter(tab[0] + tab[1], 0), b_up


def per_device(
    long_input, global_input, counts, w_query, b_query, w_key, w_value, b_value, w_out, b_out, rel_table,
    norm1_gain, norm1_bias, w_up, b_up, w_down, b_down, norm2_gain, norm2_bias, long_cot, global_cot,
):
    items = counts.shape[0]
    seq, slots, width = long_input.shape[0] // items, global_input.shape[0] // items, long_input.shape[1]
    rows, hidden = seq + slots, w_up.shape[2]
    labels = rel_table.shape[1]
    radius = (labels - 1) // 2
    weights = [w_query[0], w_key[0], w_value[0], w_out[0], w_up[0], w_down[0],
               rel_table[0],
               b_query, b_value, b_out, norm1_gain, norm1_bias, b_up, b_down, norm2_gain, norm2_bias]

    recv = long_input
    state = outs = None
    for step in range(items + 1):
        state, outs, sent = run_forward(
            step, counts, long_input, global_input, recv, weights, state, outs, seq, slots, radius)
        if step < items:
            recv = lax.ppermute(sent, "section", [(0, 1)])
    kept = dict(zip(STATE, state))
    shards = lax.axis_size("dp")
    paired = shards == SHARDS
    near = []
    if paired:
        near = [lax.ppermute(kept[S_N1], "dp", [(n, n ^ NX) for n in range(shards)]).reshape(items * rows, width)]
    named = dict(zip(WEIGHTS, weights))

    def parts_of():
        parts = {n: kept[n] for n in (S_X, S_ATT, S_N1)}
        parts.update(zip((D_FFN, D_BRANCH, D_Q, D_K, D_V), list(low) + list(made[:3])))
        return {n: t.reshape(items * rows, t.shape[2]) for n, t in parts.items()}

    low = made = None
    summed, awaited = [], near[0:1]
    for step in range(items + 1):
        low, d_ffn, small = run_hidden_back(
            step, counts, long_cot, global_cot, recv, weights, state, low, awaited if step else [], seq, slots)
        if paired:
            pairs = [(e * shards + n, e * shards + (n ^ NX)) for e in range(2) for n in range(shards)
                     if 0 <= step - (1 - e) < items]
            near.append(lax.ppermute(d_ffn, ("section", "dp"), pairs))
        made, sent = run_attention_back(
            step, counts, low[1], small, weights, state, made, seq, slots, radius)
        if step < items:
            if paired:
                sent, near[-1] = lax.optimization_barrier((sent, near[-1]))
            recv = lax.ppermute(sent, "section", [(1, 0)])
        if paired and step >= items - 1:
            turn = items - step
            awaited = [reduce_grads(turn, parts_of(), [near[0]] + near[step:step + 2], named, made[3])]
            summed += awaited
    long_back, glob_back = made[4:6]
    if paired:
        final = finish(summed[1], summed[0], labels, hidden)
        g_out, g_query, g_key, g_value, g_up, g_down, g_table = final[:7]
        g_bq, g_bv, g_bo, g_g1, g_s1, g_bd, g_g2, g_s2, g_b_up = final[7:]
    else:
        cut, g_up, g_down, table, g_b_up = [jax.tree.map(lambda t: t[None], t)
                                            for t in sums_elsewhere(parts_of(), named, made[3])]
        g_out, g_query, g_key, g_value = cut
        g_bq, g_bv, g_bo, g_g1, g_s1, g_bd, g_g2, g_s2 = [table[:, :, 192 + n] for n in range(8)]
        g_table = table[0, :, 12:12 + labels][:, ::-1].T[None]
    grads = (g_query, g_bq, g_key, g_value, g_bv, g_out, g_bo, g_table, g_g1, g_s1, g_up, g_b_up, g_down, g_bd, g_g2, g_s2)
    return tuple(t[None] for t in (outs[0], outs[1], long_back, glob_back)) + grads


def solution(mesh):
    part = P("section", "dp", None)
    vector = P("section", "dp")
    columns = P("section", None, "dp")
    matrix = P("section", None, None)
    row = P("section", None)
    items = P("dp", None)
    in_specs = (items, items, P("dp"), matrix, row, matrix, matrix, row, matrix, row, matrix, row, row,
                matrix, row, matrix, row, row, row, items, items)
    out_specs = (part, part, part, part, columns, vector, columns, columns, vector, columns, vector, columns,
                 vector, vector, columns, vector, part, vector, vector, vector)
    return jax.shard_map(per_device, mesh=mesh, in_specs=in_specs, out_specs=out_specs, check_vma=False)
```
